32 devices in a mesh: seq: 4 (over x, core), fsdp: 8 (over z, y).
Axes of the slice: x: 2, y: 2, z: 4, core: 2. Of those that a mesh axis runs over, the one named last changes fastest.
Arguments:
- tokens: bfloat16 [16, 1024, 768], P('fsdp', 'seq'), may hold values from -6 to 6
- segments: int32 [16, 1024], P('fsdp', 'seq'), may hold values from 0 to 17, as said below
- w_qkv: bfloat16 [768, 2304], P('fsdp', 'seq'), may hold values from -0.21875 to 0.21875
- w_out: bfloat16 [768, 768], P('fsdp', 'seq'), may hold values from -1.75 to 1.75
- w_in: bfloat16 [768, 2304], P('fsdp', 'seq'), may hold values from -0.21875 to 0.21875
- w_down: bfloat16 [1152, 768], P('fsdp', 'seq'), may hold values from -0.375 to 0.375
- gains: bfloat16 [2, 768], P(None, 'fsdp'), may hold values from 0.25 to 1.75
- cotangent: bfloat16 [16, 1024, 768], P('fsdp', 'seq'), may hold values from -6 to 6
Outputs:
- mixed: bfloat16 [16, 1024, 768], P('fsdp', 'seq')
- grad_tokens: bfloat16 [16, 1024, 768], P('fsdp', 'seq')
- grad_qkv: float32 [768, 2304], P('fsdp', 'seq')
- grad_out: float32 [768, 768], P('fsdp', 'seq')
- grad_in: float32 [768, 2304], P('fsdp', 'seq')
- grad_down: float32 [1152, 768], P('fsdp', 'seq')
- grad_gains: float32 [2, 768], P(None, 'fsdp')
The draws below stay inside these ranges and needn't reach their ends.
Inputs may be any that keep to these rules, and one draw needn't show every extreme that they name: `segments`: segment numbers of a sequence start at 0 and never fall; no document holds more than 800 tokens; in each run of 2 consecutive sequences at least one holds a document of exactly 800 tokens that begins at one of its positions 1 to 224; in the first run one other sequence consists of documents of exactly 60 tokens each, its last possibly shorter.
All inputs are finite; a program needn't handle non-finite values.
Results may differ from the reference program's by a relative error of at most 0.018.
Values may be sent and summed in bfloat16 or wider, within the bound.
No kernel may reach another device: no remote copies, remote signals or barrier semaphores. Data moves between devices by JAX's collectives and lax.ppermute only.
A program may use at most 128 MiB of HBM per device.

```python
import math
import jax
import jax.numpy as jnp
from jax import lax

D = 768
HEADS = 12
HEAD_DIM = 64
FF = 1152
LEN = 1024
SEQ_DEV = 2
SEQS = 16
DOC_MIN = 60
DOC_MAX = 800


def draw_segments(key, part):
    key = jax.random.fold_in(key, 7)
    count = LEN // DOC_MIN + 2
    keys = jax.random.split(key, 3)
    spans = jax.random.randint(keys[0], (SEQS, count), DOC_MIN, DOC_MAX + 1)
    chosen = jax.random.randint(keys[1], (SEQS // SEQ_DEV,), 0, SEQ_DEV)
    leading = jax.random.randint(keys[2], (SEQS,), 1, LEN - DOC_MAX + 1)
    order = jnp.arange(SEQS)
    marked = order % SEQ_DEV == jnp.repeat(chosen, SEQ_DEV)
    first = jnp.where(marked, leading, spans[:, 0])
    second = jnp.where(marked, DOC_MAX, spans[:, 1])
    spans = spans.at[:, 0].set(first).at[:, 1].set(second)
    filler = order == (chosen[0] + 1) % SEQ_DEV
    spans = jnp.where(filler[:, None], DOC_MIN, spans)
    ends = jnp.cumsum(spans, axis=1)
    places = jnp.arange(LEN)
    return jnp.sum((ends[:, None, :] <= places[None, :, None]).astype(jnp.int32), axis=2).astype(jnp.int32)


def levels(stream_key, dims, cuts, smallest, top_value):
    level, own = 1.0, jax.random.fold_in(stream_key, 6)
    for position, blocks in cuts:
        heights = jnp.exp(jax.random.uniform(jax.random.fold_in(own, position), (blocks,), jnp.float32, smallest / len(cuts), top_value / len(cuts)))
        level = level * jnp.repeat(heights, dims[position] // blocks).reshape([-1 if axis == position else 1 for axis in range(len(dims))])
    return level


def bell_draw(key, dims, scale, reach, cuts=(), held_as=jnp.bfloat16):
    loudness = levels(key, dims, cuts, -0.22, 0.18) if cuts else 1.0
    drawn = jax.random.normal(key, dims, jnp.float32) * scale * loudness
    return jnp.minimum(jnp.maximum(drawn, -reach), reach).astype(held_as)


def setup_inputs(seed: int = 0) -> dict:
    key_of = jax.random.split(jax.random.key(seed), 9)
    tokens = bell_draw(key_of[0], (SEQS, LEN, D), 1.0, 6.0, ((0, 8), (1, 4)))
    segments = draw_segments(jax.random.fold_in(key_of[8], 71), 0)
    w_qkv = bell_draw(key_of[2], (D, 3 * D), D ** -0.5, 0.21875, ((0, 8), (1, 4)))
    w_out = bell_draw(key_of[3], (D, D), (max(D // 64, 1)) ** -0.5, 1.75, ((0, 8), (1, 4)))
    w_in = bell_draw(key_of[4], (D, 2 * FF), D ** -0.5, 0.21875, ((0, 8), (1, 4)))
    w_down = bell_draw(key_of[5], (FF, D), (FF // 4) ** -0.5, 0.375, ((0, 8), (1, 4)))
    gains = jnp.clip(1.0 + 0.15 * jax.random.normal(key_of[6], (2, D), jnp.float32), 0.25, 1.75).astype(jnp.bfloat16)
    cotangent = bell_draw(key_of[7], (SEQS, LEN, D), 1.0, 6.0, ((0, 8), (1, 4)))
    return dict(tokens=tokens, segments=segments, w_qkv=w_qkv, w_out=w_out, w_in=w_in, w_down=w_down, gains=gains, cotangent=cotangent)


@jax.custom_vjp
def low(v):
    return lax.optimization_barrier(v.astype(jnp.bfloat16)).astype(jnp.float32)

@jax.custom_vjp
def low_back(v):
    return v

def low_keep(v):
    return (low(v), None)

def low_pass(kept, grad):
    return (grad,)

def back_keep(v):
    return (v, None)

def back_low(kept, grad):
    return (low(grad),)
low.defvjp(low_keep, low_pass)
low_back.defvjp(back_keep, back_low)
highest_precision_mode = lax.Precision.HIGHEST
norm_eps = 1e-05
mask_fill = -1000000000.0

def layer_norm(values, gain_row):
    center = values - lax.optimization_barrier(jnp.mean(values, axis=-1, keepdims=True))
    spread = lax.optimization_barrier(jnp.mean(center * center, axis=-1, keepdims=True))
    return center * lax.rsqrt(spread + norm_eps) * gain_row

def rope_tables(positions, head_width):
    half_width = head_width // 2
    freqs = jnp.exp(-jnp.arange(half_width, dtype=jnp.float32) * (2.0 * math.log(160000.0) / head_width))
    angles = positions[:, None] * freqs[None, :]
    return (jnp.cos(angles)[:, None, :], jnp.sin(angles)[:, None, :])

def rotate(packed, cosine, sine):
    half_width = packed.shape[-1] // 2
    first_half = packed[..., :half_width]
    second_half = packed[..., half_width:]
    return jnp.concatenate([first_half * cosine - second_half * sine, second_half * cosine + first_half * sine], axis=-1)

def attend_block(query, keys, values, same_doc, score_scale):

    def one_head(pieces):
        query_per_head, key_per_head, value_per_head = pieces
        unmasked_scores = jnp.einsum('tzg,tjg->tzj', query_per_head, key_per_head, precision=highest_precision_mode) * score_scale
        scores = low_back(jnp.where(same_doc, unmasked_scores, mask_fill))
        peak_score = lax.optimization_barrier(jnp.max(scores, axis=-1, keepdims=True))
        weights = jnp.exp(scores - peak_score)
        attention_probabilities = weights / lax.optimization_barrier(jnp.sum(weights, axis=-1, keepdims=True))
        return low_back(jnp.einsum('jhz,jzc->jhc', low(attention_probabilities), value_per_head, precision=highest_precision_mode))
    return lax.map(jax.checkpoint(one_head), (query, keys, values))

def forward(start_x, same_doc, w_qkv, w_out, w_in, w_down, gains, cosine, sine):
    batch, length, model_width = start_x.shape
    head_width = model_width // HEADS
    first_normalized = low(layer_norm(start_x, gains[0]))
    packed_query_key_value = low_back(jnp.einsum('bld,de->ble', first_normalized, w_qkv, precision=highest_precision_mode))
    head_shape = (batch, length, HEADS, head_width)
    query = low(rotate(packed_query_key_value[..., :model_width].reshape(head_shape), cosine, sine))
    keys = low(rotate(packed_query_key_value[..., model_width:2 * model_width].reshape(head_shape), cosine, sine))
    values = low(packed_query_key_value[..., 2 * model_width:].reshape(head_shape))
    heads_out = attend_block(query.transpose(2, 0, 1, 3), keys.transpose(2, 0, 1, 3), values.transpose(2, 0, 1, 3), same_doc, 1.0 / math.sqrt(head_width))
    attention_mixed = low(heads_out.transpose(1, 2, 0, 3).reshape(batch, length, model_width))
    middle = start_x + low_back(jnp.einsum('bld,de->ble', attention_mixed, w_out, precision=highest_precision_mode))
    second_normalized = low(layer_norm(middle, gains[1]))
    inner_state = low_back(jnp.einsum('bld,de->ble', second_normalized, w_in, precision=highest_precision_mode))
    hidden_state = low(jax.nn.gelu(inner_state[..., :FF], approximate=False) * inner_state[..., FF:])
    return middle + low_back(jnp.einsum('blf,fd->bld', hidden_state, w_down, precision=highest_precision_mode))

def reference(tokens, segments, w_qkv, w_out, w_in, w_down, gains, cotangent):
    batch = 4 if SEQS % 4 == 0 else 1
    groups = SEQS // batch
    weight_set = tuple((weight.astype(jnp.float32) for weight in (w_qkv, w_out, w_in, w_down, gains)))
    cosine, sine = rope_tables(jnp.arange(LEN, dtype=jnp.float32), HEAD_DIM)
    inputs = tokens.astype(jnp.float32).reshape(groups, batch, LEN, D)
    seg_blocks = segments.reshape(groups, batch, LEN)
    cot_blocks = cotangent.astype(jnp.float32).reshape(groups, batch, LEN, D)

    def accumulate(totals, item):
        block_x, block_seg, block_cot = item
        same_doc = block_seg[:, :, None] == block_seg[:, None, :]

        def apply(start_x, *weight_args):
            return forward(start_x, same_doc, *weight_args, cosine, sine)
        result, pull = jax.vjp(apply, block_x, *weight_set)
        grads = pull(block_cot)
        totals = tuple((total + grad for total, grad in zip(totals, grads[1:])))
        return (totals, (result, grads[0]))
    zeros = tuple((jnp.zeros(weight.shape, jnp.float32) for weight in weight_set))
    totals, (results, grad_x) = lax.scan(accumulate, zeros, (inputs, seg_blocks, cot_blocks))
    mixed = results.reshape(SEQS, LEN, D).astype(jnp.bfloat16)
    grad_tokens = grad_x.reshape(SEQS, LEN, D).astype(jnp.bfloat16)
    return (mixed, grad_tokens, totals[0], totals[1], totals[2], totals[3], totals[4])
```

```python
import functools
import math

import jax
import jax.numpy as jnp
from jax import lax
from jax.experimental import pallas as pl
from jax.experimental.pallas import tpu as pltpu
from jax.sharding import PartitionSpec as P

HEADS = 12
HEAD = 64
PAIR = 2 * HEAD
EPS = 1e-05
FILL = -1000000000.0
BF = jnp.bfloat16
F32 = jnp.float32
VMEM_LIMIT = 60 * 1024 * 1024

STEPS = {
    "x": [("seq", 2)],
    "y": [("fsdp", 1)],
    "z": [("fsdp", 2), ("fsdp", 4), ("fsdp", 6)],
    "core": [("seq", 1)],
}
ORDER_B = ("z", "x", "y")
ORDER_C = ("y", "z", "x")
GRID_F = 8
GRID_S = 4


def swap(value, step):
    axis, flip = step
    size = lax.axis_size(axis)
    return lax.ppermute(value, axis, [(i, i ^ flip) for i in range(size)])


def gather_part(block, order):
    held = block[None]
    for phase in order:
        held = jnp.concatenate([held] + [swap(held, step) for step in STEPS[phase]], axis=0)
    return held, swap(held, STEPS["core"][0])


def scatter_part(own, other, order):
    total = own.astype(F32) + swap(other, STEPS["core"][0]).astype(F32)
    for phase in reversed(order):
        total = total.astype(BF)
        count = total.shape[0] // (len(STEPS[phase]) + 1)
        parts = [total[:count].astype(F32)]
        for place, step in enumerate(STEPS[phase]):
            sent = total[(place + 1) * count : (place + 2) * count]
            parts.append(swap(sent, step).astype(F32))
        if len(parts) == 4:
            total = (parts[0] + parts[1]) + (parts[2] + parts[3])
        else:
            total = parts[0] + parts[1]
    return total[0]


def codes_of(order):
    codes = [(0, 0)]
    for phase in order:
        grown = list(codes)
        for axis, flip in STEPS[phase]:
            for f, s in codes:
                grown.append((f ^ flip, s) if axis == "fsdp" else (f, s ^ flip))
        codes = grown
    return codes


def place_b(xf, xs):
    return (xf >> 1) + 4 * (xs >> 1) + 8 * (xf & 1)


def place_c(xf, xs):
    return (xf & 1) + 2 * (xf >> 1) + 8 * (xs >> 1)


def dot(a, b):
    return jnp.dot(a, b, preferred_element_type=F32)


def dot_nt(a, b, precision=None):
    return lax.dot_general(
        a, b, (((1,), (1,)), ((), ())), preferred_element_type=F32, precision=precision
    )


def dot_tn(a, b, precision=None):
    return lax.dot_general(
        a, b, (((0,), (0,)), ((), ())), preferred_element_type=F32, precision=precision
    )


def norm_stats(x):
    center = x - jnp.mean(x, axis=-1, keepdims=True)
    spread = jnp.mean(center * center, axis=-1, keepdims=True)
    rate = lax.rsqrt(spread + EPS)
    return center * rate, rate


def norm_back(e, hat, rate):
    return rate * (
        e
        - jnp.mean(e, axis=-1, keepdims=True)
        - hat * jnp.mean(e * hat, axis=-1, keepdims=True)
    )


def turn(u, cosine, sine_a, sine_b):
    return u * cosine + pltpu.roll(u, PAIR - 32, 1) * sine_a + pltpu.roll(u, 32, 1) * sine_b


def turn_back(u, cosine, sine_a, sine_b):
    return u * cosine - pltpu.roll(u, PAIR - 32, 1) * sine_a - pltpu.roll(u, 32, 1) * sine_b


def pick(me, f, s, place, own, other):
    xf = me[0] ^ f
    xs = me[1] ^ s
    k = place(xf, xs)
    return lax.select((xs & 1) == 0, own[k], other[k])


def put(me, f, s, place, own, other, value):
    xf = me[0] ^ f
    xs = me[1] ^ s
    k = place(xf, xs)

    @pl.when((xs & 1) == 0)
    def _():
        own[k] = value

    @pl.when((xs & 1) != 0)
    def _():
        other[k] = value


def project_kernel(
    me, xa, xb, gb0, gb1, gc0, gc1, cos, sin_a, sin_b,
    q_o, k_o, v_o, n_o, w_o, g_o, gcol,
):
    def fill(f, carry):
        for part, (place, own, other) in enumerate(
            ((place_b, gb0, gb1), (place_c, gc0, gc1))
        ):
            row = pl.multiple_of(f * 96 + part * 48, 16)
            values = [pick(me, f, s, place, own, other) for s in range(GRID_S)]
            gcol[pl.ds(row, 48), :] = values[0][:, 512:640]
            w_o[pl.ds(row, 48), :] = jnp.concatenate([v[:, :576] for v in values], axis=1)
        return carry

    lax.fori_loop(0, GRID_F, fill, 0)
    row_i = lax.broadcasted_iota(jnp.int32, (8, 128), 0)
    lane_i = lax.broadcasted_iota(jnp.int32, (8, 128), 1)
    hot = jnp.where(lane_i == row_i + 64, 1.0, 0.0).astype(BF)
    gains = dot_nt(hot, gcol[...])
    g_o[...] = gains
    for half, xr in enumerate((xa, xb)):
        hat, _ = norm_stats(xr[...].astype(F32))
        n_o[256 * half : 256 * half + 256, :] = (hat * gains[0:1, :]).astype(BF)
    for j in range(9):
        y = dot(n_o[...], w_o[:, 256 * j : 256 * j + 256])
        if j < 6:
            y = jnp.concatenate(
                [
                    turn(y[:, 128 * i : 128 * i + 128], cos[...], sin_a[...], sin_b[...])
                    for i in range(2)
                ],
                axis=1,
            )
        if j < 3:
            q_o[:, 256 * j : 256 * j + 256] = (y.astype(BF) * 0.125).astype(BF)
        elif j < 6:
            k_o[:, 256 * (j - 3) : 256 * (j - 3) + 256] = y.astype(BF)
        else:
            v_o[:, 256 * (j - 6) : 256 * (j - 6) + 256] = y.astype(BF)


def head_masks():
    lane = lax.broadcasted_iota(jnp.int32, (1, PAIR), 1)
    first = jnp.where(lane < HEAD, 1.0, 0.0)
    return lane < HEAD, (first.astype(BF), (1.0 - first).astype(BF))


def attend_kernel(q, ka, kb, va, vb, seg_col, seg_row, out, lse, bias):
    @pl.when(pl.program_id(0) == 0)
    def _():
        bias[...] = jnp.where(seg_col[...] == seg_row[...], 0.0, FILL)

    lane, masks = head_masks()
    for t in range(2):
        rows = slice(256 * t, 256 * t + 256)
        outs, logs = [], []
        for mask in masks:
            qm = q[rows, :] * mask
            s = jnp.concatenate([dot_nt(qm, ka[...]), dot_nt(qm, kb[...])], axis=1)
            s = s + bias[rows, :]
            peak = jnp.max(s, axis=-1, keepdims=True)
            e = jnp.exp(s - peak)
            total = jnp.sum(e, axis=-1, keepdims=True)
            eb = e.astype(BF)
            o = dot(eb[:, :512], va[...]) + dot(eb[:, 512:], vb[...])
            outs.append(o * (1.0 / total))
            logs.append(peak + jnp.log(total))
        out[rows, :] = jnp.where(lane, outs[0], outs[1]).astype(BF)
        lse[rows, :] = jnp.where(lane, logs[0], logs[1])


def attend_back_kernel(
    q, ka, kb, va, vb, att, datt, lse, seg_col, seg_row, cos, sin_a, sin_b,
    dq_o, dka_o, dkb_o, dva_o, dvb_o, bias,
):
    @pl.when(pl.program_id(0) == 0)
    def _():
        bias[...] = jnp.where(seg_col[...] == seg_row[...], 0.0, FILL)

    lane, masks = head_masks()
    row_i = lax.broadcasted_iota(jnp.int32, (8, PAIR), 0)
    lane_i = lax.broadcasted_iota(jnp.int32, (8, PAIR), 1)
    hot = jnp.where(lane_i == row_i * HEAD, 1.0, 0.0)
    spread = jnp.where((lane_i // HEAD) == row_i, 1.0, 0.0)
    high = lax.Precision.HIGHEST
    log_rows = dot_nt(hot, lse[...], high)
    delta_rows = dot_nt(spread, datt[...].astype(F32) * att[...].astype(F32), high)
    dq_parts = [[None, None], [None, None]]
    dk_parts = [None, None]
    dv_parts = [None, None]
    for side, (k, v) in enumerate(((ka, va), (kb, vb))):
        keys = slice(512 * side, 512 * side + 512)
        for t in range(2):
            rows = slice(256 * t, 256 * t + 256)
            for h, mask in enumerate(masks):
                qm = q[rows, :] * mask
                dm = datt[rows, :] * mask
                s = dot_nt(k[...], qm) + bias[keys, rows]
                p = jnp.exp(s - log_rows[h : h + 1, rows])
                dp = dot_nt(v[...], dm)
                ds = (p * (dp - delta_rows[h : h + 1, rows])).astype(BF)
                dv = dot(p.astype(BF), dm)
                dk = dot(ds, qm)
                dq = dot_tn(ds, k[...])
                dv_parts[side] = dv if dv_parts[side] is None else dv_parts[side] + dv
                dk_parts[side] = dk if dk_parts[side] is None else dk_parts[side] + dk
                old = dq_parts[t][h]
                dq_parts[t][h] = dq if old is None else old + dq
    dka_o[...] = dk_parts[0]
    dkb_o[...] = dk_parts[1].astype(BF)
    dva_o[...] = dv_parts[0]
    dvb_o[...] = dv_parts[1].astype(BF)
    for t in range(2):
        rows = slice(256 * t, 256 * t + 256)
        dq = jnp.where(lane, dq_parts[t][0], dq_parts[t][1]) * 0.125
        dq_o[rows, :] = turn_back(dq, cos[rows, :], sin_a[rows, :], sin_b[rows, :]).astype(BF)


def feed_kernel(
    me, xa, xb, ca, cb, att, gains, gb0, gb1, gc0, gc1,
    mix_a, mix_b, dmid_o, datt_o, g2_o, ob0, ob1, oc0, oc1,
    win, wout, wdn, n2, hid, di, db,
):
    def fill(f, carry):
        values = [pick(me, f, s, place_b, gb0, gb1) for s in range(GRID_S)]
        row = pl.multiple_of(f * 96, 16)
        for s in range(GRID_S):
            win[s, pl.ds(row, 96), :] = values[s][:, :576]
        wout[pl.ds(row, 96), :] = jnp.concatenate([v[:, 576:768] for v in values], axis=1)
        values = [pick(me, f, s, place_c, gc0, gc1) for s in range(GRID_S)]
        for j in range(3):
            row = pl.multiple_of(f * 144 + 48 * j, 16)
            wdn[pl.ds(row, 48), :] = jnp.concatenate(
                [v[:, 192 * j : 192 * j + 192] for v in values], axis=1
            )
        return carry

    lax.fori_loop(0, GRID_F, fill, 0)
    gain = gains[1:2, :]
    gain_grad = jnp.zeros((1, 768), F32)
    for t, (xr, cr, mix) in enumerate(((xa, ca, mix_a), (xb, cb, mix_b))):
        rows = slice(256 * t, 256 * t + 256)
        mid = xr[...].astype(F32) + dot(att[rows, :], wout[...])
        hat, rate = norm_stats(mid)
        n2[rows, :] = (hat * gain).astype(BF)
        branch = None
        for h in range(2):
            down = wdn[576 * h : 576 * h + 576, :]
            a = dot(n2[rows, :], win[h])
            gate = dot(n2[rows, :], win[2 + h])
            cdf = 0.5 * (1.0 + lax.erf(a * math.sqrt(0.5)))
            gelu = a * cdf
            hidden = (gelu * gate).astype(BF)
            hid[h, rows, :] = hidden
            slope = cdf + a * (jnp.exp(-0.5 * a * a) * (1.0 / math.sqrt(2.0 * math.pi)))
            dh = dot_nt(cr[...], down)
            di[h, rows, :] = (dh * gate * slope).astype(BF)
            di[2 + h, rows, :] = (dh * gelu).astype(BF)
            part = dot(hidden, down)
            branch = part if branch is None else branch + part
        mix[...] = (mid + branch).astype(BF)
        dn = None
        for s in range(4):
            part = dot_nt(di[s, rows, :], win[s])
            dn = part if dn is None else dn + part
        gain_grad = gain_grad + jnp.sum(dn * hat, axis=0, keepdims=True)
        dmid = cr[...].astype(F32) + norm_back(dn * gain, hat, rate)
        dmid_o[rows, :] = dmid
        db[rows, :] = dmid.astype(BF)
        datt_o[rows, :] = dot_nt(db[rows, :], wout[...]).astype(BF)
    g2_o[...] = jnp.broadcast_to(gain_grad, (8, 768))

    grad_out = dot_tn(att[...], db[...]).astype(BF)
    for s in range(4):
        grad_in = dot_tn(n2[...], di[s]).astype(BF)
        for f in range(GRID_F):
            rows = slice(96 * f, 96 * f + 96)
            value = jnp.concatenate(
                [grad_in[rows, :], grad_out[rows, 192 * s : 192 * s + 192]], axis=1
            )
            put(me, f, s, place_b, ob0, ob1, value)
    cot = jnp.concatenate([ca[...], cb[...]], axis=0)
    for h in range(2):
        grad_down = dot_tn(hid[h], cot).astype(BF)
        for f in range(4):
            for s in range(4):
                value = jnp.concatenate(
                    [
                        grad_down[144 * f + 48 * j : 144 * f + 48 * j + 48, 192 * s : 192 * s + 192]
                        for j in range(3)
                    ]
                    + [jnp.zeros((48, 192), BF)],
                    axis=1,
                )
                put(me, 4 * h + f, s, place_c, oc0, oc1, value)


def last_kernel(
    me, xa, xb, norm, weight, gains, g2, dq, dka, dkb, dva, dvb, dmid, cos, sin_a, sin_b,
    gt_a, gt_b, ob0, ob1, oc0, oc1, dp,
):
    dp[:, :768] = dq[...]
    for p in range(HEADS // 2):
        cols = slice(PAIR * p, PAIR * p + PAIR)
        dk = dka[:, cols] + dkb[:, cols].astype(F32)
        dp[:, 768 + PAIR * p : 768 + PAIR * p + PAIR] = turn_back(
            dk, cos[...], sin_a[...], sin_b[...]
        ).astype(BF)
    dp[:, 1536:] = (dva[...] + dvb[...].astype(F32)).astype(BF)
    gain = gains[0:1, :]
    gain_grad = jnp.zeros((1, 768), F32)
    for t, (xr, gt) in enumerate(((xa, gt_a), (xb, gt_b))):
        rows = slice(256 * t, 256 * t + 256)
        dn = dot_nt(dp[rows, :], weight[...])
        hat, rate = norm_stats(xr[...].astype(F32))
        gain_grad = gain_grad + jnp.sum(dn * hat, axis=0, keepdims=True)
        gt[...] = (dmid[rows, :] + norm_back(dn * gain, hat, rate)).astype(BF)
    row_i = lax.broadcasted_iota(jnp.int32, (8, 128), 0)
    lane_i = lax.broadcasted_iota(jnp.int32, (8, 128), 1)
    hot = jnp.where((lane_i == row_i + 64) & (row_i < 2), 1.0, 0.0)
    row_w = lax.broadcasted_iota(jnp.int32, (8, 768), 0)
    both = jnp.where(row_w == 0, gain_grad, g2[...])
    gain_cols = dot_tn(both, hot, lax.Precision.HIGHEST)
    for s in range(4):
        part = jnp.concatenate([dp[:, 576 * s : 576 * s + 576], jnp.zeros((512, 64), BF)], axis=1)
        grad = dot_tn(norm[...], part)
        grad = jnp.concatenate([grad[:, :512], grad[:, 512:] + gain_cols], axis=1).astype(BF)
        for f in range(GRID_F):
            put(me, f, s, place_b, ob0, ob1, grad[96 * f : 96 * f + 48, :])
            put(me, f, s, place_c, oc0, oc1, grad[96 * f + 48 : 96 * f + 96, :])


def call(kernel, outs, scratch, *args, flops=0, moved=0, name=None):
    specs = [
        pl.BlockSpec(memory_space=pltpu.SMEM if a.dtype == jnp.int32 else pltpu.VMEM) for a in args
    ]
    return pl.pallas_call(
        kernel,
        out_shape=outs,
        in_specs=specs,
        out_specs=[pl.BlockSpec(memory_space=pltpu.VMEM)] * len(outs),
        scratch_shapes=scratch,
        compiler_params=pltpu.CompilerParams(vmem_limit_bytes=VMEM_LIMIT),
        cost_estimate=pl.CostEstimate(flops=flops, bytes_accessed=moved, transcendentals=0),
        name=name,
    )(*args)


def shape(dims, dtype):
    return jax.ShapeDtypeStruct(dims, dtype)


def split_slots(full, width):
    rows = full.shape[0] // GRID_F
    blocks = full.reshape(GRID_F, rows, GRID_S, width).transpose(0, 2, 1, 3)
    found = []
    for order in (ORDER_B, ORDER_C):
        for core in range(2):
            found.append(jnp.stack([blocks[f, s ^ core] for f, s in codes_of(order)]))
    return found


def join_slots(own, other, order):
    table = {}
    for k, (f, s) in enumerate(codes_of(order)):
        table[f, s] = own[k]
        table[f, s ^ 1] = other[k]
    return jnp.stack([jnp.stack([table[f, s] for s in range(GRID_S)]) for f in range(GRID_F)])


def per_device(tokens, segments, w_qkv, w_out, w_in, w_down, gains, cotangent):
    here = lax.axis_size("fsdp") == GRID_F and lax.axis_size("seq") == GRID_S
    s_index = lax.axis_index("seq")
    x_index = s_index // 2
    partner = s_index ^ 2

    def trade(pair):
        mine = lax.dynamic_index_in_dim(pair, x_index, 0, keepdims=False)
        theirs = lax.dynamic_index_in_dim(pair, 1 - x_index, 0, keepdims=False)
        return mine, swap(theirs, STEPS["x"][0])

    xa, xb = trade(tokens)
    if here:
        me = jnp.stack([lax.axis_index("fsdp"), s_index]).astype(jnp.int32)
        wide = jnp.concatenate(
            [w_qkv, gains.T, jnp.zeros((w_qkv.shape[0], 62), BF)], axis=1
        )
        qkv = gather_part(wide[:48], ORDER_B) + gather_part(wide[48:], ORDER_C)
    else:
        me = jnp.zeros((2,), jnp.int32)

        def whole(w):
            return lax.all_gather(
                lax.all_gather(w, "fsdp", axis=0, tiled=True), "seq", axis=1, tiled=True
            )

        gains_all = lax.all_gather(gains, "fsdp", axis=1, tiled=True).T
        wide = jnp.concatenate(
            [
                jnp.concatenate([block, gains_all, jnp.zeros((768, 62), BF)], axis=1)
                for block in jnp.split(whole(w_qkv), GRID_S, axis=1)
            ],
            axis=1,
        )
        slots = split_slots(wide, 640)
        qkv = (slots[0][:, :48], slots[1][:, :48], slots[2][:, 48:], slots[3][:, 48:])
    sega, segb = trade(segments)
    seg_mine = jnp.concatenate([sega, segb])
    seg_all = jnp.concatenate([seg_mine, swap(seg_mine, STEPS["core"][0])]).astype(F32)
    seg_mine = seg_mine.astype(F32)
    ca, cb = trade(cotangent)
    if here:
        third = w_down.shape[0] // 3
        part_b = jnp.concatenate([w_in, w_out], axis=1)
        part_c = jnp.concatenate(
            [w_down[third * j : third * (j + 1)] for j in range(3)]
            + [jnp.zeros((third, w_down.shape[1]), BF)],
            axis=1,
        )
        rest = gather_part(part_b, ORDER_B) + gather_part(part_c, ORDER_C)
    else:
        slots_in = split_slots(whole(w_in), 576)
        slots_out = split_slots(whole(w_out), 192)
        slots_down = split_slots(whole(w_down), 192)
        rest = tuple(
            jnp.concatenate([slots_in[i], slots_out[i]], axis=2) for i in range(2)
        ) + tuple(
            jnp.concatenate(
                [d[:, :48], d[:, 48:96], d[:, 96:], jnp.zeros_like(d[:, :48])], axis=2
            )
            for d in slots_down[2:]
        )

    rows = tokens.shape[1]
    places = jnp.concatenate(
        [s_index * rows + jnp.arange(rows), partner * rows + jnp.arange(rows)]
    ).astype(F32)
    freqs = jnp.exp(-jnp.arange(32, dtype=F32) * (2.0 * math.log(160000.0) / HEAD))
    angles = places[:, None] * freqs[None, :]
    cosine, sine = jnp.cos(angles), jnp.sin(angles)
    zero = jnp.zeros_like(sine)
    cos = jnp.concatenate([cosine] * 4, axis=1)
    sin_a = jnp.concatenate([-sine, zero] * 2, axis=1)
    sin_b = jnp.concatenate([zero, sine] * 2, axis=1)

    act = shape((512, 768), BF)
    q, k, v, norm, weight, gain_rows = call(
        project_kernel,
        [act, act, act, act, shape((768, 2304), BF), shape((8, 768), F32)],
        [pltpu.VMEM((768, 128), BF)],
        me, xa, xb, *qkv, cos, sin_a, sin_b,
        flops=2 * 512 * 768 * 2304, moved=20_000_000, name="project",
    )
    k_far = swap(k, STEPS["core"][0])
    v_far = swap(v, STEPS["core"][0])

    pair_spec = pl.BlockSpec((512, PAIR), lambda p: (0, p))

    def fixed(dims):
        return pl.BlockSpec(dims, lambda p: (0, 0))

    params = pltpu.CompilerParams(
        vmem_limit_bytes=VMEM_LIMIT, dimension_semantics=("arbitrary",)
    )
    att, lse = pl.pallas_call(
        attend_kernel,
        grid=(HEADS // 2,),
        out_shape=[act, shape((512, 768), F32)],
        in_specs=[pair_spec] * 5 + [fixed((512, 1)), fixed((1, 1024))],
        out_specs=[pair_spec] * 2,
        scratch_shapes=[pltpu.VMEM((512, 1024), F32)],
        compiler_params=params,
        cost_estimate=pl.CostEstimate(
            flops=20_000_000_000, bytes_accessed=8_000_000, transcendentals=6_000_000
        ),
        name="attend",
    )(q, k, k_far, v, v_far, seg_mine[:, None], seg_all[None, :])

    slot_b, slot_c = shape((16, 96, 768), BF), shape((16, 48, 768), BF)
    mix_a, mix_b, dmid, datt, g2, fb0, fb1, fc0, fc1 = call(
        feed_kernel,
        [
            shape((256, 768), BF), shape((256, 768), BF), shape((512, 768), F32), act,
            shape((8, 768), F32), slot_b, slot_b, slot_c, slot_c,
        ],
        [
            pltpu.VMEM((4, 768, 576), BF), pltpu.VMEM((768, 768), BF),
            pltpu.VMEM((1152, 768), BF), pltpu.VMEM((512, 768), BF),
            pltpu.VMEM((2, 512, 576), BF), pltpu.VMEM((4, 512, 576), BF),
            pltpu.VMEM((512, 768), BF),
        ],
        me, xa, xb, ca, cb, att, gain_rows, *rest,
        flops=3 * 2 * 512 * 768 * 4224, moved=30_000_000, name="feed",
    )
    mixed = untrade(mix_a, mix_b, x_index)

    dq, dka, dkb, dva, dvb = pl.pallas_call(
        attend_back_kernel,
        grid=(HEADS // 2,),
        out_shape=[act, shape((512, 768), F32), act, shape((512, 768), F32), act],
        in_specs=[pair_spec] * 8
        + [fixed((1024, 1)), fixed((1, 512))]
        + [fixed((512, PAIR))] * 3,
        out_specs=[pair_spec] * 5,
        scratch_shapes=[pltpu.VMEM((1024, 512), F32)],
        compiler_params=params,
        cost_estimate=pl.CostEstimate(
            flops=50_000_000_000, bytes_accessed=12_000_000, transcendentals=6_000_000
        ),
        name="attend_back",
    )(
        q, k, k_far, v, v_far, att, datt, lse, seg_all[:, None], seg_mine[None, :],
        cos, sin_a, sin_b,
    )
    dk_near = swap(dkb, STEPS["core"][0])
    dv_near = swap(dvb, STEPS["core"][0])

    slot = shape((16, 48, 640), BF)
    gt_a, gt_b, lb0, lb1, lc0, lc1 = call(
        last_kernel,
        [shape((256, 768), BF), shape((256, 768), BF), slot, slot, slot, slot],
        [pltpu.VMEM((512, 2304), BF)],
        me, xa, xb, norm, weight, gain_rows, g2, dq, dka, dk_near, dva, dv_near, dmid,
        cos, sin_a, sin_b,
        flops=4 * 512 * 768 * 2304, moved=20_000_000, name="last",
    )
    grad_tokens = untrade(gt_a, gt_b, x_index)

    if here:
        rest_b = scatter_part(fb0, fb1, ORDER_B)
        rest_c = scatter_part(fc0, fc1, ORDER_C)
        grad_qkv = jnp.concatenate(
            [scatter_part(lb0, lb1, ORDER_B), scatter_part(lc0, lc1, ORDER_C)], axis=0
        )
        grad_in, grad_out = rest_b[:, :576], rest_b[:, 576:]
        grad_down = jnp.concatenate([rest_c[:, 192 * j : 192 * j + 192] for j in range(3)], axis=0)
        grad_gains = grad_qkv[:, 576:578].T
        grad_qkv = grad_qkv[:, :576]
    else:
        full_b = join_slots(fb0, fb1, ORDER_B)
        full_c = join_slots(fc0, fc1, ORDER_C)
        full_q = jnp.concatenate(
            [join_slots(lb0, lb1, ORDER_B), join_slots(lc0, lc1, ORDER_C)], axis=2
        )
        full_d = jnp.concatenate([full_c[..., 192 * j : 192 * j + 192] for j in range(3)], axis=2)

        def share(full):
            flat = full.transpose(0, 2, 1, 3).reshape(-1, GRID_S * full.shape[-1])
            part = lax.psum_scatter(
                flat.astype(F32), "fsdp", scatter_dimension=0, tiled=True
            )
            return lax.psum_scatter(part, "seq", scatter_dimension=1, tiled=True)

        grad_in, grad_out = share(full_b[..., :576]), share(full_b[..., 576:])
        grad_down = share(full_d)
        grad_qkv = share(full_q[..., :576])
        gain_sum = full_q[:, 0, :, 576:578].reshape(768, 2).astype(F32).T
        grad_gains = lax.psum(
            lax.psum_scatter(gain_sum, "fsdp", scatter_dimension=1, tiled=True), "seq"
        )
    return (mixed, grad_tokens, grad_qkv, grad_out, grad_in, grad_down, grad_gains)


def untrade(mine, theirs, x_index):
    back = swap(theirs, STEPS["x"][0])
    first = x_index == 0
    return jnp.stack([jnp.where(first, mine, back), jnp.where(first, back, mine)])


def solution(mesh):
    return jax.shard_map(
        per_device,
        mesh=mesh,
        in_specs=(
            P("fsdp", "seq", None),
            P("fsdp", "seq"),
            P("fsdp", "seq"),
            P("fsdp", "seq"),
            P("fsdp", "seq"),
            P("fsdp", "seq"),
            P(None, "fsdp"),
            P("fsdp", "seq", None),
        ),
        out_specs=(
            P("fsdp", "seq", None),
            P("fsdp", "seq", None),
            P("fsdp", "seq"),
            P("fsdp", "seq"),
            P("fsdp", "seq"),
            P("fsdp", "seq"),
            P(None, "fsdp"),
        ),
        check_vma=False,
    )
```

```python
import functools
import math

import jax
import jax.numpy as jnp
from jax import lax
from jax.experimental import pallas as pl
from jax.experimental.pallas import tpu as pltpu
from jax.sharding import PartitionSpec as P

HEADS = 12
HEAD = 64
PAIR = 2 * HEAD
EPS = 1e-05
FILL = -1000000000.0
BF = jnp.bfloat16
F32 = jnp.float32
VMEM_LIMIT = 60 * 1024 * 1024

STEPS = {
    "x": [("seq", 2)],
    "y": [("fsdp", 1)],
    "z": [("fsdp", 2), ("fsdp", 4), ("fsdp", 6)],
    "core": [("seq", 1)],
}
ORDER_B = ("z", "x", "y")
ORDER_C = ("z", "y", "x")
GRID_F = 8
GRID_S = 4


def swap(value, step):
    axis, flip = step
    size = lax.axis_size(axis)
    return lax.ppermute(value, axis, [(i, i ^ flip) for i in range(size)])


tie = lax.optimization_barrier


def send_z(block):
    return (block,) + tuple(swap(block, step) for step in STEPS["z"])


def cut_rows(blocks, cut):
    return jnp.stack([b[:cut] for b in blocks]), jnp.stack([b[cut:] for b in blocks])


def double(parts, phases):
    return tuple(
        jnp.concatenate([part, swap(part, STEPS[phase][0])], axis=0)
        for part, phase in zip(parts, phases)
    )


def other_core(parts):
    return tuple(swap(part, STEPS["core"][0]) for part in parts)


def add(a, b):
    return (a.astype(F32) + b.astype(F32)).astype(BF)


def halve(parts, phases):
    found = []
    for part, phase in zip(parts, phases):
        count = part.shape[0] // 2
        found.append(add(part[:count], swap(part[count:], STEPS[phase][0])))
    return tuple(found)


def scatter_z(parts):
    whole = [jnp.concatenate([part[i] for part in parts], axis=0) for i in range(4)]
    got = [swap(whole[i + 1], step).astype(F32) for i, step in enumerate(STEPS["z"])]
    return (whole[0].astype(F32) + got[0]) + (got[1] + got[2])


def codes_of(order):
    codes = [(0, 0)]
    for phase in order:
        grown = list(codes)
        for axis, flip in STEPS[phase]:
            for f, s in codes:
                grown.append((f ^ flip, s) if axis == "fsdp" else (f, s ^ flip))
        codes = grown
    return codes


def place_b(xf, xs):
    return (xf >> 1) + 4 * (xs >> 1) + 8 * (xf & 1)


def place_c(xf, xs):
    return (xf >> 1) + 4 * (xf & 1) + 8 * (xs >> 1)


def dot(a, b):
    return jnp.dot(a, b, preferred_element_type=F32)


def dot_nt(a, b, precision=None):
    return lax.dot_general(
        a, b, (((1,), (1,)), ((), ())), preferred_element_type=F32, precision=precision
    )


def dot_tn(a, b, precision=None):
    return lax.dot_general(
        a, b, (((0,), (0,)), ((), ())), preferred_element_type=F32, precision=precision
    )


def norm_stats(x):
    center = x - jnp.mean(x, axis=-1, keepdims=True)
    spread = jnp.mean(center * center, axis=-1, keepdims=True)
    rate = lax.rsqrt(spread + EPS)
    return center * rate, rate


def norm_back(e, hat, rate):
    return rate * (
        e
        - jnp.mean(e, axis=-1, keepdims=True)
        - hat * jnp.mean(e * hat, axis=-1, keepdims=True)
    )


def turn(u, cosine, sine_a, sine_b):
    return u * cosine + pltpu.roll(u, PAIR - 32, 1) * sine_a + pltpu.roll(u, 32, 1) * sine_b


def turn_back(u, cosine, sine_a, sine_b):
    return u * cosine - pltpu.roll(u, PAIR - 32, 1) * sine_a - pltpu.roll(u, 32, 1) * sine_b


def pick(me, f, s, place, own, other):
    xf = me[0] ^ f
    xs = me[1] ^ s
    k = place(xf, xs)
    return lax.select((xs & 1) == 0, own[k], other[k])


def put(me, f, s, place, own, other, value, rows=slice(None)):
    xf = me[0] ^ f
    xs = me[1] ^ s
    k = place(xf, xs)

    @pl.when((xs & 1) == 0)
    def _():
        own[k, rows] = value

    @pl.when((xs & 1) != 0)
    def _():
        other[k, rows] = value


def project_kernel(
    me, xa, xb, gb0, gb1, gc0, gc1, cos, sin_a, sin_b,
    q_o, k_o, v_o, n_o, w_o, g_o, gcol,
):
    def fill(f, carry):
        for part, (place, own, other) in enumerate(
            ((place_b, gb0, gb1), (place_c, gc0, gc1))
        ):
            row = pl.multiple_of(f * 96 + part * 48, 16)
            values = [pick(me, f, s, place, own, other) for s in range(GRID_S)]
            gcol[pl.ds(row, 48), :] = values[0][:, 512:640]
            w_o[pl.ds(row, 48), :] = jnp.concatenate([v[:, :576] for v in values], axis=1)
        return carry

    lax.fori_loop(0, GRID_F, fill, 0)
    row_i = lax.broadcasted_iota(jnp.int32, (8, 128), 0)
    lane_i = lax.broadcasted_iota(jnp.int32, (8, 128), 1)
    hot = jnp.where(lane_i == row_i + 64, 1.0, 0.0).astype(BF)
    gains = dot_nt(hot, gcol[...])
    g_o[...] = gains
    for half, xr in enumerate((xa, xb)):
        hat, _ = norm_stats(xr[...].astype(F32))
        n_o[256 * half : 256 * half + 256, :] = (hat * gains[0:1, :]).astype(BF)
    for j in range(9):
        y = dot(n_o[...], w_o[:, 256 * j : 256 * j + 256])
        if j < 6:
            y = jnp.concatenate(
                [
                    turn(y[:, 128 * i : 128 * i + 128], cos[...], sin_a[...], sin_b[...])
                    for i in range(2)
                ],
                axis=1,
            )
        if j < 3:
            q_o[:, 256 * j : 256 * j + 256] = (y.astype(BF) * 0.125).astype(BF)
        elif j < 6:
            k_o[:, 256 * (j - 3) : 256 * (j - 3) + 256] = y.astype(BF)
        else:
            v_o[:, 256 * (j - 6) : 256 * (j - 6) + 256] = y.astype(BF)


def head_masks():
    lane = lax.broadcasted_iota(jnp.int32, (1, PAIR), 1)
    first = jnp.where(lane < HEAD, 1.0, 0.0)
    return lane < HEAD, (first.astype(BF), (1.0 - first).astype(BF))


def attend_kernel(q, ka, kb, va, vb, seg_col, seg_row, out, lse, bias):
    @pl.when(pl.program_id(0) == 0)
    def _():
        bias[...] = jnp.where(seg_col[...] == seg_row[...], 0.0, FILL)

    lane, masks = head_masks()
    for t in range(2):
        rows = slice(256 * t, 256 * t + 256)
        outs, logs = [], []
        for mask in masks:
            qm = q[rows, :] * mask
            s = jnp.concatenate([dot_nt(qm, ka[...]), dot_nt(qm, kb[...])], axis=1)
            s = s + bias[rows, :]
            peak = jnp.max(s, axis=-1, keepdims=True)
            e = jnp.exp(s - peak)
            total = jnp.sum(e, axis=-1, keepdims=True)
            eb = e.astype(BF)
            o = dot(eb[:, :512], va[...]) + dot(eb[:, 512:], vb[...])
            outs.append(o * (1.0 / total))
            logs.append(peak + jnp.log(total))
        out[rows, :] = jnp.where(lane, outs[0], outs[1]).astype(BF)
        lse[rows, :] = jnp.where(lane, logs[0], logs[1])


def attend_back_kernel(
    q, ka, kb, va, vb, att, datt, lse, seg_col, seg_row, cos, sin_a, sin_b,
    dq_o, dka_o, dkb_o, dva_o, dvb_o, bias,
):
    @pl.when(pl.program_id(0) == 0)
    def _():
        bias[...] = jnp.where(seg_col[...] == seg_row[...], 0.0, FILL)

    lane, masks = head_masks()
    row_i = lax.broadcasted_iota(jnp.int32, (8, PAIR), 0)
    lane_i = lax.broadcasted_iota(jnp.int32, (8, PAIR), 1)
    hot = jnp.where(lane_i == row_i * HEAD, 1.0, 0.0)
    spread = jnp.where((lane_i // HEAD) == row_i, 1.0, 0.0)
    high = lax.Precision.HIGHEST
    log_rows = dot_nt(hot, lse[...], high)
    delta_rows = dot_nt(spread, datt[...].astype(F32) * att[...].astype(F32), high)
    dq_parts = [[None, None], [None, None]]
    dk_parts = [None, None]
    dv_parts = [None, None]
    for side, (k, v) in enumerate(((ka, va), (kb, vb))):
        keys = slice(512 * side, 512 * side + 512)
        for t in range(2):
            rows = slice(256 * t, 256 * t + 256)
            for h, mask in enumerate(masks):
                qm = q[rows, :] * mask
                dm = datt[rows, :] * mask
                s = dot_nt(k[...], qm) + bias[keys, rows]
                p = jnp.exp(s - log_rows[h : h + 1, rows])
                dp = dot_nt(v[...], dm)
                ds = (p * (dp - delta_rows[h : h + 1, rows])).astype(BF)
                dv = dot(p.astype(BF), dm)
                dk = dot(ds, qm)
                dq = dot_tn(ds, k[...])
                dv_parts[side] = dv if dv_parts[side] is None else dv_parts[side] + dv
                dk_parts[side] = dk if dk_parts[side] is None else dk_parts[side] + dk
                old = dq_parts[t][h]
                dq_parts[t][h] = dq if old is None else old + dq
    dka_o[...] = dk_parts[0]
    dkb_o[...] = dk_parts[1].astype(BF)
    dva_o[...] = dv_parts[0]
    dvb_o[...] = dv_parts[1].astype(BF)
    for t in range(2):
        rows = slice(256 * t, 256 * t + 256)
        dq = jnp.where(lane, dq_parts[t][0], dq_parts[t][1]) * 0.125
        dq_o[rows, :] = turn_back(dq, cos[rows, :], sin_a[rows, :], sin_b[rows, :]).astype(BF)


def feed_kernel(
    me, xa, xb, ca, cb, att, gains, gb0, gb1, gc0, gc1,
    mix_a, mix_b, dmid_o, datt_o, g2_o, ob0, ob1, oc0, oc1,
    win, wout, wdn, n2, hid, di, db,
):
    def fill(f, carry):
        values = [pick(me, f, s, place_b, gb0, gb1) for s in range(GRID_S)]
        row = pl.multiple_of(f * 96, 16)
        for s in range(GRID_S):
            win[s, pl.ds(row, 80), :] = values[s][:, :576]
        wout[pl.ds(row, 80), :] = jnp.concatenate([v[:, 576:768] for v in values], axis=1)
        values = [pick(me, f, s, place_c, gc0, gc1) for s in range(GRID_S)]
        row = pl.multiple_of(f * 96 + 80, 16)
        for s in range(GRID_S):
            win[s, pl.ds(row, 16), :] = values[s][:16, :576]
        wout[pl.ds(row, 16), :] = jnp.concatenate([v[:16, 576:768] for v in values], axis=1)
        for j in range(3):
            row = pl.multiple_of(f * 144 + 48 * j, 16)
            wdn[pl.ds(row, 48), :] = jnp.concatenate(
                [v[16:, 192 * j : 192 * j + 192] for v in values], axis=1
            )
        return carry

    lax.fori_loop(0, GRID_F, fill, 0)
    gain = gains[1:2, :]
    gain_grad = jnp.zeros((1, 768), F32)
    for t, (xr, cr, mix) in enumerate(((xa, ca, mix_a), (xb, cb, mix_b))):
        rows = slice(256 * t, 256 * t + 256)
        mid = xr[...].astype(F32) + dot(att[rows, :], wout[...])
        hat, rate = norm_stats(mid)
        n2[rows, :] = (hat * gain).astype(BF)
        branch = None
        for h in range(2):
            down = wdn[576 * h : 576 * h + 576, :]
            a = dot(n2[rows, :], win[h])
            gate = dot(n2[rows, :], win[2 + h])
            cdf = 0.5 * (1.0 + lax.erf(a * math.sqrt(0.5)))
            gelu = a * cdf
            hidden = (gelu * gate).astype(BF)
            hid[h, rows, :] = hidden
            slope = cdf + a * (jnp.exp(-0.5 * a * a) * (1.0 / math.sqrt(2.0 * math.pi)))
            dh = dot_nt(cr[...], down)
            di[h, rows, :] = (dh * gate * slope).astype(BF)
            di[2 + h, rows, :] = (dh * gelu).astype(BF)
            part = dot(hidden, down)
            branch = part if branch is None else branch + part
        mix[...] = (mid + branch).astype(BF)
        dn = None
        for s in range(4):
            part = dot_nt(di[s, rows, :], win[s])
            dn = part if dn is None else dn + part
        gain_grad = gain_grad + jnp.sum(dn * hat, axis=0, keepdims=True)
        dmid = cr[...].astype(F32) + norm_back(dn * gain, hat, rate)
        dmid_o[rows, :] = dmid
        db[rows, :] = dmid.astype(BF)
        datt_o[rows, :] = dot_nt(db[rows, :], wout[...]).astype(BF)
    g2_o[...] = jnp.broadcast_to(gain_grad, (8, 768))

    grad_out = dot_tn(att[...], db[...]).astype(BF)
    for s in range(4):
        grad_in = dot_tn(n2[...], di[s]).astype(BF)
        for f in range(GRID_F):
            rows = slice(96 * f, 96 * f + 96)
            value = jnp.concatenate(
                [grad_in[rows, :], grad_out[rows, 192 * s : 192 * s + 192]], axis=1
            )
            put(me, f, s, place_b, ob0, ob1, value[:80])
            put(me, f, s, place_c, oc0, oc1, value[80:], slice(0, 16))
    cot = jnp.concatenate([ca[...], cb[...]], axis=0)
    for h in range(2):
        grad_down = dot_tn(hid[h], cot).astype(BF)
        for f in range(4):
            for s in range(4):
                value = jnp.concatenate(
                    [
                        grad_down[144 * f + 48 * j : 144 * f + 48 * j + 48, 192 * s : 192 * s + 192]
                        for j in range(3)
                    ]
                    + [jnp.zeros((48, 192), BF)],
                    axis=1,
                )
                put(me, 4 * h + f, s, place_c, oc0, oc1, value, slice(16, 64))


def weight_grad_kernel(
    me, norm, weight, gains, g2, *refs
):
    heads = refs[:15]
    cos, sin_a, sin_b, dp, ob0, ob1, oc0, oc1, grads = refs[15:]
    half = PAIR * 2
    for p in range(3):
        dq, dk, dk_far, dv, dv_far = heads[5 * p : 5 * p + 5]
        at = half * p
        dp[:, at : at + half] = dq[...]
        for i in range(2):
            cols = slice(PAIR * i, PAIR * i + PAIR)
            total = dk[:, cols] + dk_far[:, cols].astype(F32)
            start = 768 + at + PAIR * i
            dp[:, start : start + PAIR] = turn_back(
                total, cos[...], sin_a[...], sin_b[...]
            ).astype(BF)
        dp[:, 1536 + at : 1536 + at + half] = (dv[...] + dv_far[...].astype(F32)).astype(BF)
    row_i = lax.broadcasted_iota(jnp.int32, (8, 128), 0)
    lane_i = lax.broadcasted_iota(jnp.int32, (8, 128), 1)
    hot = jnp.where((lane_i == row_i + 64) & (row_i < 2), 1.0, 0.0)
    total = jnp.zeros((768, 1), F32)
    for s in range(4):
        cols = slice(576 * s, 576 * s + 576)
        grad = dot_tn(norm[...], dp[:, cols])
        total = total + jnp.sum(grad * weight[:, cols].astype(F32), axis=1, keepdims=True)
        grads[s] = jnp.concatenate([grad, jnp.zeros((768, 64), F32)], axis=1).astype(BF)
    row_w = lax.broadcasted_iota(jnp.int32, (8, 768), 0)
    rows = jnp.where(row_w == 0, 1.0 / gains[0:1, :], g2[...])
    columns = dot_tn(rows, hot, lax.Precision.HIGHEST)
    lane = lax.broadcasted_iota(jnp.int32, (1, 128), 1)
    columns = jnp.where(lane == 64, columns * total, columns).astype(BF)
    for s in range(4):
        grads[s, :, 512:] = grads[s, :, 512:] + columns
        for f in range(GRID_F):
            put(me, f, s, place_b, ob0, ob1, grads[s, 96 * f : 96 * f + 48, :])
            put(me, f, s, place_c, oc0, oc1, grads[s, 96 * f + 48 : 96 * f + 96, :])


def token_grad_kernel(xa, xb, weight, gains, dp, dmid, gt_a, gt_b):
    gain = gains[0:1, :]
    for t, (xr, gt) in enumerate(((xa, gt_a), (xb, gt_b))):
        rows = slice(256 * t, 256 * t + 256)
        dn = dot_nt(dp[rows, :], weight[...])
        hat, rate = norm_stats(xr[...].astype(F32))
        gt[...] = (dmid[rows, :] + norm_back(dn * gain, hat, rate)).astype(BF)


def call(kernel, outs, scratch, *args, flops=0, moved=0, name=None):
    specs = [
        pl.BlockSpec(memory_space=pltpu.SMEM if a.dtype == jnp.int32 else pltpu.VMEM) for a in args
    ]
    return pl.pallas_call(
        kernel,
        out_shape=outs,
        in_specs=specs,
        out_specs=[pl.BlockSpec(memory_space=pltpu.VMEM)] * len(outs),
        scratch_shapes=scratch,
        compiler_params=pltpu.CompilerParams(vmem_limit_bytes=VMEM_LIMIT),
        cost_estimate=pl.CostEstimate(flops=flops, bytes_accessed=moved, transcendentals=0),
        name=name,
    )(*args)


def shape(dims, dtype):
    return jax.ShapeDtypeStruct(dims, dtype)


def split_slots(full, width):
    rows = full.shape[0] // GRID_F
    blocks = full.reshape(GRID_F, rows, GRID_S, width).transpose(0, 2, 1, 3)
    found = []
    for order in (ORDER_B, ORDER_C):
        for core in range(2):
            found.append(jnp.stack([blocks[f, s ^ core] for f, s in codes_of(order)]))
    return found


def join_slots(own, other, order):
    table = {}
    for k, (f, s) in enumerate(codes_of(order)):
        table[f, s] = own[k]
        table[f, s ^ 1] = other[k]
    return jnp.stack([jnp.stack([table[f, s] for s in range(GRID_S)]) for f in range(GRID_F)])


def per_device(tokens, segments, w_qkv, w_out, w_in, w_down, gains, cotangent):
    here = lax.axis_size("fsdp") == GRID_F and lax.axis_size("seq") == GRID_S
    s_index = lax.axis_index("seq")
    x_index = s_index // 2
    partner = s_index ^ 2

    def trade(pair):
        mine = lax.dynamic_index_in_dim(pair, x_index, 0, keepdims=False)
        theirs = lax.dynamic_index_in_dim(pair, 1 - x_index, 0, keepdims=False)
        return mine, swap(theirs, STEPS["x"][0])

    def with_segments(i):
        marks = lax.dynamic_index_in_dim(segments, i, 0, keepdims=True).astype(BF)
        marks = jnp.pad(marks, ((0, 15), (0, tokens.shape[2] - marks.shape[1])))
        return jnp.concatenate(
            [lax.dynamic_index_in_dim(tokens, i, 0, keepdims=False), marks], axis=0
        )

    count = tokens.shape[1]
    xa = lax.dynamic_index_in_dim(tokens, x_index, 0, keepdims=False)
    sega = lax.dynamic_index_in_dim(segments, x_index, 0, keepdims=False).astype(F32)
    arrived = swap(with_segments(1 - x_index), STEPS["x"][0])
    if here:
        me = jnp.stack([lax.axis_index("fsdp"), s_index]).astype(jnp.int32)
        wide = jnp.concatenate(
            [w_qkv, gains.T, jnp.zeros((w_qkv.shape[0], 62), BF)], axis=1
        )
        third = w_down.shape[0] // 3
        part_a = jnp.concatenate([w_in, w_out], axis=1)
        part_d = jnp.concatenate(
            [w_down[third * j : third * (j + 1)] for j in range(3)]
            + [jnp.zeros((third, w_down.shape[1]), BF)],
            axis=1,
        )
        rest = jnp.concatenate([part_a, part_d], axis=0)
        held_q = send_z(wide)
        held_q, arrived, rest = tie((held_q, arrived, rest))
        held_r = send_z(rest)
        held_q = double(cut_rows(held_q, 48), ("x", "y"))
        held_q, near_z = tie((held_q, held_r[1]))
        held_r = (held_r[0], near_z) + held_r[2:]
        held_q = double(held_q, ("y", "x"))
        held_q, held_r = tie((held_q, held_r))
        far_q = other_core(held_q)
        held_r = double(cut_rows(held_r, 80), ("x", "y"))
        qkv = (held_q[0], far_q[0], held_q[1], far_q[1])
    else:
        me = jnp.zeros((2,), jnp.int32)

        def whole(w):
            return lax.all_gather(
                lax.all_gather(w, "fsdp", axis=0, tiled=True), "seq", axis=1, tiled=True
            )

        gains_all = lax.all_gather(gains, "fsdp", axis=1, tiled=True).T
        wide = jnp.concatenate(
            [
                jnp.concatenate([block, gains_all, jnp.zeros((768, 62), BF)], axis=1)
                for block in jnp.split(whole(w_qkv), GRID_S, axis=1)
            ],
            axis=1,
        )
        slots = split_slots(wide, 640)
        qkv = (slots[0][:, :48], slots[1][:, :48], slots[2][:, 48:], slots[3][:, 48:])
        slots_in = split_slots(whole(w_in), 576)
        slots_out = split_slots(whole(w_out), 192)
        slots_down = split_slots(whole(w_down), 192)
        both = [jnp.concatenate([slots_in[i], slots_out[i]], axis=2) for i in range(4)]
        downs = [
            jnp.concatenate(
                [d[:, :48], d[:, 48:96], d[:, 96:], jnp.zeros_like(d[:, :48])], axis=2
            )
            for d in slots_down
        ]
        rest = (
            both[0][:, :80], both[1][:, :80],
            jnp.concatenate([both[2][:, 80:], downs[2]], axis=1),
            jnp.concatenate([both[3][:, 80:], downs[3]], axis=1),
        )
    xb = arrived[:count]
    segb = arrived[count, :count].astype(F32)
    seg_mine = jnp.concatenate([sega, segb])
    seg_all = jnp.concatenate([seg_mine, swap(seg_mine, STEPS["core"][0])])

    rows = tokens.shape[1]
    places = jnp.concatenate(
        [s_index * rows + jnp.arange(rows), partner * rows + jnp.arange(rows)]
    ).astype(F32)
    freqs = jnp.exp(-jnp.arange(32, dtype=F32) * (2.0 * math.log(160000.0) / HEAD))
    angles = places[:, None] * freqs[None, :]
    cosine, sine = jnp.cos(angles), jnp.sin(angles)
    zero = jnp.zeros_like(sine)
    cos = jnp.concatenate([cosine] * 4, axis=1)
    sin_a = jnp.concatenate([-sine, zero] * 2, axis=1)
    sin_b = jnp.concatenate([zero, sine] * 2, axis=1)

    act = shape((512, 768), BF)
    q, k, v, norm, weight, gain_rows = call(
        project_kernel,
        [act, act, act, act, shape((768, 2304), BF), shape((8, 768), F32)],
        [pltpu.VMEM((768, 128), BF)],
        me, xa, xb, *qkv, cos, sin_a, sin_b,
        flops=2 * 512 * 768 * 2304, moved=20_000_000, name="project",
    )
    if here:
        q, k, v, held_r, cotangent = tie((q, k, v, held_r, cotangent))
        held_r = double(held_r, ("y", "x"))
    ca, cb = trade(cotangent)
    k_far, v_far = other_core((k, v))

    pair_spec = pl.BlockSpec((512, PAIR), lambda p: (0, p))

    def fixed(dims):
        return pl.BlockSpec(dims, lambda p: (0, 0))

    params = pltpu.CompilerParams(
        vmem_limit_bytes=VMEM_LIMIT, dimension_semantics=("arbitrary",)
    )
    att, lse = pl.pallas_call(
        attend_kernel,
        grid=(HEADS // 2,),
        out_shape=[act, shape((512, 768), F32)],
        in_specs=[pair_spec] * 5 + [fixed((512, 1)), fixed((1, 1024))],
        out_specs=[pair_spec] * 2,
        scratch_shapes=[pltpu.VMEM((512, 1024), F32)],
        compiler_params=params,
        cost_estimate=pl.CostEstimate(
            flops=20_000_000_000, bytes_accessed=8_000_000, transcendentals=6_000_000
        ),
        name="attend",
    )(q, k, k_far, v, v_far, seg_mine[:, None], seg_all[None, :])

    if here:
        att, lse, held_r, cb = tie((att, lse, held_r, cb))
        far_r = other_core(held_r)
        rest = (held_r[0], far_r[0], held_r[1], far_r[1])
    slot_b, slot_c = shape((16, 80, 768), BF), shape((16, 64, 768), BF)
    mix_a, mix_b, dmid, datt, g2, fb0, fb1, fc0, fc1 = call(
        feed_kernel,
        [
            shape((256, 768), BF), shape((256, 768), BF), shape((512, 768), F32), act,
            shape((8, 768), F32), slot_b, slot_b, slot_c, slot_c,
        ],
        [
            pltpu.VMEM((4, 768, 576), BF), pltpu.VMEM((768, 768), BF),
            pltpu.VMEM((1152, 768), BF), pltpu.VMEM((512, 768), BF),
            pltpu.VMEM((2, 512, 576), BF), pltpu.VMEM((4, 512, 576), BF),
            pltpu.VMEM((512, 768), BF),
        ],
        me, xa, xb, ca, cb, att, gain_rows, *rest,
        flops=3 * 2 * 512 * 768 * 4224, moved=30_000_000, name="feed",
    )

    def attend_back(first, *args):
        pair_at = pl.BlockSpec((512, PAIR), lambda p: (0, p + first))
        half = shape((512, 2 * PAIR), BF)
        wide_half = shape((512, 2 * PAIR), F32)
        return pl.pallas_call(
            attend_back_kernel,
            grid=(HEADS // 6,),
            out_shape=[half, wide_half, half, wide_half, half],
            in_specs=[pair_at] * 8
            + [fixed((1024, 1)), fixed((1, 512))]
            + [fixed((512, PAIR))] * 3,
            out_specs=[pair_spec] * 5,
            scratch_shapes=[pltpu.VMEM((1024, 512), F32)],
            compiler_params=params,
            cost_estimate=pl.CostEstimate(
                flops=8_000_000_000, bytes_accessed=4_000_000, transcendentals=2_000_000
            ),
            name="attend_back",
        )(*args)

    attend_args = (
        k, k_far, v, v_far, att, datt, lse, seg_all[:, None], seg_mine[None, :],
        cos, sin_a, sin_b,
    )
    back_a = attend_back(0, q, *attend_args)
    sent = (fb0, fc0), (fb1, fc1)
    acc_r = ()
    mix_far = swap(mix_b, STEPS["x"][0])
    if here:
        far = other_core(sent[1])
        back_a, far, mix_far = tie((back_a, far, mix_far))
        acc_r = tuple(add(o, f) for o, f in zip(sent[0], far))
        acc_r, q = tie((acc_r, q))
        acc_r = halve(acc_r, ("y", "x"))
    mixed = untrade(mix_a, mix_far, x_index)
    far_a = other_core((back_a[2], back_a[4]))
    back_b = attend_back(2, q, *attend_args)
    far_b = other_core((back_b[2], back_b[4]))
    back_c = attend_back(4, q, *attend_args)
    back_c, acc_r = tie((back_c, acc_r))
    far_c = other_core((back_c[2], back_c[4]))
    if here:
        acc_r = halve(acc_r, ("x", "y"))

    slot = shape((16, 48, 640), BF)
    dp, lb0, lb1, lc0, lc1 = call(
        weight_grad_kernel,
        [shape((512, 2304), BF), slot, slot, slot, slot],
        [pltpu.VMEM((4, 768, 640), BF)],
        me, norm, weight, gain_rows, g2,
        *(
            part
            for back, far in ((back_a, far_a), (back_b, far_b), (back_c, far_c))
            for part in (back[0], back[1], far[0], back[3], far[1])
        ),
        cos, sin_a, sin_b,
        flops=2 * 512 * 768 * 2304, moved=20_000_000, name="weight_grad",
    )
    dp, lb0, lb1, lc0, lc1, acc_r = tie((dp, lb0, lb1, lc0, lc1, acc_r))
    if here:
        far = other_core((lb1, lc1))
        rest_sum = scatter_z(acc_r)
        acc_q = tuple(add(o, f) for o, f in zip((lb0, lc0), far))
        acc_q, dp = tie((acc_q, dp))
        acc_q = halve(acc_q, ("y", "x"))
    gt_a, gt_b = call(
        token_grad_kernel,
        [shape((256, 768), BF), shape((256, 768), BF)],
        [],
        xa, xb, weight, gain_rows, dp, dmid,
        flops=2 * 512 * 768 * 2304, moved=10_000_000, name="token_grad",
    )
    gt_far = swap(gt_b, STEPS["x"][0])
    grad_tokens = untrade(gt_a, gt_far, x_index)

    if here:
        acc_q = halve(acc_q, ("x", "y"))
        acc_q, rest_sum = tie((acc_q, rest_sum))
        grad_qkv = scatter_z(acc_q)
        grad_in, grad_out = rest_sum[:96, :576], rest_sum[:96, 576:]
        grad_down = jnp.concatenate(
            [rest_sum[96:, 192 * j : 192 * j + 192] for j in range(3)], axis=0
        )
        grad_gains = grad_qkv[:, 576:578].T
        grad_qkv = grad_qkv[:, :576]
    else:
        full_b = join_slots(fb0, fb1, ORDER_B)
        full_c = join_slots(fc0, fc1, ORDER_C)
        full_q = jnp.concatenate(
            [join_slots(lb0, lb1, ORDER_B), join_slots(lc0, lc1, ORDER_C)], axis=2
        )
        full_i = jnp.concatenate([full_b, full_c[:, :, :16]], axis=2)
        full_d = jnp.concatenate(
            [full_c[:, :, 16:, 192 * j : 192 * j + 192] for j in range(3)], axis=2
        )

        def share(full):
            flat = full.transpose(0, 2, 1, 3).reshape(-1, GRID_S * full.shape[-1])
            part = lax.psum_scatter(
                flat.astype(F32), "fsdp", scatter_dimension=0, tiled=True
            )
            return lax.psum_scatter(part, "seq", scatter_dimension=1, tiled=True)

        grad_in, grad_out = share(full_i[..., :576]), share(full_i[..., 576:])
        grad_down = share(full_d)
        grad_qkv = share(full_q[..., :576])
        gain_sum = full_q[:, 0, :, 576:578].reshape(768, 2).astype(F32).T
        grad_gains = lax.psum(
            lax.psum_scatter(gain_sum, "fsdp", scatter_dimension=1, tiled=True), "seq"
        )
    return (mixed, grad_tokens, grad_qkv, grad_out, grad_in, grad_down, grad_gains)


def untrade(mine, back, x_index):
    first = x_index == 0
    return jnp.stack([jnp.where(first, mine, back), jnp.where(first, back, mine)])


def solution(mesh):
    return jax.shard_map(
        per_device,
        mesh=mesh,
        in_specs=(
            P("fsdp", "seq", None),
            P("fsdp", "seq"),
            P("fsdp", "seq"),
            P("fsdp", "seq"),
            P("fsdp", "seq"),
            P("fsdp", "seq"),
            P(None, "fsdp"),
            P("fsdp", "seq", None),
        ),
        out_specs=(
            P("fsdp", "seq", None),
            P("fsdp", "seq", None),
            P("fsdp", "seq"),
            P("fsdp", "seq"),
            P("fsdp", "seq"),
            P("fsdp", "seq"),
            P(None, "fsdp"),
        ),
        check_vma=False,
    )
```

```python
import functools
import math

import jax
import jax.numpy as jnp
from jax import lax
from jax.experimental import pallas as pl
from jax.experimental.pallas import tpu as pltpu
from jax.sharding import PartitionSpec as P

HEADS = 12
HEAD = 64
PAIR = 2 * HEAD
EPS = 1e-05
FILL = -1000000000.0
BF = jnp.bfloat16
F32 = jnp.float32
VMEM_LIMIT = 60 * 1024 * 1024

STEPS = {
    "x": [("seq", 2)],
    "y": [("fsdp", 1)],
    "z": [("fsdp", 2), ("fsdp", 4), ("fsdp", 6)],
    "core": [("seq", 1)],
}
ORDER_B = ("z", "x", "y")
ORDER_C = ("z", "y", "x")
GRID_F = 8
GRID_S = 4


def swap(value, step):
    axis, flip = step
    size = lax.axis_size(axis)
    return lax.ppermute(value, axis, [(i, i ^ flip) for i in range(size)])


tie = lax.optimization_barrier


def send_z(block):
    return (block,) + tuple(swap(block, step) for step in STEPS["z"])


def cut_rows(blocks, cut):
    return jnp.stack([b[:cut] for b in blocks]), jnp.stack([b[cut:] for b in blocks])


def join(held, got):
    return tuple(jnp.concatenate(pair, axis=0) for pair in zip(held, got))


def interleave(*lists):
    return tuple(piece for part in zip(*lists) for piece in part)


def other_core(parts):
    return tuple(swap(part, STEPS["core"][0]) for part in parts)


def level(value):
    return lax.reduce_precision(value, 8, 7)


def first_sum(own, far, at):
    return level(own[at].astype(F32) + far[at].astype(F32))


def second_sum(own, far, one, at):
    return level(first_sum(own, far, at) + one[at].astype(F32))


def third_sum(own, far, one, two, at):
    return level(second_sum(own, far, one, at) + two[at].astype(F32))


def first_sent(owns, fars):
    return tuple(first_sum(o, f, slice(8, 16)).astype(BF) for o, f in zip(owns, fars))


def second_sent(*lists):
    return tuple(second_sum(*part, slice(4, 8)).astype(BF) for part in zip(*lists))


def third_sent(*lists):
    return [
        jnp.concatenate([third_sum(*part, i) for part in zip(*lists)], axis=0)
        for i in range(4)
    ]


def swap_each(parts, phases):
    return tuple(swap(part, STEPS[phase][0]) for part, phase in zip(parts, phases))


def swap_z(blocks):
    return tuple(swap(blocks[i + 1].astype(BF), step) for i, step in enumerate(STEPS["z"]))


def last_sum(mine, got):
    got = [g.astype(F32) for g in got]
    return (mine + got[0]) + (got[1] + got[2])


def codes_of(order):
    codes = [(0, 0)]
    for phase in order:
        grown = list(codes)
        for axis, flip in STEPS[phase]:
            for f, s in codes:
                grown.append((f ^ flip, s) if axis == "fsdp" else (f, s ^ flip))
        codes = grown
    return codes


def dot(a, b):
    return jnp.dot(a, b, preferred_element_type=F32)


def dot_nt(a, b, precision=None):
    return lax.dot_general(
        a, b, (((1,), (1,)), ((), ())), preferred_element_type=F32, precision=precision
    )


def dot_tn(a, b, precision=None):
    return lax.dot_general(
        a, b, (((0,), (0,)), ((), ())), preferred_element_type=F32, precision=precision
    )


def norm_stats(x):
    center = x - jnp.mean(x, axis=-1, keepdims=True)
    spread = jnp.mean(center * center, axis=-1, keepdims=True)
    rate = lax.rsqrt(spread + EPS)
    return center * rate, rate


def norm_back(e, hat, rate):
    return rate * (
        e
        - jnp.mean(e, axis=-1, keepdims=True)
        - hat * jnp.mean(e * hat, axis=-1, keepdims=True)
    )


def turn(u, cosine, sine_a, sine_b):
    return u * cosine + pltpu.roll(u, PAIR - 32, 1) * sine_a + pltpu.roll(u, 32, 1) * sine_b


def turn_back(u, cosine, sine_a, sine_b):
    return u * cosine - pltpu.roll(u, PAIR - 32, 1) * sine_a - pltpu.roll(u, 32, 1) * sine_b


def owners(me, order, pieces):
    codes = codes_of(order)
    for i, piece in enumerate(pieces):
        far, later = divmod(i, 2)
        for k in range(8):
            f, s = codes[8 * later + k]
            yield piece, k, me[0] ^ f, me[1] ^ (s ^ far)


def results(me, order, near, far):
    for core, out in enumerate((near, far)):
        for k, (f, s) in enumerate(codes_of(order)):
            yield out, k, me[0] ^ f, me[1] ^ (s ^ core)


def rows_at(start, count):
    return pl.ds(pl.multiple_of(start, 16), count)


def await_all(ref, sem):
    pltpu.make_async_copy(ref, ref, sem).wait()


def project_kernel(me, xa, xb, cos, sin_a, sin_b, *refs):
    pieces = refs[:8]
    q_o, kv_o, n_o, w_o, g_o, gcol, buf, sem = refs[8:]
    for order, start, part in ((ORDER_B, 0, pieces[:4]), (ORDER_C, 48, pieces[4:])):
        for piece, k, f, s in owners(me, order, part):
            to = buf.at[s, rows_at(f * 96 + start, 48)]
            pltpu.make_async_copy(piece.at[k], to, sem).start()
    await_all(buf, sem)
    gcol[...] = buf[0, :, 512:640]
    for f in range(GRID_F):
        rows = slice(96 * f, 96 * f + 96)
        w_o[rows, :] = jnp.concatenate([buf[s, rows, :576] for s in range(GRID_S)], axis=1)
    row_i = lax.broadcasted_iota(jnp.int32, (8, 128), 0)
    lane_i = lax.broadcasted_iota(jnp.int32, (8, 128), 1)
    hot = jnp.where(lane_i == row_i + 64, 1.0, 0.0).astype(BF)
    gains = dot_nt(hot, gcol[...])
    g_o[...] = gains
    for half, xr in enumerate((xa, xb)):
        hat, _ = norm_stats(xr[...].astype(F32))
        n_o[256 * half : 256 * half + 256, :] = (hat * gains[0:1, :]).astype(BF)
    for j in range(9):
        y = dot(n_o[...], w_o[:, 256 * j : 256 * j + 256])
        if j < 6:
            y = jnp.concatenate(
                [
                    turn(y[:, 128 * i : 128 * i + 128], cos[...], sin_a[...], sin_b[...])
                    for i in range(2)
                ],
                axis=1,
            )
        if j < 3:
            q_o[:, 256 * j : 256 * j + 256] = (y.astype(BF) * 0.125).astype(BF)
        else:
            kv_o[:, 256 * (j - 3) : 256 * (j - 3) + 256] = y.astype(BF)


def head_masks():
    lane = lax.broadcasted_iota(jnp.int32, (1, PAIR), 1)
    first = jnp.where(lane < HEAD, 1.0, 0.0)
    return lane < HEAD, (first.astype(BF), (1.0 - first).astype(BF))


def attend_kernel(q, ka, kb, va, vb, seg_col, seg_row, out, lse, bias):
    @pl.when(pl.program_id(0) == 0)
    def _():
        bias[...] = jnp.where(seg_col[...] == seg_row[...], 0.0, FILL)

    lane, masks = head_masks()
    for t in range(2):
        rows = slice(256 * t, 256 * t + 256)
        outs, logs = [], []
        for mask in masks:
            qm = q[rows, :] * mask
            s = jnp.concatenate([dot_nt(qm, ka[...]), dot_nt(qm, kb[...])], axis=1)
            s = s + bias[rows, :]
            peak = jnp.max(s, axis=-1, keepdims=True)
            e = jnp.exp(s - peak)
            total = jnp.sum(e, axis=-1, keepdims=True)
            eb = e.astype(BF)
            o = dot(eb[:, :512], va[...]) + dot(eb[:, 512:], vb[...])
            outs.append(o * (1.0 / total))
            logs.append(peak + jnp.log(total))
        out[rows, :] = jnp.where(lane, outs[0], outs[1]).astype(BF)
        lse[rows, :] = jnp.where(lane, logs[0], logs[1])


def attend_back_kernel(
    q, ka, kb, va, vb, att, datt, lse, seg_col, seg_row, cos, sin_a, sin_b,
    dq_o, near_o, far_o, bias,
):
    @pl.when(pl.program_id(0) == 0)
    def _():
        bias[...] = jnp.where(seg_col[...] == seg_row[...], 0.0, FILL)

    lane, masks = head_masks()
    row_i = lax.broadcasted_iota(jnp.int32, (8, PAIR), 0)
    lane_i = lax.broadcasted_iota(jnp.int32, (8, PAIR), 1)
    hot = jnp.where(lane_i == row_i * HEAD, 1.0, 0.0)
    spread = jnp.where((lane_i // HEAD) == row_i, 1.0, 0.0)
    high = lax.Precision.HIGHEST
    log_rows = dot_nt(hot, lse[...], high)
    delta_rows = dot_nt(spread, datt[...].astype(F32) * att[...].astype(F32), high)
    dq_parts = [[None, None], [None, None]]
    dk_parts = [None, None]
    dv_parts = [None, None]
    for side, (k, v) in enumerate(((ka, va), (kb, vb))):
        keys = slice(512 * side, 512 * side + 512)
        for t in range(2):
            rows = slice(256 * t, 256 * t + 256)
            for h, mask in enumerate(masks):
                qm = q[rows, :] * mask
                dm = datt[rows, :] * mask
                s = dot_nt(k[...], qm) + bias[keys, rows]
                p = jnp.exp(s - log_rows[h : h + 1, rows])
                dp = dot_nt(v[...], dm)
                ds = (p * (dp - delta_rows[h : h + 1, rows])).astype(BF)
                dv = dot(p.astype(BF), dm)
                dk = dot(ds, qm)
                dq = dot_tn(ds, k[...])
                dv_parts[side] = dv if dv_parts[side] is None else dv_parts[side] + dv
                dk_parts[side] = dk if dk_parts[side] is None else dk_parts[side] + dk
                old = dq_parts[t][h]
                dq_parts[t][h] = dq if old is None else old + dq
    near_o[:, :PAIR] = dk_parts[0]
    near_o[:, PAIR:] = dv_parts[0]
    far_o[:, :PAIR] = dk_parts[1].astype(BF)
    far_o[:, PAIR:] = dv_parts[1].astype(BF)
    for t in range(2):
        rows = slice(256 * t, 256 * t + 256)
        dq = jnp.where(lane, dq_parts[t][0], dq_parts[t][1]) * 0.125
        dq_o[rows, :] = turn_back(dq, cos[rows, :], sin_a[rows, :], sin_b[rows, :]).astype(BF)


def feed_kernel(me, xa, xb, ca, cb, att, gains, *refs):
    pieces = refs[:8]
    mix_a, mix_b, dmid_o, datt_o, g2_o, near_b, far_b, near_c, far_c = refs[8:17]
    wide, wide_dn, wdn, n2, hid, di, db, grads, grads_dn, sem = refs[17:]
    for piece, k, f, s in owners(me, ORDER_B, pieces[:4]):
        to = wide.at[s, rows_at(f * 96, 80)]
        pltpu.make_async_copy(piece.at[k], to, sem.at[0]).start()
    for piece, k, f, s in owners(me, ORDER_C, pieces[4:]):
        to = wide.at[s, rows_at(f * 96 + 80, 16)]
        pltpu.make_async_copy(piece.at[k, pl.ds(0, 16)], to, sem.at[0]).start()
        to = wide_dn.at[f, s]
        pltpu.make_async_copy(piece.at[k, pl.ds(16, 48)], to, sem.at[1]).start()
    di[:, :, 512:] = jnp.zeros((4, 512, 256), BF)
    await_all(wide, sem.at[0])
    await_all(wide_dn, sem.at[1])
    for f in range(GRID_F):
        for j in range(3):
            wdn[144 * f + 48 * j : 144 * f + 48 * j + 48, :] = jnp.concatenate(
                [wide_dn[f, s, :, 192 * j : 192 * j + 192] for s in range(GRID_S)], axis=1
            )
    gain = gains[1:2, :]
    gain_grad = jnp.zeros((1, 768), F32)
    for t, (xr, cr, mix) in enumerate(((xa, ca, mix_a), (xb, cb, mix_b))):
        rows = slice(256 * t, 256 * t + 256)
        mid = xr[...].astype(F32) + jnp.concatenate(
            [dot(att[rows, :], wide[s, :, 512:])[:, 64:] for s in range(GRID_S)], axis=1
        )
        hat, rate = norm_stats(mid)
        n2[rows, :] = (hat * gain).astype(BF)
        branch = None
        for h in range(2):
            down = wdn[576 * h : 576 * h + 576, :]
            a = dot(n2[rows, :], wide[h, :, :576])
            gate = dot(n2[rows, :], wide[2 + h, :, :576])
            cdf = 0.5 * (1.0 + lax.erf(a * math.sqrt(0.5)))
            gelu = a * cdf
            hidden = (gelu * gate).astype(BF)
            hid[h, rows, :] = hidden
            slope = cdf + a * (jnp.exp(-0.5 * a * a) * (1.0 / math.sqrt(2.0 * math.pi)))
            dh = dot_nt(cr[...], down)
            di[h, rows, :576] = (dh * gate * slope).astype(BF)
            di[2 + h, rows, :576] = (dh * gelu).astype(BF)
            part = dot(hidden, down)
            branch = part if branch is None else branch + part
        mix[...] = (mid + branch).astype(BF)
        dn = None
        for s in range(4):
            part = dot_nt(di[s, rows, :576], wide[s, :, :576])
            dn = part if dn is None else dn + part
        gain_grad = gain_grad + jnp.sum(dn * hat, axis=0, keepdims=True)
        dmid = cr[...].astype(F32) + norm_back(dn * gain, hat, rate)
        dmid_o[rows, :] = dmid
        branch_grad = dmid.astype(BF)
        datt = None
        for s in range(4):
            db[s, rows, :] = jnp.concatenate(
                [jnp.zeros((256, 64), BF), branch_grad[:, 192 * s : 192 * s + 192]], axis=1
            )
            part = dot_nt(db[s, rows, :], wide[s, :, 512:])
            datt = part if datt is None else datt + part
        datt_o[rows, :] = datt.astype(BF)
    g2_o[...] = jnp.broadcast_to(gain_grad, (8, 768))

    for s in range(4):
        grad = dot_tn(n2[...], di[s])
        grads[s, :, :512] = grad[:, :512].astype(BF)
        grads[s, :, 512:] = (grad[:, 512:] + dot_tn(att[...], db[s])).astype(BF)
    for out, k, f, s in results(me, ORDER_B, near_b, far_b):
        start = grads.at[s, rows_at(f * 96, 80)]
        pltpu.make_async_copy(start, out.at[k], sem.at[0]).start()
    for out, k, f, s in results(me, ORDER_C, near_c, far_c):
        start = grads.at[s, rows_at(f * 96 + 80, 16)]
        pltpu.make_async_copy(start, out.at[k, pl.ds(0, 16)], sem.at[0]).start()
    cot = jnp.concatenate([ca[...], cb[...]], axis=0)
    for h in range(2):
        grad_down = dot_tn(hid[h], cot).astype(BF)
        for f in range(4):
            for s in range(4):
                grads_dn[4 * h + f, s] = jnp.concatenate(
                    [
                        grad_down[144 * f + 48 * j : 144 * f + 48 * j + 48, 192 * s : 192 * s + 192]
                        for j in range(3)
                    ]
                    + [jnp.zeros((48, 192), BF)],
                    axis=1,
                )
    for out, k, f, s in results(me, ORDER_C, near_c, far_c):
        to = out.at[k, pl.ds(16, 48)]
        pltpu.make_async_copy(grads_dn.at[f, s], to, sem.at[1]).start()
    await_all(grads, sem.at[0])
    await_all(grads_dn, sem.at[1])


def weight_grad_kernel(
    me, norm, weight, gains, g2, *refs
):
    heads = refs[:6]
    cos, sin_a, sin_b, dp, near_b, far_b, near_c, far_c, grads, sem = refs[6:]
    for p, (at, pairs) in enumerate(((0, 2), (2 * PAIR, 4))):
        dq, near, far = heads[3 * p : 3 * p + 3]
        dp[:, at : at + pairs * PAIR] = dq[...]
        for i in range(pairs):
            cols = slice(2 * PAIR * i, 2 * PAIR * i + 2 * PAIR)
            total = near[:, cols] + far[:, cols].astype(F32)
            start = 768 + at + PAIR * i
            dp[:, start : start + PAIR] = turn_back(
                total[:, :PAIR], cos[...], sin_a[...], sin_b[...]
            ).astype(BF)
            dp[:, 768 + start : 768 + start + PAIR] = total[:, PAIR:].astype(BF)
    row_i = lax.broadcasted_iota(jnp.int32, (8, 128), 0)
    lane_i = lax.broadcasted_iota(jnp.int32, (8, 128), 1)
    hot = jnp.where((lane_i == row_i + 64) & (row_i < 2), 1.0, 0.0)
    total = jnp.zeros((768, 1), F32)
    for s in range(4):
        cols = slice(576 * s, 576 * s + 576)
        grad = dot_tn(norm[...], dp[:, cols])
        total = total + jnp.sum(grad * weight[:, cols].astype(F32), axis=1, keepdims=True)
        grads[s] = jnp.concatenate([grad, jnp.zeros((768, 64), F32)], axis=1).astype(BF)
    row_w = lax.broadcasted_iota(jnp.int32, (8, 768), 0)
    rows = jnp.where(row_w == 0, 1.0 / gains[0:1, :], g2[...])
    columns = dot_tn(rows, hot, lax.Precision.HIGHEST)
    lane = lax.broadcasted_iota(jnp.int32, (1, 128), 1)
    columns = jnp.where(lane == 64, columns * total, columns).astype(BF)
    for s in range(4):
        grads[s, :, 512:] = grads[s, :, 512:] + columns
    for order, start, near, far in ((ORDER_B, 0, near_b, far_b), (ORDER_C, 48, near_c, far_c)):
        for out, k, f, s in results(me, order, near, far):
            held = grads.at[s, rows_at(f * 96 + start, 48)]
            pltpu.make_async_copy(held, out.at[k], sem).start()
    await_all(grads, sem)


def token_grad_kernel(xa, xb, weight, gains, dp, dmid, gt_a, gt_b):
    gain = gains[0:1, :]
    for t, (xr, gt) in enumerate(((xa, gt_a), (xb, gt_b))):
        rows = slice(256 * t, 256 * t + 256)
        dn = dot_nt(dp[rows, :], weight[...])
        hat, rate = norm_stats(xr[...].astype(F32))
        gt[...] = (dmid[rows, :] + norm_back(dn * gain, hat, rate)).astype(BF)


def call(kernel, outs, scratch, *args, flops=0, moved=0, name=None):
    def spec(a):
        space = pltpu.SMEM if a.dtype == jnp.int32 else pltpu.VMEM
        return pl.BlockSpec(memory_space=pl.ANY if len(a.shape) == 3 else space)

    specs = [spec(a) for a in args]
    return pl.pallas_call(
        kernel,
        out_shape=outs,
        in_specs=specs,
        out_specs=[spec(a) for a in outs],
        scratch_shapes=scratch,
        compiler_params=pltpu.CompilerParams(vmem_limit_bytes=VMEM_LIMIT),
        cost_estimate=pl.CostEstimate(flops=flops, bytes_accessed=moved, transcendentals=0),
        name=name,
    )(*args)


def shape(dims, dtype):
    return jax.ShapeDtypeStruct(dims, dtype)


def split_slots(full, width):
    rows = full.shape[0] // GRID_F
    blocks = full.reshape(GRID_F, rows, GRID_S, width).transpose(0, 2, 1, 3)
    found = []
    for order in (ORDER_B, ORDER_C):
        for core in range(2):
            found.append(jnp.stack([blocks[f, s ^ core] for f, s in codes_of(order)]))
    return found


def join_slots(own, other, order):
    table = {}
    for k, (f, s) in enumerate(codes_of(order)):
        table[f, s] = own[k]
        table[f, s ^ 1] = other[k]
    return jnp.stack([jnp.stack([table[f, s] for s in range(GRID_S)]) for f in range(GRID_F)])


def per_device(tokens, segments, w_qkv, w_out, w_in, w_down, gains, cotangent):
    here = lax.axis_size("fsdp") == GRID_F and lax.axis_size("seq") == GRID_S
    s_index = lax.axis_index("seq")
    x_index = s_index // 2
    partner = s_index ^ 2

    def trade(pair):
        mine = lax.dynamic_index_in_dim(pair, x_index, 0, keepdims=False)
        theirs = lax.dynamic_index_in_dim(pair, 1 - x_index, 0, keepdims=False)
        return mine, swap(theirs, STEPS["x"][0])

    def with_segments(i):
        marks = lax.dynamic_index_in_dim(segments, i, 0, keepdims=True).astype(BF)
        marks = jnp.pad(marks, ((0, 15), (0, tokens.shape[2] - marks.shape[1])))
        return jnp.concatenate(
            [lax.dynamic_index_in_dim(tokens, i, 0, keepdims=False), marks], axis=0
        )

    count = tokens.shape[1]
    xa = lax.dynamic_index_in_dim(tokens, x_index, 0, keepdims=False)
    sega = lax.dynamic_index_in_dim(segments, x_index, 0, keepdims=False).astype(F32)
    arrived = swap(with_segments(1 - x_index), STEPS["x"][0])
    if here:
        me = jnp.stack([lax.axis_index("fsdp"), s_index]).astype(jnp.int32)
        wide = jnp.concatenate(
            [w_qkv, gains.T, jnp.zeros((w_qkv.shape[0], 62), BF)], axis=1
        )
        third = w_down.shape[0] // 3
        part_a = jnp.concatenate([w_in, w_out], axis=1)
        part_d = jnp.concatenate(
            [w_down[third * j : third * (j + 1)] for j in range(3)]
            + [jnp.zeros((third, w_down.shape[1]), BF)],
            axis=1,
        )
        rest = jnp.concatenate([part_a, part_d], axis=0)
        held_q = send_z(wide)
        held_q, arrived, rest, cotangent = tie((held_q, arrived, rest, cotangent))
        ca, cb = trade(cotangent)
        held_r = send_z(rest)
        held_q = cut_rows(held_q, 48)
        got = swap_each(held_q, ("x", "y"))
        held_q, got, cb, near_z, far_z = tie((held_q, got, cb, held_r[1], held_r[2]))
        held_q = join(held_q, got)
        later_q = swap_each(held_q, ("y", "x"))
        far_q = other_core(held_q)
        later_q, far_q, last_z = tie((later_q, far_q, held_r[3]))
        held_r = cut_rows((held_r[0], near_z, far_z, last_z), 80)
        far_later_q = other_core(later_q)
        got_r = swap_each(held_r, ("x", "y"))
        qkv = interleave(held_q, later_q, far_q, far_later_q)
    else:
        me = jnp.zeros((2,), jnp.int32)

        def whole(w):
            return lax.all_gather(
                lax.all_gather(w, "fsdp", axis=0, tiled=True), "seq", axis=1, tiled=True
            )

        gains_all = lax.all_gather(gains, "fsdp", axis=1, tiled=True).T
        wide = jnp.concatenate(
            [
                jnp.concatenate([block, gains_all, jnp.zeros((768, 62), BF)], axis=1)
                for block in jnp.split(whole(w_qkv), GRID_S, axis=1)
            ],
            axis=1,
        )
        slots = split_slots(wide, 640)
        qkv = (slots[0][:, :48], slots[1][:, :48], slots[2][:, 48:], slots[3][:, 48:])
        qkv = tuple(half for part in qkv for half in (part[:8], part[8:]))
        slots_in = split_slots(whole(w_in), 576)
        slots_out = split_slots(whole(w_out), 192)
        slots_down = split_slots(whole(w_down), 192)
        both = [jnp.concatenate([slots_in[i], slots_out[i]], axis=2) for i in range(4)]
        downs = [
            jnp.concatenate(
                [d[:, :48], d[:, 48:96], d[:, 96:], jnp.zeros_like(d[:, :48])], axis=2
            )
            for d in slots_down
        ]
        rest = (
            both[0][:, :80], both[1][:, :80],
            jnp.concatenate([both[2][:, 80:], downs[2]], axis=1),
            jnp.concatenate([both[3][:, 80:], downs[3]], axis=1),
        )
        rest = tuple(half for part in rest for half in (part[:8], part[8:]))
        ca, cb = trade(cotangent)
    xb = arrived[:count]
    segb = arrived[count, :count].astype(F32)
    seg_mine = jnp.concatenate([sega, segb])
    seg_all = jnp.concatenate([seg_mine, swap(seg_mine, STEPS["core"][0])])

    rows = tokens.shape[1]
    places = jnp.concatenate(
        [s_index * rows + jnp.arange(rows), partner * rows + jnp.arange(rows)]
    ).astype(F32)
    freqs = jnp.exp(-jnp.arange(32, dtype=F32) * (2.0 * math.log(160000.0) / HEAD))
    angles = places[:, None] * freqs[None, :]
    cosine, sine = jnp.cos(angles), jnp.sin(angles)
    zero = jnp.zeros_like(sine)
    cos = jnp.concatenate([cosine] * 4, axis=1)
    sin_a = jnp.concatenate([-sine, zero] * 2, axis=1)
    sin_b = jnp.concatenate([zero, sine] * 2, axis=1)

    act = shape((512, 768), BF)
    q, kv, norm, weight, gain_rows = call(
        project_kernel,
        [act, shape((512, 1536), BF), act, shape((768, 2304), BF), shape((8, 768), F32)],
        [
            pltpu.VMEM((768, 128), BF), pltpu.VMEM((4, 768, 640), BF),
            pltpu.SemaphoreType.DMA,
        ],
        me, xa, xb, cos, sin_a, sin_b, *qkv,
        flops=10_000_000_000, moved=20_000_000, name="project",
    )
    far_r, later_r = (), ()
    if here:
        q, kv, held_r, got_r = tie((q, kv, held_r, got_r))
        held_r = join(held_r, got_r)
        later_r = swap_each(held_r, ("y", "x"))
        far_r = other_core(held_r)
    kv_far = swap(kv, STEPS["core"][0])

    pair_spec = pl.BlockSpec((512, PAIR), lambda p: (0, p))
    value_spec = pl.BlockSpec((512, PAIR), lambda p: (0, p + HEADS // 2))

    def fixed(dims):
        return pl.BlockSpec(dims, lambda p: (0, 0))

    params = pltpu.CompilerParams(
        vmem_limit_bytes=VMEM_LIMIT, dimension_semantics=("arbitrary",)
    )
    att, lse = pl.pallas_call(
        attend_kernel,
        grid=(HEADS // 2,),
        out_shape=[act, shape((512, 768), F32)],
        in_specs=[pair_spec] * 3 + [value_spec] * 2 + [fixed((512, 1)), fixed((1, 1024))],
        out_specs=[pair_spec] * 2,
        scratch_shapes=[pltpu.VMEM((512, 1024), F32)],
        compiler_params=params,
        cost_estimate=pl.CostEstimate(
            flops=17_000_000_000, bytes_accessed=8_000_000, transcendentals=6_000_000
        ),
        name="attend",
    )(q, kv, kv_far, kv, kv_far, seg_mine[:, None], seg_all[None, :])

    if here:
        att, lse, far_r, later_r = tie((att, lse, far_r, later_r))
        rest = interleave(held_r, later_r, far_r, other_core(later_r))
    slot_b, slot_c = shape((16, 80, 768), BF), shape((16, 64, 768), BF)
    mix_a, mix_b, dmid, datt, g2, fb0, fb1, fc0, fc1 = call(
        feed_kernel,
        [
            shape((256, 768), BF), shape((256, 768), BF), shape((512, 768), F32), act,
            shape((8, 768), F32), slot_b, slot_b, slot_c, slot_c,
        ],
        [
            pltpu.VMEM((4, 768, 768), BF), pltpu.VMEM((8, 4, 48, 768), BF),
            pltpu.VMEM((1152, 768), BF), pltpu.VMEM((512, 768), BF),
            pltpu.VMEM((2, 512, 576), BF), pltpu.VMEM((4, 512, 768), BF),
            pltpu.VMEM((4, 512, 256), BF), pltpu.VMEM((4, 768, 768), BF),
            pltpu.VMEM((8, 4, 48, 768), BF), pltpu.SemaphoreType.DMA((2,)),
        ],
        me, xa, xb, ca, cb, att, gain_rows, *rest,
        flops=35_000_000_000, moved=30_000_000, name="feed",
    )

    def attend_back(first, pairs, *args):
        pair_at = pl.BlockSpec((512, PAIR), lambda p: (0, p + first))
        value_at = pl.BlockSpec((512, PAIR), lambda p: (0, p + first + HEADS // 2))
        both_spec = pl.BlockSpec((512, 2 * PAIR), lambda p: (0, p))
        return pl.pallas_call(
            attend_back_kernel,
            grid=(pairs,),
            out_shape=[
                shape((512, pairs * PAIR), BF),
                shape((512, 2 * pairs * PAIR), F32),
                shape((512, 2 * pairs * PAIR), BF),
            ],
            in_specs=[pair_at] * 3 + [value_at] * 2 + [pair_at] * 3
            + [fixed((1024, 1)), fixed((1, 512))]
            + [fixed((512, PAIR))] * 3,
            out_specs=[pair_spec, both_spec, both_spec],
            scratch_shapes=[pltpu.VMEM((1024, 512), F32)],
            compiler_params=params,
            cost_estimate=pl.CostEstimate(
                flops=6_000_000_000 * pairs, bytes_accessed=4_000_000, transcendentals=2_000_000
            ),
            name="attend_back",
        )(*args)

    attend_args = (
        kv, kv_far, kv, kv_far, att, datt, lse, seg_all[:, None], seg_mine[None, :],
        cos, sin_a, sin_b,
    )
    back_a = attend_back(0, 2, q, *attend_args)
    own_r, far_r, one_r, two_r = (fb0, fc0), (), (), ()
    mix_far = swap(mix_b, STEPS["x"][0])
    if here:
        far_r = other_core((fb1, fc1))
        back_a, far_r, mix_far = tie((back_a, far_r, mix_far))
        sent = first_sent(own_r, far_r)
        sent, q = tie((sent, q))
        one_r = swap_each(sent, ("y", "x"))
    mixed = untrade(mix_a, mix_far, x_index)
    far_a = swap(back_a[2], STEPS["core"][0])
    back_b = attend_back(2, 4, q, *attend_args)
    back_b, one_r = tie((back_b, one_r))
    far_b = swap(back_b[2], STEPS["core"][0])
    if here:
        sent = second_sent(own_r, far_r, one_r)
        sent, far_b = tie((sent, far_b))
        two_r = swap_each(sent, ("x", "y"))

    slot = shape((16, 48, 640), BF)
    dp, lb0, lb1, lc0, lc1 = call(
        weight_grad_kernel,
        [shape((512, 2304), BF), slot, slot, slot, slot],
        [pltpu.VMEM((4, 768, 640), BF), pltpu.SemaphoreType.DMA],
        me, norm, weight, gain_rows, g2,
        *(
            part
            for back, far in ((back_a, far_a), (back_b, far_b))
            for part in (back[0], back[1], far)
        ),
        cos, sin_a, sin_b,
        flops=14_000_000_000, moved=20_000_000, name="weight_grad",
    )
    dp, lb0, lb1, lc0, lc1, two_r = tie((dp, lb0, lb1, lc0, lc1, two_r))
    if here:
        own_q = (lb0, lc0)
        far_q = other_core((lb1, lc1))
        blocks = third_sent(own_r, far_r, one_r, two_r)
        got_r = swap_z(blocks)
        sent, dp = tie((first_sent(own_q, far_q), dp))
        one_q = swap_each(sent, ("y", "x"))
    gt_a, gt_b = call(
        token_grad_kernel,
        [shape((256, 768), BF), shape((256, 768), BF)],
        [],
        xa, xb, weight, gain_rows, dp, dmid,
        flops=8_000_000_000, moved=10_000_000, name="token_grad",
    )
    if here:
        gt_a, gt_b, one_q = tie((gt_a, gt_b, one_q))
        two_q = swap_each(second_sent(own_q, far_q, one_q), ("x", "y"))
    gt_far = swap(gt_b, STEPS["x"][0])
    grad_tokens = untrade(gt_a, gt_far, x_index)

    if here:
        two_q, got_r, mixed = tie((two_q, got_r, mixed))
        rest_sum = last_sum(blocks[0], got_r)
        blocks = third_sent(own_q, far_q, one_q, two_q)
        grad_qkv = last_sum(blocks[0], swap_z(blocks))
        grad_in, grad_out = rest_sum[:96, :576], rest_sum[:96, 576:]
        grad_down = jnp.concatenate(
            [rest_sum[96:, 192 * j : 192 * j + 192] for j in range(3)], axis=0
        )
        grad_gains = grad_qkv[:, 576:578].T
        grad_qkv = grad_qkv[:, :576]
    else:
        full_b = join_slots(fb0, fb1, ORDER_B)
        full_c = join_slots(fc0, fc1, ORDER_C)
        full_q = jnp.concatenate(
            [join_slots(lb0, lb1, ORDER_B), join_slots(lc0, lc1, ORDER_C)], axis=2
        )
        full_i = jnp.concatenate([full_b, full_c[:, :, :16]], axis=2)
        full_d = jnp.concatenate(
            [full_c[:, :, 16:, 192 * j : 192 * j + 192] for j in range(3)], axis=2
        )

        def share(full):
            flat = full.transpose(0, 2, 1, 3).reshape(-1, GRID_S * full.shape[-1])
            part = lax.psum_scatter(
                flat.astype(F32), "fsdp", scatter_dimension=0, tiled=True
            )
            return lax.psum_scatter(part, "seq", scatter_dimension=1, tiled=True)

        grad_in, grad_out = share(full_i[..., :576]), share(full_i[..., 576:])
        grad_down = share(full_d)
        grad_qkv = share(full_q[..., :576])
        gain_sum = full_q[:, 0, :, 576:578].reshape(768, 2).astype(F32).T
        grad_gains = lax.psum(
            lax.psum_scatter(gain_sum, "fsdp", scatter_dimension=1, tiled=True), "seq"
        )
    return (mixed, grad_tokens, grad_qkv, grad_out, grad_in, grad_down, grad_gains)


def untrade(mine, back, x_index):
    first = x_index == 0
    return jnp.stack([jnp.where(first, mine, back), jnp.where(first, back, mine)])


def solution(mesh):
    return jax.shard_map(
        per_device,
        mesh=mesh,
        in_specs=(
            P("fsdp", "seq", None),
            P("fsdp", "seq"),
            P("fsdp", "seq"),
            P("fsdp", "seq"),
            P("fsdp", "seq"),
            P("fsdp", "seq"),
            P(None, "fsdp"),
            P("fsdp", "seq", None),
        ),
        out_specs=(
            P("fsdp", "seq", None),
            P("fsdp", "seq", None),
            P("fsdp", "seq"),
            P("fsdp", "seq"),
            P("fsdp", "seq"),
            P("fsdp", "seq"),
            P(None, "fsdp"),
        ),
        check_vma=False,
    )
```

```python
import functools
import math

import jax
import jax.numpy as jnp
from jax import lax
from jax.experimental import pallas as pl
from jax.experimental.pallas import tpu as pltpu
from jax.sharding import PartitionSpec as P

HEADS = 12
HEAD = 64
PAIR = 2 * HEAD
EPS = 1e-05
FILL = -1000000000.0
BF = jnp.bfloat16
F32 = jnp.float32
VMEM_LIMIT = 60 * 1024 * 1024

STEPS = {
    "x": [("seq", 2)],
    "y": [("fsdp", 1)],
    "z": [("fsdp", 2), ("fsdp", 4), ("fsdp", 6)],
    "core": [("seq", 1)],
}
ORDER_B = ("z", "x", "y")
ORDER_C = ("z", "y", "x")
GRID_F = 8
GRID_S = 4


def swap(value, step):
    axis, flip = step
    size = lax.axis_size(axis)
    return lax.ppermute(value, axis, [(i, i ^ flip) for i in range(size)])


tie = lax.optimization_barrier


def send_z(block):
    return (block,) + tuple(swap(block, step) for step in STEPS["z"])


def cut_rows(blocks, cut):
    return jnp.stack([b[:cut] for b in blocks]), jnp.stack([b[cut:] for b in blocks])


def join(held, got):
    return tuple(jnp.concatenate(pair, axis=0) for pair in zip(held, got))


def interleave(*lists):
    return tuple(piece for part in zip(*lists) for piece in part)


def other_core(parts):
    return tuple(swap(part, STEPS["core"][0]) for part in parts)


def level(value):
    return lax.reduce_precision(value, 8, 7)


def first_sum(own, far, at):
    return level(own[at].astype(F32) + far[at].astype(F32))


def second_sum(own, far, one, at):
    return level(first_sum(own, far, at) + one[at].astype(F32))


def third_sum(own, far, one, two, at):
    return level(second_sum(own, far, one, at) + two[at].astype(F32))


def first_sent(owns, fars):
    return tuple(first_sum(o, f, slice(8, 16)).astype(BF) for o, f in zip(owns, fars))


def second_sent(*lists):
    return tuple(second_sum(*part, slice(4, 8)).astype(BF) for part in zip(*lists))


def third_sums(*lists):
    return [third_sum(*part, slice(0, 4)).astype(BF) for part in zip(*lists)]


def z_blocks(sums):
    return [jnp.concatenate([part[i] for part in sums], axis=0) for i in range(4)]


def swap_each(parts, phases):
    return tuple(swap(part, STEPS[phase][0]) for part, phase in zip(parts, phases))


def swap_z(blocks):
    return tuple(swap(blocks[i + 1], step) for i, step in enumerate(STEPS["z"]))


def last_sum(mine, got):
    got = [g.astype(F32) for g in got]
    return (mine.astype(F32) + got[0]) + (got[1] + got[2])


def codes_of(order):
    codes = [(0, 0)]
    for phase in order:
        grown = list(codes)
        for axis, flip in STEPS[phase]:
            for f, s in codes:
                grown.append((f ^ flip, s) if axis == "fsdp" else (f, s ^ flip))
        codes = grown
    return codes


def dot(a, b):
    return jnp.dot(a, b, preferred_element_type=F32)


def dot_nt(a, b, precision=None):
    return lax.dot_general(
        a, b, (((1,), (1,)), ((), ())), preferred_element_type=F32, precision=precision
    )


def dot_tn(a, b, precision=None):
    return lax.dot_general(
        a, b, (((0,), (0,)), ((), ())), preferred_element_type=F32, precision=precision
    )


def norm_stats(x):
    center = x - jnp.mean(x, axis=-1, keepdims=True)
    spread = jnp.mean(center * center, axis=-1, keepdims=True)
    rate = lax.rsqrt(spread + EPS)
    return center * rate, rate


def norm_back(e, hat, rate):
    return rate * (
        e
        - jnp.mean(e, axis=-1, keepdims=True)
        - hat * jnp.mean(e * hat, axis=-1, keepdims=True)
    )


def turn(u, cosine, sine_a, sine_b):
    return u * cosine + pltpu.roll(u, PAIR - 32, 1) * sine_a + pltpu.roll(u, 32, 1) * sine_b


def turn_back(u, cosine, sine_a, sine_b):
    return u * cosine - pltpu.roll(u, PAIR - 32, 1) * sine_a - pltpu.roll(u, 32, 1) * sine_b


def owners(me, order, pieces):
    codes = codes_of(order)
    for i, piece in enumerate(pieces):
        far, later = divmod(i, 2)
        for k in range(8):
            f, s = codes[8 * later + k]
            yield piece, k, me[0] ^ f, me[1] ^ (s ^ far)


def results(me, order, near, far):
    for core, out in enumerate((near, far)):
        for k, (f, s) in enumerate(codes_of(order)):
            yield out, k, me[0] ^ f, me[1] ^ (s ^ core)


def rows_at(start, count):
    return pl.ds(pl.multiple_of(start, 16), count)


def await_all(ref, sem):
    pltpu.make_async_copy(ref, ref, sem).wait()


def project_kernel(me, xa, xb, cos, sin_a, sin_b, *refs):
    pieces = refs[:8]
    q_o, kv_o, n_o, w_o, g_o, gcol, buf, sem = refs[8:]
    for order, start, part in ((ORDER_B, 0, pieces[:4]), (ORDER_C, 48, pieces[4:])):
        for piece, k, f, s in owners(me, order, part):
            to = buf.at[s, rows_at(f * 96 + start, 48)]
            pltpu.make_async_copy(piece.at[k], to, sem).start()
    await_all(buf, sem)
    gcol[...] = buf[0, :, 512:640]
    for f in range(GRID_F):
        rows = slice(96 * f, 96 * f + 96)
        w_o[rows, :] = jnp.concatenate([buf[s, rows, :576] for s in range(GRID_S)], axis=1)
    row_i = lax.broadcasted_iota(jnp.int32, (8, 128), 0)
    lane_i = lax.broadcasted_iota(jnp.int32, (8, 128), 1)
    hot = jnp.where(lane_i == row_i + 64, 1.0, 0.0).astype(BF)
    gains = dot_nt(hot, gcol[...])
    g_o[...] = gains
    for half, xr in enumerate((xa, xb)):
        hat, _ = norm_stats(xr[...].astype(F32))
        n_o[256 * half : 256 * half + 256, :] = (hat * gains[0:1, :]).astype(BF)
    for j in range(9):
        y = dot(n_o[...], w_o[:, 256 * j : 256 * j + 256])
        if j < 6:
            y = jnp.concatenate(
                [
                    turn(y[:, 128 * i : 128 * i + 128], cos[...], sin_a[...], sin_b[...])
                    for i in range(2)
                ],
                axis=1,
            )
        if j < 3:
            q_o[:, 256 * j : 256 * j + 256] = (y.astype(BF) * 0.125).astype(BF)
        else:
            kv_o[:, 256 * (j - 3) : 256 * (j - 3) + 256] = y.astype(BF)


def head_masks():
    lane = lax.broadcasted_iota(jnp.int32, (1, PAIR), 1)
    first = jnp.where(lane < HEAD, 1.0, 0.0)
    return lane < HEAD, (first.astype(BF), (1.0 - first).astype(BF))


def attend_kernel(q, ka, kb, va, vb, seg_col, seg_row, out, lse, bias):
    @pl.when(pl.program_id(0) == 0)
    def _():
        bias[...] = jnp.where(seg_col[...] == seg_row[...], 0.0, FILL)

    lane, masks = head_masks()
    column = lax.broadcasted_iota(jnp.int32, (512, PAIR), 1)
    ones = jnp.where(column == 0, 1.0, 0.0).astype(BF)
    near, far = (jnp.concatenate([v[...], ones], axis=1) for v in (va, vb))
    for t in range(4):
        rows = slice(128 * t, 128 * t + 128)
        outs, logs = [], []
        for mask in masks:
            qm = q[rows, :] * mask
            sa = dot_nt(qm, ka[...]) + bias[rows, :512]
            sb = dot_nt(qm, kb[...]) + bias[rows, 512:]
            peak = jnp.max(jnp.maximum(sa, sb), axis=-1, keepdims=True)
            ea = jnp.exp(sa - peak).astype(BF)
            eb = jnp.exp(sb - peak).astype(BF)
            o = dot(ea, near) + dot(eb, far)
            total = o[:, PAIR : PAIR + 1]
            outs.append(o[:, :PAIR] * (1.0 / total))
            logs.append(peak + jnp.log(total))
        out[rows, :] = jnp.where(lane, outs[0], outs[1]).astype(BF)
        lse[rows, :] = jnp.where(lane, logs[0], logs[1])


def attend_back_kernel(
    q, ka, kb, va, vb, att, datt, lse, seg_col, seg_row, cos, sin_a, sin_b,
    dq_o, near_o, far_o, bias,
):
    @pl.when(pl.program_id(0) == 0)
    def _():
        bias[...] = jnp.where(seg_col[...] == seg_row[...], 0.0, FILL)

    lane, masks = head_masks()
    row_i = lax.broadcasted_iota(jnp.int32, (8, PAIR), 0)
    lane_i = lax.broadcasted_iota(jnp.int32, (8, PAIR), 1)
    hot = jnp.where(lane_i == row_i * HEAD, 1.0, 0.0)
    spread = jnp.where((lane_i // HEAD) == row_i, 1.0, 0.0)
    high = lax.Precision.HIGHEST
    log_rows = dot_nt(hot, lse[...], high)
    delta_rows = dot_nt(spread, datt[...].astype(F32) * att[...].astype(F32), high)
    dq_parts = [[None, None], [None, None]]
    dk_parts = [None, None]
    dv_parts = [None, None]
    for side, (k, v) in enumerate(((ka, va), (kb, vb))):
        keys = slice(512 * side, 512 * side + 512)
        for t in range(2):
            rows = slice(256 * t, 256 * t + 256)
            for h, mask in enumerate(masks):
                qm = q[rows, :] * mask
                dm = datt[rows, :] * mask
                s = dot_nt(k[...], qm) + bias[keys, rows]
                p = jnp.exp(s - log_rows[h : h + 1, rows])
                dp = dot_nt(v[...], dm)
                ds = (p * (dp - delta_rows[h : h + 1, rows])).astype(BF)
                dv = dot(p.astype(BF), dm)
                dk = dot(ds, qm)
                dq = dot_tn(ds, k[...])
                dv_parts[side] = dv if dv_parts[side] is None else dv_parts[side] + dv
                dk_parts[side] = dk if dk_parts[side] is None else dk_parts[side] + dk
                old = dq_parts[t][h]
                dq_parts[t][h] = dq if old is None else old + dq
    near_o[:, :PAIR] = dk_parts[0]
    near_o[:, PAIR:] = dv_parts[0]
    far_o[:, :PAIR] = dk_parts[1].astype(BF)
    far_o[:, PAIR:] = dv_parts[1].astype(BF)
    for t in range(2):
        rows = slice(256 * t, 256 * t + 256)
        dq = jnp.where(lane, dq_parts[t][0], dq_parts[t][1]) * 0.125
        dq_o[rows, :] = turn_back(dq, cos[rows, :], sin_a[rows, :], sin_b[rows, :]).astype(BF)


def feed_kernel(me, place, xa, xb, ca, cb, att, gains, *refs):
    pieces = refs[:8]
    mix_pair, mix_b, dmid_o, datt_o, g2_o, near_b, far_b, near_c, far_c = refs[8:17]
    wide, wide_dn, wdn, n2, hid, di, db, grads, grads_dn, flip, sem, mix_a = refs[17:]
    for piece, k, f, s in owners(me, ORDER_B, pieces[:4]):
        to = wide.at[s, rows_at(f * 96, 80)]
        pltpu.make_async_copy(piece.at[k], to, sem.at[0]).start()
    for piece, k, f, s in owners(me, ORDER_C, pieces[4:]):
        to = wide.at[s, rows_at(f * 96 + 80, 16)]
        pltpu.make_async_copy(piece.at[k, pl.ds(0, 16)], to, sem.at[0]).start()
        to = wide_dn.at[f, s]
        pltpu.make_async_copy(piece.at[k, pl.ds(16, 48)], to, sem.at[1]).start()
    di[:, :, 512:] = jnp.zeros((4, 512, 256), BF)
    await_all(wide, sem.at[0])
    await_all(wide_dn, sem.at[1])
    for f in range(GRID_F):
        for j in range(3):
            wdn[144 * f + 48 * j : 144 * f + 48 * j + 48, :] = jnp.concatenate(
                [wide_dn[f, s, :, 192 * j : 192 * j + 192] for s in range(GRID_S)], axis=1
            )
    gain = gains[1:2, :]
    gain_grad = jnp.zeros((1, 768), F32)
    for t, (xr, cr, mix) in enumerate(((xa, ca, mix_a), (xb, cb, mix_b))):
        rows = slice(256 * t, 256 * t + 256)
        mid = xr[...].astype(F32) + jnp.concatenate(
            [dot(att[rows, :], wide[s, :, 512:])[:, 64:] for s in range(GRID_S)], axis=1
        )
        hat, rate = norm_stats(mid)
        n2[rows, :] = (hat * gain).astype(BF)
        branch = None
        for h in range(2):
            down = wdn[576 * h : 576 * h + 576, :]
            a = dot(n2[rows, :], wide[h, :, :576])
            gate = dot(n2[rows, :], wide[2 + h, :, :576])
            cdf = 0.5 * (1.0 + lax.erf(a * math.sqrt(0.5)))
            gelu = a * cdf
            hidden = (gelu * gate).astype(BF)
            hid[h, rows, :] = hidden
            slope = cdf + a * (jnp.exp(-0.5 * a * a) * (1.0 / math.sqrt(2.0 * math.pi)))
            dh = dot_nt(cr[...], down)
            di[h, rows, :576] = (dh * gate * slope).astype(BF)
            di[2 + h, rows, :576] = (dh * gelu).astype(BF)
            part = dot(hidden, down)
            branch = part if branch is None else branch + part
        mix[...] = (mid + branch).astype(BF)
        dn = None
        for s in range(4):
            part = dot_nt(di[s, rows, :576], wide[s, :, :576])
            dn = part if dn is None else dn + part
        gain_grad = gain_grad + jnp.sum(dn * hat, axis=0, keepdims=True)
        dmid = cr[...].astype(F32) + norm_back(dn * gain, hat, rate)
        dmid_o[rows, :] = dmid
        branch_grad = dmid.astype(BF)
        datt = None
        for s in range(4):
            db[s, rows, :] = jnp.concatenate(
                [jnp.zeros((256, 64), BF), branch_grad[:, 192 * s : 192 * s + 192]], axis=1
            )
            part = dot_nt(db[s, rows, :], wide[s, :, 512:])
            datt = part if datt is None else datt + part
        datt_o[rows, :] = datt.astype(BF)
    g2_o[...] = jnp.broadcast_to(gain_grad, (8, 768))

    own = pltpu.make_async_copy(mix_a, mix_pair.at[place[1] >> 1], sem.at[2])
    own.start()
    flip[0] = n2[...].T
    flip[1] = att[...].T
    for s in range(4):
        grad = dot(flip[0], di[s])
        grads[s, :, :512] = grad[:, :512].astype(BF)
        grads[s, :, 512:] = (grad[:, 512:] + dot(flip[1], db[s])).astype(BF)
    for out, k, f, s in results(me, ORDER_B, near_b, far_b):
        start = grads.at[s, rows_at(f * 96, 80)]
        pltpu.make_async_copy(start, out.at[k], sem.at[0]).start()
    for out, k, f, s in results(me, ORDER_C, near_c, far_c):
        start = grads.at[s, rows_at(f * 96 + 80, 16)]
        pltpu.make_async_copy(start, out.at[k, pl.ds(0, 16)], sem.at[0]).start()
    cot = jnp.concatenate([ca[...], cb[...]], axis=0)
    for h in range(2):
        grad_down = dot_tn(hid[h], cot).astype(BF)
        for f in range(4):
            for s in range(4):
                grads_dn[4 * h + f, s] = jnp.concatenate(
                    [
                        grad_down[144 * f + 48 * j : 144 * f + 48 * j + 48, 192 * s : 192 * s + 192]
                        for j in range(3)
                    ]
                    + [jnp.zeros((48, 192), BF)],
                    axis=1,
                )
    for out, k, f, s in results(me, ORDER_C, near_c, far_c):
        to = out.at[k, pl.ds(16, 48)]
        pltpu.make_async_copy(grads_dn.at[f, s], to, sem.at[1]).start()
    await_all(grads, sem.at[0])
    await_all(grads_dn, sem.at[1])
    own.wait()


def weight_grad_kernel(
    me, norm, weight, gains, g2, *refs
):
    heads = refs[:6]
    cos, sin_a, sin_b, dp, near_b, far_b, near_c, far_c, grads, flip, sem = refs[6:]
    for p, (at, pairs) in enumerate(((0, 2), (2 * PAIR, 4))):
        dq, near, far = heads[3 * p : 3 * p + 3]
        dp[:, at : at + pairs * PAIR] = dq[...]
        for i in range(pairs):
            cols = slice(2 * PAIR * i, 2 * PAIR * i + 2 * PAIR)
            total = near[:, cols] + far[:, cols].astype(F32)
            start = 768 + at + PAIR * i
            dp[:, start : start + PAIR] = turn_back(
                total[:, :PAIR], cos[...], sin_a[...], sin_b[...]
            ).astype(BF)
            dp[:, 768 + start : 768 + start + PAIR] = total[:, PAIR:].astype(BF)
    row_i = lax.broadcasted_iota(jnp.int32, (8, 128), 0)
    lane_i = lax.broadcasted_iota(jnp.int32, (8, 128), 1)
    hot = jnp.where((lane_i == row_i + 64) & (row_i < 2), 1.0, 0.0)
    total = jnp.zeros((768, 1), F32)
    flip[...] = norm[...].T
    for s in range(4):
        cols = slice(576 * s, 576 * s + 576)
        grad = dot(flip[...], dp[:, cols])
        total = total + jnp.sum(grad * weight[:, cols].astype(F32), axis=1, keepdims=True)
        grads[s] = jnp.concatenate([grad, jnp.zeros((768, 64), F32)], axis=1).astype(BF)
    row_w = lax.broadcasted_iota(jnp.int32, (8, 768), 0)
    rows = jnp.where(row_w == 0, 1.0 / gains[0:1, :], g2[...])
    columns = dot_tn(rows, hot, lax.Precision.HIGHEST)
    lane = lax.broadcasted_iota(jnp.int32, (1, 128), 1)
    columns = jnp.where(lane == 64, columns * total, columns).astype(BF)
    for s in range(4):
        grads[s, :, 512:] = grads[s, :, 512:] + columns
    for order, start, near, far in ((ORDER_B, 0, near_b, far_b), (ORDER_C, 48, near_c, far_c)):
        for out, k, f, s in results(me, order, near, far):
            held = grads.at[s, rows_at(f * 96 + start, 48)]
            pltpu.make_async_copy(held, out.at[k], sem).start()
    await_all(grads, sem)


def token_grad_kernel(place, xa, xb, weight, gains, dp, dmid, gt_pair, gt_b, gt_a, sem):
    gain = gains[0:1, :]
    for t, (xr, gt) in enumerate(((xa, gt_a), (xb, gt_b))):
        rows = slice(256 * t, 256 * t + 256)
        dn = dot_nt(dp[rows, :], weight[...])
        hat, rate = norm_stats(xr[...].astype(F32))
        gt[...] = (dmid[rows, :] + norm_back(dn * gain, hat, rate)).astype(BF)
    own = pltpu.make_async_copy(gt_a, gt_pair.at[place[1] >> 1], sem)
    own.start()
    own.wait()


def call(kernel, outs, scratch, *args, flops=0, moved=0, name=None):
    def spec(a):
        space = pltpu.SMEM if a.dtype == jnp.int32 else pltpu.VMEM
        return pl.BlockSpec(memory_space=pl.ANY if len(a.shape) == 3 else space)

    specs = [spec(a) for a in args]
    return pl.pallas_call(
        kernel,
        out_shape=outs,
        in_specs=specs,
        out_specs=[spec(a) for a in outs],
        scratch_shapes=scratch,
        compiler_params=pltpu.CompilerParams(vmem_limit_bytes=VMEM_LIMIT),
        cost_estimate=pl.CostEstimate(flops=flops, bytes_accessed=moved, transcendentals=0),
        name=name,
    )(*args)


def shape(dims, dtype):
    return jax.ShapeDtypeStruct(dims, dtype)


def split_slots(full, width):
    rows = full.shape[0] // GRID_F
    blocks = full.reshape(GRID_F, rows, GRID_S, width).transpose(0, 2, 1, 3)
    found = []
    for order in (ORDER_B, ORDER_C):
        for core in range(2):
            found.append(jnp.stack([blocks[f, s ^ core] for f, s in codes_of(order)]))
    return found


def join_slots(own, other, order):
    table = {}
    for k, (f, s) in enumerate(codes_of(order)):
        table[f, s] = own[k]
        table[f, s ^ 1] = other[k]
    return jnp.stack([jnp.stack([table[f, s] for s in range(GRID_S)]) for f in range(GRID_F)])


def per_device(tokens, segments, w_qkv, w_out, w_in, w_down, gains, cotangent):
    here = lax.axis_size("fsdp") == GRID_F and lax.axis_size("seq") == GRID_S
    s_index = lax.axis_index("seq")
    x_index = s_index // 2
    partner = s_index ^ 2

    def trade(pair):
        mine = lax.dynamic_index_in_dim(pair, x_index, 0, keepdims=False)
        theirs = lax.dynamic_index_in_dim(pair, 1 - x_index, 0, keepdims=False)
        return mine, swap(theirs, STEPS["x"][0])

    def with_segments(i):
        marks = lax.dynamic_index_in_dim(segments, i, 0, keepdims=True).astype(BF)
        marks = jnp.pad(marks, ((0, 15), (0, tokens.shape[2] - marks.shape[1])))
        return jnp.concatenate(
            [lax.dynamic_index_in_dim(tokens, i, 0, keepdims=False), marks], axis=0
        )

    count = tokens.shape[1]
    place = jnp.stack([lax.axis_index("fsdp"), s_index]).astype(jnp.int32)
    xa = lax.dynamic_index_in_dim(tokens, x_index, 0, keepdims=False)
    sega = lax.dynamic_index_in_dim(segments, x_index, 0, keepdims=False).astype(F32)
    arrived = swap(with_segments(1 - x_index), STEPS["x"][0])
    if here:
        me = place
        wide = jnp.concatenate(
            [w_qkv, gains.T, jnp.zeros((w_qkv.shape[0], 62), BF)], axis=1
        )
        third = w_down.shape[0] // 3
        part_a = jnp.concatenate([w_in, w_out], axis=1)
        part_d = jnp.concatenate(
            [w_down[third * j : third * (j + 1)] for j in range(3)]
            + [jnp.zeros((third, w_down.shape[1]), BF)],
            axis=1,
        )
        rest = jnp.concatenate([part_a, part_d], axis=0)
        held_q = send_z(wide)
        held_q, arrived, rest, cotangent = tie((held_q, arrived, rest, cotangent))
        ca, cb = trade(cotangent)
        near_z, far_z = (swap(rest, step) for step in STEPS["z"][:2])
        held_q = cut_rows(held_q, 48)
        got = swap_each(held_q, ("x", "y"))
        held_q, got, near_z, far_z, rest, cb = tie((held_q, got, near_z, far_z, rest, cb))
        held_q = join(held_q, got)
        later_q = swap_each(held_q, ("y", "x"))
        far_q = other_core(held_q)
        last_z = swap(rest, STEPS["z"][2])
        later_q, far_q, last_z = tie((later_q, far_q, last_z))
        held_r = cut_rows((rest, near_z, far_z, last_z), 80)
        far_later_q = other_core(later_q)
        got_r = swap_each(held_r, ("x", "y"))
        qkv = interleave(held_q, later_q, far_q, far_later_q)
    else:
        me = jnp.zeros((2,), jnp.int32)

        def whole(w):
            return lax.all_gather(
                lax.all_gather(w, "fsdp", axis=0, tiled=True), "seq", axis=1, tiled=True
            )

        gains_all = lax.all_gather(gains, "fsdp", axis=1, tiled=True).T
        wide = jnp.concatenate(
            [
                jnp.concatenate([block, gains_all, jnp.zeros((768, 62), BF)], axis=1)
                for block in jnp.split(whole(w_qkv), GRID_S, axis=1)
            ],
            axis=1,
        )
        slots = split_slots(wide, 640)
        qkv = (slots[0][:, :48], slots[1][:, :48], slots[2][:, 48:], slots[3][:, 48:])
        qkv = tuple(half for part in qkv for half in (part[:8], part[8:]))
        slots_in = split_slots(whole(w_in), 576)
        slots_out = split_slots(whole(w_out), 192)
        slots_down = split_slots(whole(w_down), 192)
        both = [jnp.concatenate([slots_in[i], slots_out[i]], axis=2) for i in range(4)]
        downs = [
            jnp.concatenate(
                [d[:, :48], d[:, 48:96], d[:, 96:], jnp.zeros_like(d[:, :48])], axis=2
            )
            for d in slots_down
        ]
        rest = (
            both[0][:, :80], both[1][:, :80],
            jnp.concatenate([both[2][:, 80:], downs[2]], axis=1),
            jnp.concatenate([both[3][:, 80:], downs[3]], axis=1),
        )
        rest = tuple(half for part in rest for half in (part[:8], part[8:]))
        ca, cb = trade(cotangent)
    xb = arrived[:count]
    segb = arrived[count, :count].astype(F32)
    seg_mine = jnp.concatenate([sega, segb])
    seg_all = jnp.concatenate([seg_mine, swap(seg_mine, STEPS["core"][0])])

    rows = tokens.shape[1]
    places = jnp.concatenate(
        [s_index * rows + jnp.arange(rows), partner * rows + jnp.arange(rows)]
    ).astype(F32)
    freqs = jnp.exp(-jnp.arange(32, dtype=F32) * (2.0 * math.log(160000.0) / HEAD))
    angles = places[:, None] * freqs[None, :]
    cosine, sine = jnp.cos(angles), jnp.sin(angles)
    zero = jnp.zeros_like(sine)
    cos = jnp.concatenate([cosine] * 4, axis=1)
    sin_a = jnp.concatenate([-sine, zero] * 2, axis=1)
    sin_b = jnp.concatenate([zero, sine] * 2, axis=1)

    act = shape((512, 768), BF)
    q, kv, norm, weight, gain_rows = call(
        project_kernel,
        [act, shape((512, 1536), BF), act, shape((768, 2304), BF), shape((8, 768), F32)],
        [
            pltpu.VMEM((768, 128), BF), pltpu.VMEM((4, 768, 640), BF),
            pltpu.SemaphoreType.DMA,
        ],
        me, xa, xb, cos, sin_a, sin_b, *qkv,
        flops=10_000_000_000, moved=20_000_000, name="project",
    )
    far_r, later_r = (), ()
    if here:
        q, kv, held_r, got_r = tie((q, kv, held_r, got_r))
        held_r = join(held_r, got_r)
        later_r = swap_each(held_r, ("y", "x"))
        far_r = other_core(held_r)
    kv_far = swap(kv, STEPS["core"][0])

    pair_spec = pl.BlockSpec((512, PAIR), lambda p: (0, p))
    value_spec = pl.BlockSpec((512, PAIR), lambda p: (0, p + HEADS // 2))

    def fixed(dims):
        return pl.BlockSpec(dims, lambda p: (0, 0))

    params = pltpu.CompilerParams(
        vmem_limit_bytes=VMEM_LIMIT, dimension_semantics=("arbitrary",)
    )
    att, lse = pl.pallas_call(
        attend_kernel,
        grid=(HEADS // 2,),
        out_shape=[act, shape((512, 768), F32)],
        in_specs=[pair_spec] * 3 + [value_spec] * 2 + [fixed((512, 1)), fixed((1, 1024))],
        out_specs=[pair_spec] * 2,
        scratch_shapes=[pltpu.VMEM((512, 1024), F32)],
        compiler_params=params,
        cost_estimate=pl.CostEstimate(
            flops=17_000_000_000, bytes_accessed=8_000_000, transcendentals=6_000_000
        ),
        name="attend",
    )(q, kv, kv_far, kv, kv_far, seg_mine[:, None], seg_all[None, :])

    if here:
        att, lse, far_r, later_r = tie((att, lse, far_r, later_r))
        rest = interleave(held_r, later_r, far_r, other_core(later_r))
    slot_b, slot_c = shape((16, 80, 768), BF), shape((16, 64, 768), BF)
    mix_pair, mix_b, dmid, datt, g2, fb0, fb1, fc0, fc1 = call(
        feed_kernel,
        [
            shape((2, 256, 768), BF), shape((256, 768), BF), shape((512, 768), F32), act,
            shape((8, 768), F32), slot_b, slot_b, slot_c, slot_c,
        ],
        [
            pltpu.VMEM((4, 768, 768), BF), pltpu.VMEM((8, 4, 48, 768), BF),
            pltpu.VMEM((1152, 768), BF), pltpu.VMEM((512, 768), BF),
            pltpu.VMEM((2, 512, 576), BF), pltpu.VMEM((4, 512, 768), BF),
            pltpu.VMEM((4, 512, 256), BF), pltpu.VMEM((4, 768, 768), BF),
            pltpu.VMEM((8, 4, 48, 768), BF), pltpu.VMEM((2, 768, 512), BF),
            pltpu.SemaphoreType.DMA((3,)), pltpu.VMEM((256, 768), BF),
        ],
        me, place, xa, xb, ca, cb, att, gain_rows, *rest,
        flops=35_000_000_000, moved=30_000_000, name="feed",
    )

    def attend_back(first, pairs, *args):
        pair_at = pl.BlockSpec((512, PAIR), lambda p: (0, p + first))
        value_at = pl.BlockSpec((512, PAIR), lambda p: (0, p + first + HEADS // 2))
        both_spec = pl.BlockSpec((512, 2 * PAIR), lambda p: (0, p))
        return pl.pallas_call(
            attend_back_kernel,
            grid=(pairs,),
            out_shape=[
                shape((512, pairs * PAIR), BF),
                shape((512, 2 * pairs * PAIR), F32),
                shape((512, 2 * pairs * PAIR), BF),
            ],
            in_specs=[pair_at] * 3 + [value_at] * 2 + [pair_at] * 3
            + [fixed((1024, 1)), fixed((1, 512))]
            + [fixed((512, PAIR))] * 3,
            out_specs=[pair_spec, both_spec, both_spec],
            scratch_shapes=[pltpu.VMEM((1024, 512), F32)],
            compiler_params=params,
            cost_estimate=pl.CostEstimate(
                flops=6_000_000_000 * pairs, bytes_accessed=4_000_000, transcendentals=2_000_000
            ),
            name="attend_back",
        )(*args)

    attend_args = (
        kv, kv_far, kv, kv_far, att, datt, lse, seg_all[:, None], seg_mine[None, :],
        cos, sin_a, sin_b,
    )
    back_a = attend_back(0, 2, q, *attend_args)
    own_r, far_r, one_r, two_r = (fb0, fc0), (), (), ()
    mix_far = swap(mix_b, STEPS["x"][0])
    if here:
        far_r = other_core((fb1, fc1))
        back_a, far_r, mix_far = tie((back_a, far_r, mix_far))
        sent = first_sent(own_r, far_r)
        sent, q = tie((sent, q))
        one_r = swap_each(sent, ("y", "x"))
    mixed = untrade(place, mix_pair, mix_far)
    far_a = swap(back_a[2], STEPS["core"][0])
    back_b = attend_back(2, 4, q, *attend_args)
    back_b, one_r, mixed = tie((back_b, one_r, mixed))
    far_b = swap(back_b[2], STEPS["core"][0])
    if here:
        sent = second_sent(own_r, far_r, one_r)
        sent, far_b = tie((sent, far_b))
        two_r = swap_each(sent, ("x", "y"))

    slot = shape((16, 48, 640), BF)
    dp, lb0, lb1, lc0, lc1 = call(
        weight_grad_kernel,
        [shape((512, 2304), BF), slot, slot, slot, slot],
        [
            pltpu.VMEM((4, 768, 640), BF), pltpu.VMEM((768, 512), BF),
            pltpu.SemaphoreType.DMA,
        ],
        me, norm, weight, gain_rows, g2,
        *(
            part
            for back, far in ((back_a, far_a), (back_b, far_b))
            for part in (back[0], back[1], far)
        ),
        cos, sin_a, sin_b,
        flops=14_000_000_000, moved=20_000_000, name="weight_grad",
    )
    dp, lb0, lb1, lc0, lc1, two_r = tie((dp, lb0, lb1, lc0, lc1, two_r))
    if here:
        own_q = (lb0, lc0)
        far_q = other_core((lb1, lc1))
        sums_r = third_sums(own_r, far_r, one_r, two_r)
        far_q, sums_r = tie((far_q, sums_r))
        sent, sums_r, dp = tie((first_sent(own_q, far_q), sums_r, dp))
        one_q = swap_each(sent, ("y", "x"))
        blocks_r = z_blocks(sums_r)
        got_r = swap_z(blocks_r)
    gt_pair, gt_b = call(
        token_grad_kernel,
        [shape((2, 256, 768), BF), shape((256, 768), BF)],
        [pltpu.VMEM((256, 768), BF), pltpu.SemaphoreType.DMA],
        place, xa, xb, weight, gain_rows, dp, dmid,
        flops=8_000_000_000, moved=10_000_000, name="token_grad",
    )
    if here:
        gt_pair, gt_b, one_q = tie((gt_pair, gt_b, one_q))
        sent, gt_b = tie((second_sent(own_q, far_q, one_q), gt_b))
        two_q = swap_each(sent, ("x", "y"))
    gt_far = swap(gt_b, STEPS["x"][0])
    grad_tokens = untrade(place, gt_pair, gt_far)

    if here:
        two_q, got_r = tie((two_q, got_r))
        blocks = z_blocks(third_sums(own_q, far_q, one_q, two_q))
        rest_sum = last_sum(blocks_r[0], got_r)
        grad_qkv = last_sum(blocks[0], swap_z(blocks))
        grad_in, grad_out = rest_sum[:96, :576], rest_sum[:96, 576:]
        grad_down = jnp.concatenate(
            [rest_sum[96:, 192 * j : 192 * j + 192] for j in range(3)], axis=0
        )
        grad_gains = grad_qkv[:, 576:578].T
        grad_qkv = grad_qkv[:, :576]
    else:
        full_b = join_slots(fb0, fb1, ORDER_B)
        full_c = join_slots(fc0, fc1, ORDER_C)
        full_q = jnp.concatenate(
            [join_slots(lb0, lb1, ORDER_B), join_slots(lc0, lc1, ORDER_C)], axis=2
        )
        full_i = jnp.concatenate([full_b, full_c[:, :, :16]], axis=2)
        full_d = jnp.concatenate(
            [full_c[:, :, 16:, 192 * j : 192 * j + 192] for j in range(3)], axis=2
        )

        def share(full):
            flat = full.transpose(0, 2, 1, 3).reshape(-1, GRID_S * full.shape[-1])
            part = lax.psum_scatter(
                flat.astype(F32), "fsdp", scatter_dimension=0, tiled=True
            )
            return lax.psum_scatter(part, "seq", scatter_dimension=1, tiled=True)

        grad_in, grad_out = share(full_i[..., :576]), share(full_i[..., 576:])
        grad_down = share(full_d)
        grad_qkv = share(full_q[..., :576])
        gain_sum = full_q[:, 0, :, 576:578].reshape(768, 2).astype(F32).T
        grad_gains = lax.psum(
            lax.psum_scatter(gain_sum, "fsdp", scatter_dimension=1, tiled=True), "seq"
        )
    return (mixed, grad_tokens, grad_qkv, grad_out, grad_in, grad_down, grad_gains)


def place_kernel(place, pair, back, out, sem):
    copy = pltpu.make_async_copy(back, out.at[1 - (place[1] >> 1)], sem)
    copy.start()
    copy.wait()


def untrade(place, pair, back):
    anywhere = pl.BlockSpec(memory_space=pl.ANY)
    return pl.pallas_call(
        place_kernel,
        out_shape=shape(pair.shape, pair.dtype),
        in_specs=[
            pl.BlockSpec(memory_space=pltpu.SMEM), anywhere,
            pl.BlockSpec(memory_space=pltpu.VMEM),
        ],
        out_specs=anywhere,
        scratch_shapes=[pltpu.SemaphoreType.DMA],
        input_output_aliases={1: 0},
        name="place",
    )(place, pair, back)


def solution(mesh):
    return jax.shard_map(
        per_device,
        mesh=mesh,
        in_specs=(
            P("fsdp", "seq", None),
            P("fsdp", "seq"),
            P("fsdp", "seq"),
            P("fsdp", "seq"),
            P("fsdp", "seq"),
            P("fsdp", "seq"),
            P(None, "fsdp"),
            P("fsdp", "seq", None),
        ),
        out_specs=(
            P("fsdp", "seq", None),
            P("fsdp", "seq", None),
            P("fsdp", "seq"),
            P("fsdp", "seq"),
            P("fsdp", "seq"),
            P("fsdp", "seq"),
            P(None, "fsdp"),
        ),
        check_vma=False,
    )
```

```python
import functools
import math

import jax
import jax.numpy as jnp
from jax import lax
from jax.experimental import pallas as pl
from jax.experimental.pallas import tpu as pltpu
from jax.sharding import PartitionSpec as P

HEADS = 12
HEAD = 64
PAIR = 2 * HEAD
EPS = 1e-05
FILL = -1000000000.0
BF = jnp.bfloat16
F32 = jnp.float32
VMEM_LIMIT = 60 * 1024 * 1024

STEPS = {
    "x": [("seq", 2)],
    "y": [("fsdp", 1)],
    "z": [("fsdp", 2), ("fsdp", 4), ("fsdp", 6)],
    "core": [("seq", 1)],
}
ORDER_B = ("z", "x", "y")
ORDER_C = ("z", "y", "x")
GRID_F = 8
GRID_S = 4


def swap(value, step):
    axis, flip = step
    size = lax.axis_size(axis)
    return lax.ppermute(value, axis, [(i, i ^ flip) for i in range(size)])


tie = lax.optimization_barrier


def send_z(block):
    return (block,) + tuple(swap(block, step) for step in STEPS["z"])


def cut_rows(blocks, cut):
    return jnp.stack([b[:cut] for b in blocks]), jnp.stack([b[cut:] for b in blocks])


def join(held, got):
    return tuple(jnp.concatenate(pair, axis=0) for pair in zip(held, got))


def interleave(*lists):
    return tuple(piece for part in zip(*lists) for piece in part)


def other_core(parts):
    return tuple(swap(part, STEPS["core"][0]) for part in parts)


def sum_kernel(arrays, joined, *refs):
    ins, outs = refs[: 2 * arrays], refs[2 * arrays :]
    top = 0
    for part in range(2):
        total = ins[arrays * part][...]
        for ref in ins[arrays * part + 1 : arrays * part + arrays]:
            total = (total.astype(F32) + ref[...].astype(F32)).astype(BF)
        rows = total.shape[1]
        if joined:
            for i, out in enumerate(outs):
                out[top : top + rows, :] = total[i]
        else:
            outs[part][...] = total
        top += rows


def sums(lists, start, count, steps, joined=False):
    parts = list(zip(*lists))
    size = count // steps
    ins, specs, outs = [], [], []
    for part in parts:
        rows, width = part[0].shape[1:]
        for array in part:
            ins.append(array)
            specs.append(
                pl.BlockSpec((size, rows, width), lambda i: (start // size + i, 0, 0))
            )
        outs.append(shape((count, rows, width), BF))
    out_specs = [pl.BlockSpec((size,) + o.shape[1:], lambda i: (i, 0, 0)) for o in outs]
    if joined:
        rows = sum(o.shape[1] for o in outs)
        outs = [shape((rows, width), BF)] * count
        out_specs = [pl.BlockSpec((rows, width), lambda i: (0, 0))] * count
    return pl.pallas_call(
        functools.partial(sum_kernel, len(lists), joined),
        grid=(steps,),
        out_shape=outs,
        in_specs=specs,
        out_specs=out_specs,
        compiler_params=pltpu.CompilerParams(dimension_semantics=("arbitrary",)),
        cost_estimate=pl.CostEstimate(
            flops=1_000_000, bytes_accessed=3_000_000, transcendentals=0
        ),
        name="sums",
    )(*ins)


def level(value):
    return lax.reduce_precision(value, 8, 7)


def level_sum(arrays, at):
    total = arrays[0][at].astype(F32)
    for array in arrays[1:]:
        total = level(total + array[at].astype(F32))
    return total.astype(BF)


def small_sums(lists, start, count):
    return tuple(level_sum(part, slice(start, start + count)) for part in zip(*lists))


def small_blocks(lists):
    parts = [level_sum(part, slice(0, 4)) for part in zip(*lists)]
    return [jnp.concatenate([part[i] for part in parts], axis=0) for i in range(4)]


def swap_each(parts, phases):
    return tuple(swap(part, STEPS[phase][0]) for part, phase in zip(parts, phases))


def swap_z(blocks):
    return tuple(swap(blocks[i + 1], step) for i, step in enumerate(STEPS["z"]))


def last_sum(mine, got):
    got = [g.astype(F32) for g in got]
    return (mine.astype(F32) + got[0]) + (got[1] + got[2])


def codes_of(order):
    codes = [(0, 0)]
    for phase in order:
        grown = list(codes)
        for axis, flip in STEPS[phase]:
            for f, s in codes:
                grown.append((f ^ flip, s) if axis == "fsdp" else (f, s ^ flip))
        codes = grown
    return codes


def dot(a, b):
    return jnp.dot(a, b, preferred_element_type=F32)


def dot_nt(a, b, precision=None):
    return lax.dot_general(
        a, b, (((1,), (1,)), ((), ())), preferred_element_type=F32, precision=precision
    )


def dot_tn(a, b, precision=None):
    return lax.dot_general(
        a, b, (((0,), (0,)), ((), ())), preferred_element_type=F32, precision=precision
    )


def norm_stats(x):
    center = x - jnp.mean(x, axis=-1, keepdims=True)
    spread = jnp.mean(center * center, axis=-1, keepdims=True)
    rate = lax.rsqrt(spread + EPS)
    return center * rate, rate


def norm_back(e, hat, rate):
    return rate * (
        e
        - jnp.mean(e, axis=-1, keepdims=True)
        - hat * jnp.mean(e * hat, axis=-1, keepdims=True)
    )


def turn(u, cosine, sine_a, sine_b):
    return u * cosine + pltpu.roll(u, PAIR - 32, 1) * sine_a + pltpu.roll(u, 32, 1) * sine_b


def turn_back(u, cosine, sine_a, sine_b):
    return u * cosine - pltpu.roll(u, PAIR - 32, 1) * sine_a - pltpu.roll(u, 32, 1) * sine_b


def owners(me, order, pieces):
    codes = codes_of(order)
    for i, piece in enumerate(pieces):
        far, later = divmod(i, 2)
        for k in range(8):
            f, s = codes[8 * later + k]
            yield piece, k, me[0] ^ f, me[1] ^ (s ^ far)


def results(me, order, near, far):
    for core, out in enumerate((near, far)):
        for k, (f, s) in enumerate(codes_of(order)):
            yield out, k, me[0] ^ f, me[1] ^ (s ^ core)


def rows_at(start, count):
    return pl.ds(pl.multiple_of(start, 16), count)


def await_all(ref, sem):
    pltpu.make_async_copy(ref, ref, sem).wait()


def project_kernel(me, xa, xb, seg, cos, sin_a, sin_b, *refs):
    pieces = refs[:8]
    q_o, kv_o, n_o, w_o, g_o, gcol, buf, sem = refs[8:]
    kv_o[:, 1536:] = jnp.broadcast_to(seg[...], (PAIR, 512)).T.astype(BF)
    for order, start, part in ((ORDER_B, 0, pieces[:4]), (ORDER_C, 48, pieces[4:])):
        for piece, k, f, s in owners(me, order, part):
            to = buf.at[s, rows_at(f * 96 + start, 48)]
            pltpu.make_async_copy(piece.at[k], to, sem).start()
    await_all(buf, sem)
    gcol[...] = buf[0, :, 512:640]
    for f in range(GRID_F):
        rows = slice(96 * f, 96 * f + 96)
        w_o[rows, :] = jnp.concatenate([buf[s, rows, :576] for s in range(GRID_S)], axis=1)
    row_i = lax.broadcasted_iota(jnp.int32, (8, 128), 0)
    lane_i = lax.broadcasted_iota(jnp.int32, (8, 128), 1)
    hot = jnp.where(lane_i == row_i + 64, 1.0, 0.0).astype(BF)
    gains = dot_nt(hot, gcol[...])
    g_o[...] = gains
    for half, xr in enumerate((xa, xb)):
        hat, _ = norm_stats(xr[...].astype(F32))
        n_o[256 * half : 256 * half + 256, :] = (hat * gains[0:1, :]).astype(BF)
    for j in range(9):
        y = dot(n_o[...], w_o[:, 256 * j : 256 * j + 256])
        if j < 6:
            y = jnp.concatenate(
                [
                    turn(y[:, 128 * i : 128 * i + 128], cos[...], sin_a[...], sin_b[...])
                    for i in range(2)
                ],
                axis=1,
            )
        if j < 3:
            q_o[:, 256 * j : 256 * j + 256] = (y.astype(BF) * 0.125).astype(BF)
        else:
            kv_o[:, 256 * (j - 3) : 256 * (j - 3) + 256] = y.astype(BF)


def head_masks():
    lane = lax.broadcasted_iota(jnp.int32, (1, PAIR), 1)
    first = jnp.where(lane < HEAD, 1.0, 0.0)
    return lane < HEAD, (first.astype(BF), (1.0 - first).astype(BF))


def attend_kernel(q, ka, kb, va, vb, seg_a, seg_b, out, lse, bias):
    @pl.when(pl.program_id(0) == 0)
    def _():
        own, far = seg_a[...].astype(F32), seg_b[...].astype(F32)
        for side, keys in enumerate((own, far)):
            same = own[:, :1] == keys.T[:1, :]
            bias[:, 512 * side : 512 * side + 512] = jnp.where(same, 0.0, FILL)

    lane, masks = head_masks()
    column = lax.broadcasted_iota(jnp.int32, (512, PAIR), 1)
    ones = jnp.where(column == 0, 1.0, 0.0).astype(BF)
    near, far = (jnp.concatenate([v[...], ones], axis=1) for v in (va, vb))
    for t in range(4):
        rows = slice(128 * t, 128 * t + 128)
        outs, logs = [], []
        for mask in masks:
            qm = q[rows, :] * mask
            sa = dot_nt(qm, ka[...]) + bias[rows, :512]
            sb = dot_nt(qm, kb[...]) + bias[rows, 512:]
            peak = jnp.max(jnp.maximum(sa, sb), axis=-1, keepdims=True)
            ea = jnp.exp(sa - peak).astype(BF)
            eb = jnp.exp(sb - peak).astype(BF)
            o = dot(ea, near) + dot(eb, far)
            total = o[:, PAIR : PAIR + 1]
            outs.append(o[:, :PAIR] * (1.0 / total))
            logs.append(peak + jnp.log(total))
        out[rows, :] = jnp.where(lane, outs[0], outs[1]).astype(BF)
        lse[rows, :] = jnp.where(lane, logs[0], logs[1])


def attend_back_kernel(
    q, ka, kb, va, vb, att, datt, lse, seg_a, seg_b, cos, sin_a, sin_b,
    dq_o, near_o, far_o, bias,
):
    @pl.when(pl.program_id(0) == 0)
    def _():
        own, far = seg_a[...].astype(F32), seg_b[...].astype(F32)
        for side, keys in enumerate((own, far)):
            same = keys[:, :1] == own.T[:1, :]
            bias[512 * side : 512 * side + 512, :] = jnp.where(same, 0.0, FILL)

    lane, masks = head_masks()
    row_i = lax.broadcasted_iota(jnp.int32, (8, PAIR), 0)
    lane_i = lax.broadcasted_iota(jnp.int32, (8, PAIR), 1)
    hot = jnp.where(lane_i == row_i * HEAD, 1.0, 0.0)
    spread = jnp.where((lane_i // HEAD) == row_i, 1.0, 0.0)
    high = lax.Precision.HIGHEST
    log_rows = dot_nt(hot, lse[...], high)
    delta_rows = dot_nt(spread, datt[...].astype(F32) * att[...].astype(F32), high)
    dq_parts = [[None, None], [None, None]]
    dk_parts = [None, None]
    dv_parts = [None, None]
    for side, (k, v) in enumerate(((ka, va), (kb, vb))):
        keys = slice(512 * side, 512 * side + 512)
        for t in range(2):
            rows = slice(256 * t, 256 * t + 256)
            for h, mask in enumerate(masks):
                qm = q[rows, :] * mask
                dm = datt[rows, :] * mask
                s = dot_nt(k[...], qm) + bias[keys, rows]
                p = jnp.exp(s - log_rows[h : h + 1, rows])
                dp = dot_nt(v[...], dm)
                ds = (p * (dp - delta_rows[h : h + 1, rows])).astype(BF)
                dv = dot(p.astype(BF), dm)
                dk = dot(ds, qm)
                dq = dot_tn(ds, k[...])
                dv_parts[side] = dv if dv_parts[side] is None else dv_parts[side] + dv
                dk_parts[side] = dk if dk_parts[side] is None else dk_parts[side] + dk
                old = dq_parts[t][h]
                dq_parts[t][h] = dq if old is None else old + dq
    near_o[:, :PAIR] = dk_parts[0]
    near_o[:, PAIR:] = dv_parts[0]
    far_o[:, :PAIR] = dk_parts[1].astype(BF)
    far_o[:, PAIR:] = dv_parts[1].astype(BF)
    for t in range(2):
        rows = slice(256 * t, 256 * t + 256)
        dq = jnp.where(lane, dq_parts[t][0], dq_parts[t][1]) * 0.125
        dq_o[rows, :] = turn_back(dq, cos[rows, :], sin_a[rows, :], sin_b[rows, :]).astype(BF)


def feed_kernel(me, place, xa, xb, ca, cb, att, gains, *refs):
    pieces = refs[:8]
    mix_pair, mix_b, dmid_o, datt_o, g2_o, near_b, far_b, near_c, far_c = refs[8:17]
    wide, wide_dn, wdn, n2, hid, di, db, grads, grads_dn, flip, sem, mix_a, cot = refs[17:]
    for piece, k, f, s in owners(me, ORDER_B, pieces[:4]):
        to = wide.at[s, rows_at(f * 96, 80)]
        pltpu.make_async_copy(piece.at[k], to, sem.at[0]).start()
    for piece, k, f, s in owners(me, ORDER_C, pieces[4:]):
        to = wide.at[s, rows_at(f * 96 + 80, 16)]
        pltpu.make_async_copy(piece.at[k, pl.ds(0, 16)], to, sem.at[0]).start()
        to = wide_dn.at[f, s]
        pltpu.make_async_copy(piece.at[k, pl.ds(16, 48)], to, sem.at[1]).start()
    di[:, :, 512:] = jnp.zeros((4, 512, 256), BF)
    await_all(wide, sem.at[0])
    await_all(wide_dn, sem.at[1])
    for f in range(GRID_F):
        for j in range(3):
            wdn[144 * f + 48 * j : 144 * f + 48 * j + 48, :] = jnp.concatenate(
                [wide_dn[f, s, :, 192 * j : 192 * j + 192] for s in range(GRID_S)], axis=1
            )
    gain = gains[1:2, :]
    gain_grad = jnp.zeros((1, 768), F32)
    tokens = jnp.concatenate([xa[...], xb[...]], axis=0)
    cot[:256, :] = ca[...]
    cot[256:, :] = cb[:256, :]
    mid = tokens.astype(F32) + jnp.concatenate(
        [dot(att[...], wide[s, :, 512:])[:, 64:] for s in range(GRID_S)], axis=1
    )
    hat, rate = norm_stats(mid)
    n2[...] = (hat * gain).astype(BF)
    branch = None
    for h in range(2):
        down = wdn[576 * h : 576 * h + 576, :]
        a = dot(n2[...], wide[h, :, :576])
        gate = dot(n2[...], wide[2 + h, :, :576])
        cdf = 0.5 * (1.0 + lax.erf(a * math.sqrt(0.5)))
        gelu = a * cdf
        hidden = (gelu * gate).astype(BF)
        hid[h] = hidden
        slope = cdf + a * (jnp.exp(-0.5 * a * a) * (1.0 / math.sqrt(2.0 * math.pi)))
        dh = dot_nt(cot[...], down)
        di[h, :, :576] = (dh * gate * slope).astype(BF)
        di[2 + h, :, :576] = (dh * gelu).astype(BF)
        part = dot(hidden, down)
        branch = part if branch is None else branch + part
    mixed = (mid + branch).astype(BF)
    mix_a[...] = mixed[:256]
    mix_b[...] = mixed[256:]
    dn = None
    for s in range(4):
        part = dot_nt(di[s, :, :576], wide[s, :, :576])
        dn = part if dn is None else dn + part
    gain_grad = gain_grad + jnp.sum(dn * hat, axis=0, keepdims=True)
    dmid = cot[...].astype(F32) + norm_back(dn * gain, hat, rate)
    dmid_o[...] = dmid
    branch_grad = dmid.astype(BF)
    datt = None
    for s in range(4):
        db[s] = jnp.concatenate(
            [jnp.zeros((512, 64), BF), branch_grad[:, 192 * s : 192 * s + 192]], axis=1
        )
        part = dot_nt(db[s], wide[s, :, 512:])
        datt = part if datt is None else datt + part
    datt_o[...] = datt.astype(BF)
    g2_o[...] = jnp.broadcast_to(gain_grad, (8, 768))

    own = pltpu.make_async_copy(mix_a, mix_pair.at[place[1] >> 1], sem.at[2])
    own.start()
    flip[0] = n2[...].T
    flip[1] = att[...].T
    for s in range(4):
        grad = dot(flip[0], di[s])
        grads[s, :, :512] = grad[:, :512].astype(BF)
        grads[s, :, 512:] = (grad[:, 512:] + dot(flip[1], db[s])).astype(BF)
    for out, k, f, s in results(me, ORDER_B, near_b, far_b):
        start = grads.at[s, rows_at(f * 96, 80)]
        pltpu.make_async_copy(start, out.at[k], sem.at[0]).start()
    for out, k, f, s in results(me, ORDER_C, near_c, far_c):
        start = grads.at[s, rows_at(f * 96 + 80, 16)]
        pltpu.make_async_copy(start, out.at[k, pl.ds(0, 16)], sem.at[0]).start()
    for h in range(2):
        grad_down = dot_tn(hid[h], cot[...]).astype(BF)
        for f in range(4):
            for s in range(4):
                grads_dn[4 * h + f, s] = jnp.concatenate(
                    [
                        grad_down[144 * f + 48 * j : 144 * f + 48 * j + 48, 192 * s : 192 * s + 192]
                        for j in range(3)
                    ]
                    + [jnp.zeros((48, 192), BF)],
                    axis=1,
                )
    for out, k, f, s in results(me, ORDER_C, near_c, far_c):
        to = out.at[k, pl.ds(16, 48)]
        pltpu.make_async_copy(grads_dn.at[f, s], to, sem.at[1]).start()
    await_all(grads, sem.at[0])
    await_all(grads_dn, sem.at[1])
    own.wait()


def weight_grad_kernel(
    me, norm, weight, gains, g2, *refs
):
    heads = refs[:6]
    cos, sin_a, sin_b, dp, near_b, far_b, near_c, far_c, grads, flip, sem = refs[6:]
    for p, (at, pairs) in enumerate(((0, 2), (2 * PAIR, 4))):
        dq, near, far = heads[3 * p : 3 * p + 3]
        dp[:, at : at + pairs * PAIR] = dq[...]
        for i in range(pairs):
            cols = slice(2 * PAIR * i, 2 * PAIR * i + 2 * PAIR)
            total = near[:, cols] + far[:, cols].astype(F32)
            start = 768 + at + PAIR * i
            dp[:, start : start + PAIR] = turn_back(
                total[:, :PAIR], cos[...], sin_a[...], sin_b[...]
            ).astype(BF)
            dp[:, 768 + start : 768 + start + PAIR] = total[:, PAIR:].astype(BF)
    row_i = lax.broadcasted_iota(jnp.int32, (8, 128), 0)
    lane_i = lax.broadcasted_iota(jnp.int32, (8, 128), 1)
    hot = jnp.where((lane_i == row_i + 64) & (row_i < 2), 1.0, 0.0)
    total = jnp.zeros((768, 1), F32)
    flip[...] = norm[...].T
    for s in range(4):
        cols = slice(576 * s, 576 * s + 576)
        grad = dot(flip[...], dp[:, cols])
        total = total + jnp.sum(grad * weight[:, cols].astype(F32), axis=1, keepdims=True)
        grads[s] = jnp.concatenate([grad, jnp.zeros((768, 64), F32)], axis=1).astype(BF)
    row_w = lax.broadcasted_iota(jnp.int32, (8, 768), 0)
    rows = jnp.where(row_w == 0, 1.0 / gains[0:1, :], g2[...])
    columns = dot_tn(rows, hot, lax.Precision.HIGHEST)
    lane = lax.broadcasted_iota(jnp.int32, (1, 128), 1)
    columns = jnp.where(lane == 64, columns * total, columns).astype(BF)
    for s in range(4):
        grads[s, :, 512:] = grads[s, :, 512:] + columns
    for order, start, near, far in ((ORDER_B, 0, near_b, far_b), (ORDER_C, 48, near_c, far_c)):
        for out, k, f, s in results(me, order, near, far):
            held = grads.at[s, rows_at(f * 96 + start, 48)]
            pltpu.make_async_copy(held, out.at[k], sem).start()
    await_all(grads, sem)


def token_grad_kernel(place, xa, xb, weight, gains, dp, dmid, gt_pair, gt_b, gt_a, sem):
    gain = gains[0:1, :]
    for t, (xr, gt) in enumerate(((xa, gt_a), (xb, gt_b))):
        rows = slice(256 * t, 256 * t + 256)
        dn = dot_nt(dp[rows, :], weight[...])
        hat, rate = norm_stats(xr[...].astype(F32))
        gt[...] = (dmid[rows, :] + norm_back(dn * gain, hat, rate)).astype(BF)
    own = pltpu.make_async_copy(gt_a, gt_pair.at[place[1] >> 1], sem)
    own.start()
    own.wait()


def call(kernel, outs, scratch, *args, flops=0, moved=0, name=None):
    def spec(a):
        space = pltpu.SMEM if a.dtype == jnp.int32 else pltpu.VMEM
        return pl.BlockSpec(memory_space=pl.ANY if len(a.shape) == 3 else space)

    specs = [spec(a) for a in args]
    return pl.pallas_call(
        kernel,
        out_shape=outs,
        in_specs=specs,
        out_specs=[spec(a) for a in outs],
        scratch_shapes=scratch,
        compiler_params=pltpu.CompilerParams(vmem_limit_bytes=VMEM_LIMIT),
        cost_estimate=pl.CostEstimate(flops=flops, bytes_accessed=moved, transcendentals=0),
        name=name,
    )(*args)


def shape(dims, dtype):
    return jax.ShapeDtypeStruct(dims, dtype)


def split_slots(full, width):
    rows = full.shape[0] // GRID_F
    blocks = full.reshape(GRID_F, rows, GRID_S, width).transpose(0, 2, 1, 3)
    found = []
    for order in (ORDER_B, ORDER_C):
        for core in range(2):
            found.append(jnp.stack([blocks[f, s ^ core] for f, s in codes_of(order)]))
    return found


def join_slots(own, other, order):
    table = {}
    for k, (f, s) in enumerate(codes_of(order)):
        table[f, s] = own[k]
        table[f, s ^ 1] = other[k]
    return jnp.stack([jnp.stack([table[f, s] for s in range(GRID_S)]) for f in range(GRID_F)])


def per_device(tokens, segments, w_qkv, w_out, w_in, w_down, gains, cotangent):
    here = lax.axis_size("fsdp") == GRID_F and lax.axis_size("seq") == GRID_S
    s_index = lax.axis_index("seq")
    x_index = s_index // 2
    partner = s_index ^ 2

    count = tokens.shape[1]
    place = jnp.stack([lax.axis_index("fsdp"), s_index]).astype(jnp.int32)

    def pick(pair, i):
        return lax.dynamic_index_in_dim(pair, i, 0, keepdims=False)

    xa, ca = pick(tokens, x_index), pick(cotangent, x_index)
    sega = pick(segments, x_index).astype(F32)
    marks = pick(segments, 1 - x_index).astype(BF)[None]
    marks = jnp.pad(marks, ((0, 15), (0, tokens.shape[2] - count)))
    theirs = jnp.concatenate([pick(cotangent, 1 - x_index), marks], axis=0)
    xb = swap(pick(tokens, 1 - x_index), STEPS["x"][0])

    rows = tokens.shape[1]
    places = jnp.concatenate(
        [s_index * rows + jnp.arange(rows), partner * rows + jnp.arange(rows)]
    ).astype(F32)
    freqs = jnp.exp(-jnp.arange(32, dtype=F32) * (2.0 * math.log(160000.0) / HEAD))
    angles = places[:, None] * freqs[None, :]
    cosine, sine = jnp.cos(angles), jnp.sin(angles)
    zero = jnp.zeros_like(sine)
    cos = jnp.concatenate([cosine] * 4, axis=1)
    sin_a = jnp.concatenate([-sine, zero] * 2, axis=1)
    sin_b = jnp.concatenate([zero, sine] * 2, axis=1)
    if here:
        me = place
        wide = jnp.concatenate(
            [w_qkv, gains.T, jnp.zeros((w_qkv.shape[0], 62), BF)], axis=1
        )
        third = w_down.shape[0] // 3
        part_a = jnp.concatenate([w_in, w_out], axis=1)
        part_d = jnp.concatenate(
            [w_down[third * j : third * (j + 1)] for j in range(3)]
            + [jnp.zeros((third, w_down.shape[1]), BF)],
            axis=1,
        )
        rest = jnp.concatenate([part_a, part_d], axis=0)
        held_q = send_z(wide)
        held_q, xb, rest, theirs, xa, ca, sega, place, cos, sin_a, sin_b = tie(
            (held_q, xb, rest, theirs, xa, ca, sega, place, cos, sin_a, sin_b)
        )
        me = place
        cb = swap(theirs, STEPS["x"][0])
        near_z, far_z = (swap(rest, step) for step in STEPS["z"][:2])
        held_q = cut_rows(held_q, 48)
        got = swap_each(held_q, ("x", "y"))
        held_q, got, near_z, far_z, rest, cb = tie((held_q, got, near_z, far_z, rest, cb))
        held_q = join(held_q, got)
        later_q = swap_each(held_q, ("y", "x"))
        far_q = other_core(held_q)
        last_z = swap(rest, STEPS["z"][2])
        later_q, far_q, last_z = tie((later_q, far_q, last_z))
        held_r = cut_rows((rest, near_z, far_z, last_z), 80)
        far_later_q = other_core(later_q)
        got_r = swap_each(held_r, ("x", "y"))
        qkv = interleave(held_q, later_q, far_q, far_later_q)
    else:
        me = jnp.zeros((2,), jnp.int32)

        def whole(w):
            return lax.all_gather(
                lax.all_gather(w, "fsdp", axis=0, tiled=True), "seq", axis=1, tiled=True
            )

        gains_all = lax.all_gather(gains, "fsdp", axis=1, tiled=True).T
        wide = jnp.concatenate(
            [
                jnp.concatenate([block, gains_all, jnp.zeros((768, 62), BF)], axis=1)
                for block in jnp.split(whole(w_qkv), GRID_S, axis=1)
            ],
            axis=1,
        )
        slots = split_slots(wide, 640)
        qkv = (slots[0][:, :48], slots[1][:, :48], slots[2][:, 48:], slots[3][:, 48:])
        qkv = tuple(half for part in qkv for half in (part[:8], part[8:]))
        slots_in = split_slots(whole(w_in), 576)
        slots_out = split_slots(whole(w_out), 192)
        slots_down = split_slots(whole(w_down), 192)
        both = [jnp.concatenate([slots_in[i], slots_out[i]], axis=2) for i in range(4)]
        downs = [
            jnp.concatenate(
                [d[:, :48], d[:, 48:96], d[:, 96:], jnp.zeros_like(d[:, :48])], axis=2
            )
            for d in slots_down
        ]
        rest = (
            both[0][:, :80], both[1][:, :80],
            jnp.concatenate([both[2][:, 80:], downs[2]], axis=1),
            jnp.concatenate([both[3][:, 80:], downs[3]], axis=1),
        )
        rest = tuple(half for part in rest for half in (part[:8], part[8:]))
        cb = swap(theirs, STEPS["x"][0])
    seg_mine = jnp.concatenate([sega, cb[count, :count].astype(F32)])[None]

    act = shape((512, 768), BF)
    q, kv, norm, weight, gain_rows = call(
        project_kernel,
        [act, shape((512, 1536 + PAIR), BF), act, shape((768, 2304), BF), shape((8, 768), F32)],
        [
            pltpu.VMEM((768, 128), BF), pltpu.VMEM((4, 768, 640), BF),
            pltpu.SemaphoreType.DMA,
        ],
        me, xa, xb, seg_mine, cos, sin_a, sin_b, *qkv,
        flops=10_000_000_000, moved=20_000_000, name="project",
    )
    far_r, later_r = (), ()
    if here:
        q, kv, held_r, got_r = tie((q, kv, held_r, got_r))
        held_r = join(held_r, got_r)
        later_r = swap_each(held_r, ("y", "x"))
        far_r = other_core(held_r)
    kv_far = swap(kv, STEPS["core"][0])

    pair_spec = pl.BlockSpec((512, PAIR), lambda p: (0, p))
    value_spec = pl.BlockSpec((512, PAIR), lambda p: (0, p + HEADS // 2))
    mark_spec = pl.BlockSpec((512, PAIR), lambda p: (0, HEADS))

    def fixed(dims):
        return pl.BlockSpec(dims, lambda p: (0, 0))

    params = pltpu.CompilerParams(
        vmem_limit_bytes=VMEM_LIMIT, dimension_semantics=("arbitrary",)
    )
    att, lse = pl.pallas_call(
        attend_kernel,
        grid=(HEADS // 2,),
        out_shape=[act, shape((512, 768), F32)],
        in_specs=[pair_spec] * 3 + [value_spec] * 2 + [mark_spec] * 2,
        out_specs=[pair_spec] * 2,
        scratch_shapes=[pltpu.VMEM((512, 1024), F32)],
        compiler_params=params,
        cost_estimate=pl.CostEstimate(
            flops=17_000_000_000, bytes_accessed=8_000_000, transcendentals=6_000_000
        ),
        name="attend",
    )(q, kv, kv_far, kv, kv_far, kv, kv_far)

    if here:
        att, lse, far_r, later_r = tie((att, lse, far_r, later_r))
        rest = interleave(held_r, later_r, far_r, other_core(later_r))
    slot_b, slot_c = shape((16, 80, 768), BF), shape((16, 64, 768), BF)
    mix_pair, mix_b, dmid, datt, g2, fb0, fb1, fc0, fc1 = call(
        feed_kernel,
        [
            shape((2, 256, 768), BF), shape((256, 768), BF), shape((512, 768), F32), act,
            shape((8, 768), F32), slot_b, slot_b, slot_c, slot_c,
        ],
        [
            pltpu.VMEM((4, 768, 768), BF), pltpu.VMEM((8, 4, 48, 768), BF),
            pltpu.VMEM((1152, 768), BF), pltpu.VMEM((512, 768), BF),
            pltpu.VMEM((2, 512, 576), BF), pltpu.VMEM((4, 512, 768), BF),
            pltpu.VMEM((4, 512, 256), BF), pltpu.VMEM((4, 768, 768), BF),
            pltpu.VMEM((8, 4, 48, 768), BF), pltpu.VMEM((2, 768, 512), BF),
            pltpu.SemaphoreType.DMA((3,)), pltpu.VMEM((256, 768), BF),
            pltpu.VMEM((512, 768), BF),
        ],
        me, place, xa, xb, ca, cb, att, gain_rows, *rest,
        flops=35_000_000_000, moved=30_000_000, name="feed",
    )

    def attend_back(first, pairs, *args):
        pair_at = pl.BlockSpec((512, PAIR), lambda p: (0, p + first))
        value_at = pl.BlockSpec((512, PAIR), lambda p: (0, p + first + HEADS // 2))
        both_spec = pl.BlockSpec((512, 2 * PAIR), lambda p: (0, p))
        return pl.pallas_call(
            attend_back_kernel,
            grid=(pairs,),
            out_shape=[
                shape((512, pairs * PAIR), BF),
                shape((512, 2 * pairs * PAIR), F32),
                shape((512, 2 * pairs * PAIR), BF),
            ],
            in_specs=[pair_at] * 3 + [value_at] * 2 + [pair_at] * 3
            + [mark_spec] * 2
            + [fixed((512, PAIR))] * 3,
            out_specs=[pair_spec, both_spec, both_spec],
            scratch_shapes=[pltpu.VMEM((1024, 512), F32)],
            compiler_params=params,
            cost_estimate=pl.CostEstimate(
                flops=6_000_000_000 * pairs, bytes_accessed=4_000_000, transcendentals=2_000_000
            ),
            name="attend_back",
        )(*args)

    attend_args = (
        kv, kv_far, kv, kv_far, att, datt, lse, kv, kv_far,
        cos, sin_a, sin_b,
    )
    back_a = attend_back(0, 2, q, *attend_args)
    own_r, far_r, one_r, two_r = (fb0, fc0), (), (), ()
    mix_far = swap(mix_b, STEPS["x"][0])
    if here:
        far_r = other_core((fb1, fc1))
        back_a, far_r, mix_far = tie((back_a, far_r, mix_far))
        sent = tuple(sums((own_r, far_r), 8, 8, 4))
        sent, q = tie((sent, q))
        one_r = swap_each(sent, ("y", "x"))
    mixed = untrade(place, mix_pair, mix_far)
    far_a = swap(back_a[2], STEPS["core"][0])
    back_b = attend_back(2, 4, q, *attend_args)
    back_b, one_r, mixed = tie((back_b, one_r, mixed))
    far_b = swap(back_b[2], STEPS["core"][0])
    if here:
        sent = tuple(sums((own_r, far_r, one_r), 4, 4, 2))
        sent, far_b = tie((sent, far_b))
        two_r = swap_each(sent, ("x", "y"))

    slot = shape((16, 48, 640), BF)
    dp, lb0, lb1, lc0, lc1 = call(
        weight_grad_kernel,
        [shape((512, 2304), BF), slot, slot, slot, slot],
        [
            pltpu.VMEM((4, 768, 640), BF), pltpu.VMEM((768, 512), BF),
            pltpu.SemaphoreType.DMA,
        ],
        me, norm, weight, gain_rows, g2,
        *(
            part
            for back, far in ((back_a, far_a), (back_b, far_b))
            for part in (back[0], back[1], far)
        ),
        cos, sin_a, sin_b,
        flops=14_000_000_000, moved=20_000_000, name="weight_grad",
    )
    dp, lb0, lb1, lc0, lc1, two_r = tie((dp, lb0, lb1, lc0, lc1, two_r))
    if here:
        own_q = (lb0, lc0)
        far_q = other_core((lb1, lc1))
        blocks_r = tuple(sums((own_r, far_r, one_r, two_r), 0, 4, 1, joined=True))
        far_q, blocks_r = tie((far_q, blocks_r))
        sent, blocks_r, dp = tie((small_sums((own_q, far_q), 8, 8), blocks_r, dp))
        one_q = swap_each(sent, ("y", "x"))
    gt_pair, gt_b = call(
        token_grad_kernel,
        [shape((2, 256, 768), BF), shape((256, 768), BF)],
        [pltpu.VMEM((256, 768), BF), pltpu.SemaphoreType.DMA],
        place, xa, xb, weight, gain_rows, dp, dmid,
        flops=8_000_000_000, moved=10_000_000, name="token_grad",
    )
    if here:
        half = blocks_r[2].shape[0] // 2
        last_z = swap(blocks_r[3], STEPS["z"][2])
        far_z = swap(blocks_r[2][:half], STEPS["z"][1])
        gt_pair, gt_b, one_q, last_z, far_z, blocks_r = tie(
            (gt_pair, gt_b, one_q, last_z, far_z, blocks_r)
        )
        near_z = swap(blocks_r[1], STEPS["z"][0])
        far_z = (far_z, swap(blocks_r[2][half:], STEPS["z"][1]))
        sent, gt_b = tie((small_sums((own_q, far_q, one_q), 4, 4), gt_b))
        two_q = swap_each(sent, ("x", "y"))
    gt_far = swap(gt_b, STEPS["x"][0])
    grad_tokens = untrade(place, gt_pair, gt_far)

    if here:
        two_q, gt_pair, near_z, far_z = tie((two_q, gt_pair, near_z, far_z))
        got_r = (near_z, jnp.concatenate(far_z, axis=0), last_z)
        blocks = small_blocks((own_q, far_q, one_q, two_q))
        rest_sum = last_sum(blocks_r[0], got_r)
        got_q, grad_tokens = tie((swap_z(blocks), grad_tokens))
        grad_qkv = last_sum(blocks[0], got_q)
        grad_in, grad_out = rest_sum[:96, :576], rest_sum[:96, 576:]
        grad_down = jnp.concatenate(
            [rest_sum[96:, 192 * j : 192 * j + 192] for j in range(3)], axis=0
        )
        grad_gains = grad_qkv[:, 576:578].T
        grad_qkv = grad_qkv[:, :576]
    else:
        full_b = join_slots(fb0, fb1, ORDER_B)
        full_c = join_slots(fc0, fc1, ORDER_C)
        full_q = jnp.concatenate(
            [join_slots(lb0, lb1, ORDER_B), join_slots(lc0, lc1, ORDER_C)], axis=2
        )
        full_i = jnp.concatenate([full_b, full_c[:, :, :16]], axis=2)
        full_d = jnp.concatenate(
            [full_c[:, :, 16:, 192 * j : 192 * j + 192] for j in range(3)], axis=2
        )

        def share(full):
            flat = full.transpose(0, 2, 1, 3).reshape(-1, GRID_S * full.shape[-1])
            part = lax.psum_scatter(
                flat.astype(F32), "fsdp", scatter_dimension=0, tiled=True
            )
            return lax.psum_scatter(part, "seq", scatter_dimension=1, tiled=True)

        grad_in, grad_out = share(full_i[..., :576]), share(full_i[..., 576:])
        grad_down = share(full_d)
        grad_qkv = share(full_q[..., :576])
        gain_sum = full_q[:, 0, :, 576:578].reshape(768, 2).astype(F32).T
        grad_gains = lax.psum(
            lax.psum_scatter(gain_sum, "fsdp", scatter_dimension=1, tiled=True), "seq"
        )
    return (mixed, grad_tokens, grad_qkv, grad_out, grad_in, grad_down, grad_gains)


def place_kernel(place, pair, back, out, sem):
    copy = pltpu.make_async_copy(back, out.at[1 - (place[1] >> 1)], sem)
    copy.start()
    copy.wait()


def untrade(place, pair, back):
    anywhere = pl.BlockSpec(memory_space=pl.ANY)
    return pl.pallas_call(
        place_kernel,
        out_shape=shape(pair.shape, pair.dtype),
        in_specs=[
            pl.BlockSpec(memory_space=pltpu.SMEM), anywhere,
            pl.BlockSpec(memory_space=pltpu.VMEM),
        ],
        out_specs=anywhere,
        scratch_shapes=[pltpu.SemaphoreType.DMA],
        input_output_aliases={1: 0},
        name="place",
    )(place, pair, back)


def solution(mesh):
    return jax.shard_map(
        per_device,
        mesh=mesh,
        in_specs=(
            P("fsdp", "seq", None),
            P("fsdp", "seq"),
            P("fsdp", "seq"),
            P("fsdp", "seq"),
            P("fsdp", "seq"),
            P("fsdp", "seq"),
            P(None, "fsdp"),
            P("fsdp", "seq", None),
        ),
        out_specs=(
            P("fsdp", "seq", None),
            P("fsdp", "seq", None),
            P("fsdp", "seq"),
            P("fsdp", "seq"),
            P("fsdp", "seq"),
            P("fsdp", "seq"),
            P(None, "fsdp"),
        ),
        check_vma=False,
    )
```

```python
import functools
import math

import jax
import jax.numpy as jnp
from jax import lax
from jax.experimental import pallas as pl
from jax.experimental.pallas import tpu as pltpu
from jax.sharding import PartitionSpec as P

HEADS = 12
HEAD = 64
PAIR = 2 * HEAD
EPS = 1e-05
FILL = -1000000000.0
BF = jnp.bfloat16
F32 = jnp.float32
VMEM_LIMIT = 60 * 1024 * 1024

STEPS = {
    "x": [("seq", 2)],
    "y": [("fsdp", 1)],
    "z": [("fsdp", 2), ("fsdp", 4), ("fsdp", 6)],
    "core": [("seq", 1)],
}
ORDER_B = ("z", "x", "y")
ORDER_C = ("z", "y", "x")
GRID_F = 8
GRID_S = 4


def swap(value, step):
    axis, flip = step
    size = lax.axis_size(axis)
    return lax.ppermute(value, axis, [(i, i ^ flip) for i in range(size)])


tie = lax.optimization_barrier


def send_z(block):
    return (block,) + tuple(swap(block, step) for step in STEPS["z"])


def cut_rows(blocks, cut):
    return jnp.stack([b[:cut] for b in blocks]), jnp.stack([b[cut:] for b in blocks])


def join(held, got):
    return tuple(jnp.concatenate(pair, axis=0) for pair in zip(held, got))


def interleave(*lists):
    return tuple(piece for part in zip(*lists) for piece in part)


def other_core(parts):
    return tuple(swap(part, STEPS["core"][0]) for part in parts)


def sum_kernel(arrays, joined, *refs):
    ins, outs = refs[: 2 * arrays], refs[2 * arrays :]
    top = 0
    for part in range(2):
        total = ins[arrays * part][...]
        for ref in ins[arrays * part + 1 : arrays * part + arrays]:
            total = (total.astype(F32) + ref[...].astype(F32)).astype(BF)
        rows = total.shape[1]
        if joined:
            for i, out in enumerate(outs):
                out[top : top + rows, :] = total[i]
        else:
            outs[part][...] = total
        top += rows


def sums(lists, start, count, steps, joined=False):
    parts = list(zip(*lists))
    size = count // steps
    ins, specs, outs = [], [], []
    for part in parts:
        rows, width = part[0].shape[1:]
        for array in part:
            ins.append(array)
            specs.append(
                pl.BlockSpec((size, rows, width), lambda i: (start // size + i, 0, 0))
            )
        outs.append(shape((count, rows, width), BF))
    out_specs = [pl.BlockSpec((size,) + o.shape[1:], lambda i: (i, 0, 0)) for o in outs]
    if joined:
        rows = sum(o.shape[1] for o in outs)
        outs = [shape((rows, width), BF)] * count
        out_specs = [pl.BlockSpec((rows, width), lambda i: (0, 0))] * count
    return pl.pallas_call(
        functools.partial(sum_kernel, len(lists), joined),
        grid=(steps,),
        out_shape=outs,
        in_specs=specs,
        out_specs=out_specs,
        compiler_params=pltpu.CompilerParams(dimension_semantics=("arbitrary",)),
        cost_estimate=pl.CostEstimate(
            flops=1_000_000, bytes_accessed=3_000_000, transcendentals=0
        ),
        name="sums",
    )(*ins)


def level(value):
    return lax.reduce_precision(value, 8, 7)


def level_sum(arrays, at):
    total = arrays[0][at].astype(F32)
    for array in arrays[1:]:
        total = level(total + array[at].astype(F32))
    return total.astype(BF)


def small_sums(lists, start, count):
    return tuple(level_sum(part, slice(start, start + count)) for part in zip(*lists))


def small_blocks(lists):
    parts = [level_sum(part, slice(0, 4)) for part in zip(*lists)]
    return [jnp.concatenate([part[i] for part in parts], axis=0) for i in range(4)]


def swap_each(parts, phases):
    return tuple(swap(part, STEPS[phase][0]) for part, phase in zip(parts, phases))


def swap_z(blocks):
    return tuple(swap(blocks[i + 1], step) for i, step in enumerate(STEPS["z"]))


def last_sum(mine, got):
    got = [g.astype(F32) for g in got]
    return (mine.astype(F32) + got[0]) + (got[1] + got[2])


def codes_of(order):
    codes = [(0, 0)]
    for phase in order:
        grown = list(codes)
        for axis, flip in STEPS[phase]:
            for f, s in codes:
                grown.append((f ^ flip, s) if axis == "fsdp" else (f, s ^ flip))
        codes = grown
    return codes


def dot(a, b):
    return jnp.dot(a, b, preferred_element_type=F32)


def dot_nt(a, b, precision=None):
    return lax.dot_general(
        a, b, (((1,), (1,)), ((), ())), preferred_element_type=F32, precision=precision
    )


def dot_tn(a, b, precision=None):
    return lax.dot_general(
        a, b, (((0,), (0,)), ((), ())), preferred_element_type=F32, precision=precision
    )


def norm_stats(x):
    center = x - jnp.mean(x, axis=-1, keepdims=True)
    spread = jnp.mean(center * center, axis=-1, keepdims=True)
    rate = lax.rsqrt(spread + EPS)
    return center * rate, rate


def norm_back(e, hat, rate):
    return rate * (
        e
        - jnp.mean(e, axis=-1, keepdims=True)
        - hat * jnp.mean(e * hat, axis=-1, keepdims=True)
    )


def turn(u, cosine, sine_a, sine_b):
    return u * cosine + pltpu.roll(u, PAIR - 32, 1) * sine_a + pltpu.roll(u, 32, 1) * sine_b


def turn_back(u, cosine, sine_a, sine_b):
    return u * cosine - pltpu.roll(u, PAIR - 32, 1) * sine_a - pltpu.roll(u, 32, 1) * sine_b


def owners(me, order, pieces):
    codes = codes_of(order)
    for i, piece in enumerate(pieces):
        far, later = divmod(i, 2)
        for k in range(8):
            f, s = codes[8 * later + k]
            yield piece, k, me[0] ^ f, me[1] ^ (s ^ far)


def results(me, order, near, far):
    for core, out in enumerate((near, far)):
        for k, (f, s) in enumerate(codes_of(order)):
            yield out, k, me[0] ^ f, me[1] ^ (s ^ core)


def rows_at(start, count):
    return pl.ds(pl.multiple_of(start, 16), count)


def await_all(ref, sem):
    pltpu.make_async_copy(ref, ref, sem).wait()


def project_kernel(me, xa, xb, seg, cos, sin_a, sin_b, *refs):
    pieces = refs[:8]
    q_o, kv_o, n_o, w_o, g_o, gcol, buf, sem = refs[8:]
    kv_o[:, 1536:] = jnp.broadcast_to(seg[...], (PAIR, 512)).T.astype(BF)
    for order, start, part in ((ORDER_B, 0, pieces[:4]), (ORDER_C, 48, pieces[4:])):
        for piece, k, f, s in owners(me, order, part):
            to = buf.at[s, rows_at(f * 96 + start, 48)]
            pltpu.make_async_copy(piece.at[k], to, sem).start()
    await_all(buf, sem)
    gcol[...] = buf[0, :, 512:640]
    for f in range(GRID_F):
        rows = slice(96 * f, 96 * f + 96)
        w_o[rows, :] = jnp.concatenate([buf[s, rows, :576] for s in range(GRID_S)], axis=1)
    row_i = lax.broadcasted_iota(jnp.int32, (8, 128), 0)
    lane_i = lax.broadcasted_iota(jnp.int32, (8, 128), 1)
    hot = jnp.where(lane_i == row_i + 64, 1.0, 0.0).astype(BF)
    gains = dot_nt(hot, gcol[...])
    g_o[...] = gains
    for half, xr in enumerate((xa, xb)):
        hat, _ = norm_stats(xr[...].astype(F32))
        n_o[256 * half : 256 * half + 256, :] = (hat * gains[0:1, :]).astype(BF)
    for j in range(9):
        y = dot(n_o[...], w_o[:, 256 * j : 256 * j + 256])
        if j < 6:
            y = jnp.concatenate(
                [
                    turn(y[:, 128 * i : 128 * i + 128], cos[...], sin_a[...], sin_b[...])
                    for i in range(2)
                ],
                axis=1,
            )
        if j < 3:
            q_o[:, 256 * j : 256 * j + 256] = (y.astype(BF) * 0.125).astype(BF)
        else:
            kv_o[:, 256 * (j - 3) : 256 * (j - 3) + 256] = y.astype(BF)


def head_masks():
    lane = lax.broadcasted_iota(jnp.int32, (1, PAIR), 1)
    first = jnp.where(lane < HEAD, 1.0, 0.0)
    return lane < HEAD, (first.astype(BF), (1.0 - first).astype(BF))


def attend_kernel(q, ka, kb, va, vb, seg_a, seg_b, out, lse, bias):
    @pl.when(pl.program_id(0) == 0)
    def _():
        own, far = seg_a[...].astype(F32), seg_b[...].astype(F32)
        for side, keys in enumerate((own, far)):
            same = own[:, :1] == keys.T[:1, :]
            bias[:, 512 * side : 512 * side + 512] = jnp.where(same, 0.0, FILL)

    lane, masks = head_masks()
    column = lax.broadcasted_iota(jnp.int32, (512, PAIR), 1)
    ones = jnp.where(column == 0, 1.0, 0.0).astype(BF)
    near, far = (jnp.concatenate([v[...], ones], axis=1) for v in (va, vb))
    for t in range(4):
        rows = slice(128 * t, 128 * t + 128)
        outs, logs = [], []
        for mask in masks:
            qm = q[rows, :] * mask
            sa = dot_nt(qm, ka[...]) + bias[rows, :512]
            sb = dot_nt(qm, kb[...]) + bias[rows, 512:]
            peak = jnp.max(jnp.maximum(sa, sb), axis=-1, keepdims=True)
            ea = jnp.exp(sa - peak).astype(BF)
            eb = jnp.exp(sb - peak).astype(BF)
            o = dot(ea, near) + dot(eb, far)
            total = o[:, PAIR : PAIR + 1]
            outs.append(o[:, :PAIR] * (1.0 / total))
            logs.append(peak + jnp.log(total))
        out[rows, :] = jnp.where(lane, outs[0], outs[1]).astype(BF)
        lse[rows, :] = jnp.where(lane, logs[0], logs[1])


def attend_back_kernel(
    q, ka, kb, va, vb, att, datt, lse, seg_a, seg_b, cos, sin_a, sin_b,
    dq_o, near_o, far_o, bias,
):
    @pl.when(pl.program_id(0) == 0)
    def _():
        own, far = seg_a[...].astype(F32), seg_b[...].astype(F32)
        for side, keys in enumerate((own, far)):
            same = keys[:, :1] == own.T[:1, :]
            bias[512 * side : 512 * side + 512, :] = jnp.where(same, 0.0, FILL)

    lane, masks = head_masks()
    row_i = lax.broadcasted_iota(jnp.int32, (8, PAIR), 0)
    lane_i = lax.broadcasted_iota(jnp.int32, (8, PAIR), 1)
    hot = jnp.where(lane_i == row_i * HEAD, 1.0, 0.0)
    spread = jnp.where((lane_i // HEAD) == row_i, 1.0, 0.0)
    high = lax.Precision.HIGHEST
    log_rows = dot_nt(hot, lse[...], high)
    delta_rows = dot_nt(spread, datt[...].astype(F32) * att[...].astype(F32), high)
    dq_parts = [[None, None], [None, None]]
    dk_parts = [None, None]
    dv_parts = [None, None]
    for side, (k, v) in enumerate(((ka, va), (kb, vb))):
        keys = slice(512 * side, 512 * side + 512)
        for t in range(2):
            rows = slice(256 * t, 256 * t + 256)
            for h, mask in enumerate(masks):
                qm = q[rows, :] * mask
                dm = datt[rows, :] * mask
                s = dot_nt(k[...], qm) + bias[keys, rows]
                p = jnp.exp(s - log_rows[h : h + 1, rows])
                dp = dot_nt(v[...], dm)
                ds = (p * (dp - delta_rows[h : h + 1, rows])).astype(BF)
                dv = dot(p.astype(BF), dm)
                dk = dot(ds, qm)
                dq = dot_tn(ds, k[...])
                dv_parts[side] = dv if dv_parts[side] is None else dv_parts[side] + dv
                dk_parts[side] = dk if dk_parts[side] is None else dk_parts[side] + dk
                old = dq_parts[t][h]
                dq_parts[t][h] = dq if old is None else old + dq
    near_o[:, :PAIR] = dk_parts[0]
    near_o[:, PAIR:] = dv_parts[0]
    far_o[:, :PAIR] = dk_parts[1].astype(BF)
    far_o[:, PAIR:] = dv_parts[1].astype(BF)
    for t in range(2):
        rows = slice(256 * t, 256 * t + 256)
        dq = jnp.where(lane, dq_parts[t][0], dq_parts[t][1]) * 0.125
        dq_o[rows, :] = turn_back(dq, cos[rows, :], sin_a[rows, :], sin_b[rows, :]).astype(BF)


def feed_kernel(me, place, xa, xb, ca, cb, att, gains, *refs):
    pieces = refs[:8]
    mix_pair, mix_b, dmid_o, datt_o, g2_o, near_b, far_b, near_c, far_c = refs[8:17]
    wide, wide_dn, wout, wdn, n2, hid, di, db, grads, grads_dn, flip, sem, mix_a, cot = refs[17:]
    for piece, k, f, s in owners(me, ORDER_B, pieces[:4]):
        to = wide.at[s, rows_at(f * 96, 80)]
        pltpu.make_async_copy(piece.at[k], to, sem.at[0]).start()
    for piece, k, f, s in owners(me, ORDER_C, pieces[4:]):
        to = wide.at[s, rows_at(f * 96 + 80, 16)]
        pltpu.make_async_copy(piece.at[k, pl.ds(0, 16)], to, sem.at[0]).start()
        to = wide_dn.at[f, s]
        pltpu.make_async_copy(piece.at[k, pl.ds(16, 64)], to, sem.at[1]).start()
    await_all(wide, sem.at[0])
    await_all(wide_dn, sem.at[1])
    for f in range(GRID_F):
        at, low = 96 * f, 144 * f
        first, second, third = (
            jnp.concatenate(
                [wide_dn[f, s, :, 192 * j : 192 * j + 192] for s in range(GRID_S)], axis=1
            )
            for j in range(3)
        )
        wout[at : at + 64, :] = first
        wout[at + 64 : at + 96, :] = second[:32]
        wdn[low : low + 32, :] = second[32:]
        wdn[low + 32 : low + 96, :] = third
        wdn[low + 96 : low + 144, :] = jnp.concatenate(
            [
                strip
                for s in range(GRID_S)
                for strip in (
                    wide[s, at : at + 48, 576:],
                    wide[s, at + 48 : at + 96, 576:],
                    wide_dn[f, s, :48, 576:],
                )
            ],
            axis=1,
        )
    gain = gains[1:2, :]
    gain_grad = jnp.zeros((1, 768), F32)
    tokens = jnp.concatenate([xa[...], xb[...]], axis=0)
    cot[:256, :] = ca[...]
    cot[256:, :] = cb[:256, :]
    mid = tokens.astype(F32) + dot(att[...], wout[...])
    hat, rate = norm_stats(mid)
    n2[...] = (hat * gain).astype(BF)
    branch = None
    for h in range(2):
        down = wdn[576 * h : 576 * h + 576, :]
        a = dot(n2[...], wide[h, :, :576])
        gate = dot(n2[...], wide[2 + h, :, :576])
        cdf = 0.5 * (1.0 + lax.erf(a * math.sqrt(0.5)))
        gelu = a * cdf
        hidden = (gelu * gate).astype(BF)
        hid[h] = hidden
        slope = cdf + a * (jnp.exp(-0.5 * a * a) * (1.0 / math.sqrt(2.0 * math.pi)))
        dh = dot_nt(cot[...], down)
        di[h] = (dh * gate * slope).astype(BF)
        di[2 + h] = (dh * gelu).astype(BF)
        part = dot(hidden, down)
        branch = part if branch is None else branch + part
    mixed = (mid + branch).astype(BF)
    mix_a[...] = mixed[:256]
    mix_b[...] = mixed[256:]
    dn = None
    for s in range(4):
        part = dot_nt(di[s], wide[s, :, :576])
        dn = part if dn is None else dn + part
    gain_grad = gain_grad + jnp.sum(dn * hat, axis=0, keepdims=True)
    dmid = cot[...].astype(F32) + norm_back(dn * gain, hat, rate)
    dmid_o[...] = dmid
    db[...] = dmid.astype(BF)
    datt_o[...] = dot_nt(db[...], wout[...]).astype(BF)
    g2_o[...] = jnp.broadcast_to(gain_grad, (8, 768))

    own = pltpu.make_async_copy(mix_a, mix_pair.at[place[1] >> 1], sem.at[2])
    own.start()
    flip[0] = n2[...].T
    flip[1] = att[...].T
    grad_out = dot(flip[1], db[...]).astype(BF)
    for h in range(2):
        grad_down = dot_tn(hid[h], cot[...]).astype(BF)
        for part in range(4):
            f = 4 * h + part
            at = 96 * f
            for s in range(4):
                out = grad_out[at : at + 96, 192 * s : 192 * s + 192]
                low = grad_down[144 * part : 144 * part + 144, 192 * s : 192 * s + 192]
                grads_dn[f, s] = jnp.concatenate(
                    [
                        out[:64],
                        jnp.concatenate([out[64:], low[:32]], axis=0),
                        low[32:96],
                        jnp.concatenate([low[96:, 128:], jnp.zeros((16, 64), BF)], axis=0),
                    ],
                    axis=1,
                )
                grads[s, at : at + 48, 576:] = low[96:, :64]
                grads[s, at + 48 : at + 96, 576:] = low[96:, 64:128]
    for out, k, f, s in results(me, ORDER_C, near_c, far_c):
        to = out.at[k, pl.ds(16, 64)]
        pltpu.make_async_copy(grads_dn.at[f, s], to, sem.at[1]).start()
    for s in range(4):
        grads[s, :, :576] = dot(flip[0], di[s]).astype(BF)
    for out, k, f, s in results(me, ORDER_B, near_b, far_b):
        held = grads.at[s, rows_at(f * 96, 80)]
        pltpu.make_async_copy(held, out.at[k], sem.at[0]).start()
    for out, k, f, s in results(me, ORDER_C, near_c, far_c):
        held = grads.at[s, rows_at(f * 96 + 80, 16)]
        pltpu.make_async_copy(held, out.at[k, pl.ds(0, 16)], sem.at[0]).start()
    await_all(grads, sem.at[0])
    await_all(grads_dn, sem.at[1])
    own.wait()


def weight_grad_kernel(
    me, norm, weight, gains, g2, *refs
):
    heads = refs[:6]
    cos, sin_a, sin_b, dp, near_b, far_b, near_c, far_c, grads, flip, sem = refs[6:]
    for p, (at, pairs) in enumerate(((0, 2), (2 * PAIR, 4))):
        dq, near, far = heads[3 * p : 3 * p + 3]
        dp[:, at : at + pairs * PAIR] = dq[...]
        for i in range(pairs):
            cols = slice(2 * PAIR * i, 2 * PAIR * i + 2 * PAIR)
            total = near[:, cols] + far[:, cols].astype(F32)
            start = 768 + at + PAIR * i
            dp[:, start : start + PAIR] = turn_back(
                total[:, :PAIR], cos[...], sin_a[...], sin_b[...]
            ).astype(BF)
            dp[:, 768 + start : 768 + start + PAIR] = total[:, PAIR:].astype(BF)
    row_i = lax.broadcasted_iota(jnp.int32, (8, 128), 0)
    lane_i = lax.broadcasted_iota(jnp.int32, (8, 128), 1)
    hot = jnp.where((lane_i == row_i + 64) & (row_i < 2), 1.0, 0.0)
    total = jnp.zeros((768, 1), F32)
    flip[...] = norm[...].T
    for s in range(4):
        cols = slice(576 * s, 576 * s + 576)
        grad = dot(flip[...], dp[:, cols])
        total = total + jnp.sum(grad * weight[:, cols].astype(F32), axis=1, keepdims=True)
        grads[s] = jnp.concatenate([grad, jnp.zeros((768, 64), F32)], axis=1).astype(BF)
    row_w = lax.broadcasted_iota(jnp.int32, (8, 768), 0)
    rows = jnp.where(row_w == 0, 1.0 / gains[0:1, :], g2[...])
    columns = dot_tn(rows, hot, lax.Precision.HIGHEST)
    lane = lax.broadcasted_iota(jnp.int32, (1, 128), 1)
    columns = jnp.where(lane == 64, columns * total, columns).astype(BF)
    for s in range(4):
        grads[s, :, 512:] = grads[s, :, 512:] + columns
    for order, start, near, far in ((ORDER_B, 0, near_b, far_b), (ORDER_C, 48, near_c, far_c)):
        for out, k, f, s in results(me, order, near, far):
            held = grads.at[s, rows_at(f * 96 + start, 48)]
            pltpu.make_async_copy(held, out.at[k], sem).start()
    await_all(grads, sem)


def token_grad_kernel(place, xa, xb, weight, gains, dp, dmid, gt_pair, gt_b, gt_a, sem):
    gain = gains[0:1, :]
    for t, (xr, gt) in enumerate(((xa, gt_a), (xb, gt_b))):
        rows = slice(256 * t, 256 * t + 256)
        dn = dot_nt(dp[rows, :], weight[...])
        hat, rate = norm_stats(xr[...].astype(F32))
        gt[...] = (dmid[rows, :] + norm_back(dn * gain, hat, rate)).astype(BF)
    own = pltpu.make_async_copy(gt_a, gt_pair.at[place[1] >> 1], sem)
    own.start()
    own.wait()


def call(kernel, outs, scratch, *args, flops=0, moved=0, name=None):
    def spec(a):
        space = pltpu.SMEM if a.dtype == jnp.int32 else pltpu.VMEM
        return pl.BlockSpec(memory_space=pl.ANY if len(a.shape) == 3 else space)

    specs = [spec(a) for a in args]
    return pl.pallas_call(
        kernel,
        out_shape=outs,
        in_specs=specs,
        out_specs=[spec(a) for a in outs],
        scratch_shapes=scratch,
        compiler_params=pltpu.CompilerParams(vmem_limit_bytes=VMEM_LIMIT),
        cost_estimate=pl.CostEstimate(flops=flops, bytes_accessed=moved, transcendentals=0),
        name=name,
    )(*args)


def shape(dims, dtype):
    return jax.ShapeDtypeStruct(dims, dtype)


def pack(w_in, w_out, w_down):
    both = jnp.concatenate([w_out, w_down], axis=-2)
    rest = both[..., 192:, :]
    strip = jnp.concatenate([rest[..., :64], rest[..., 64:128]], axis=-2)
    tail = jnp.concatenate([rest[..., 128:], jnp.zeros_like(rest[..., :16, 128:])], axis=-2)
    chunks = [both[..., 64 * j : 64 * j + 64, :] for j in range(3)]
    return jnp.concatenate(
        [
            jnp.concatenate([w_in, strip], axis=-1),
            jnp.concatenate(chunks + [tail], axis=-1),
        ],
        axis=-2,
    )


def unpack(block):
    top, low = block[..., :96, :], block[..., 96:, :]
    chunks = [low[..., 192 * j : 192 * j + 192] for j in range(3)]
    strip = jnp.concatenate(
        [top[..., :48, 576:], top[..., 48:, 576:], low[..., :48, 576:]], axis=-1
    )
    both = jnp.concatenate(chunks + [strip], axis=-2)
    return top[..., :576], both[..., :96, :], both[..., 96:, :]


def split_slots(full, width):
    rows = full.shape[0] // GRID_F
    blocks = full.reshape(GRID_F, rows, GRID_S, width).transpose(0, 2, 1, 3)
    found = []
    for order in (ORDER_B, ORDER_C):
        for core in range(2):
            found.append(jnp.stack([blocks[f, s ^ core] for f, s in codes_of(order)]))
    return found


def join_slots(own, other, order):
    table = {}
    for k, (f, s) in enumerate(codes_of(order)):
        table[f, s] = own[k]
        table[f, s ^ 1] = other[k]
    return jnp.stack([jnp.stack([table[f, s] for s in range(GRID_S)]) for f in range(GRID_F)])


def per_device(tokens, segments, w_qkv, w_out, w_in, w_down, gains, cotangent):
    here = lax.axis_size("fsdp") == GRID_F and lax.axis_size("seq") == GRID_S
    s_index = lax.axis_index("seq")
    x_index = s_index // 2
    partner = s_index ^ 2

    count = tokens.shape[1]
    place = jnp.stack([lax.axis_index("fsdp"), s_index]).astype(jnp.int32)

    def pick(pair, i):
        return lax.dynamic_index_in_dim(pair, i, 0, keepdims=False)

    xa, ca = pick(tokens, x_index), pick(cotangent, x_index)
    sega = pick(segments, x_index).astype(F32)
    marks = pick(segments, 1 - x_index).astype(BF)[None]
    marks = jnp.pad(marks, ((0, 15), (0, tokens.shape[2] - count)))
    theirs = jnp.concatenate([pick(cotangent, 1 - x_index), marks], axis=0)
    xb = swap(pick(tokens, 1 - x_index), STEPS["x"][0])

    rows = tokens.shape[1]
    places = jnp.concatenate(
        [s_index * rows + jnp.arange(rows), partner * rows + jnp.arange(rows)]
    ).astype(F32)
    freqs = jnp.exp(-jnp.arange(32, dtype=F32) * (2.0 * math.log(160000.0) / HEAD))
    angles = places[:, None] * freqs[None, :]
    cosine, sine = jnp.cos(angles), jnp.sin(angles)
    zero = jnp.zeros_like(sine)
    cos = jnp.concatenate([cosine] * 4, axis=1)
    sin_a = jnp.concatenate([-sine, zero] * 2, axis=1)
    sin_b = jnp.concatenate([zero, sine] * 2, axis=1)
    if here:
        me = place
        wide = jnp.concatenate(
            [w_qkv, gains.T, jnp.zeros((w_qkv.shape[0], 62), BF)], axis=1
        )
        rest = pack(w_in, w_out, w_down)
        held_q = send_z(wide)
        held_q, xb, rest, theirs, xa, ca, sega, place, cos, sin_a, sin_b = tie(
            (held_q, xb, rest, theirs, xa, ca, sega, place, cos, sin_a, sin_b)
        )
        me = place
        cb = swap(theirs, STEPS["x"][0])
        near_z, far_z = (swap(rest, step) for step in STEPS["z"][:2])
        held_q = cut_rows(held_q, 48)
        got = swap_each(held_q, ("x", "y"))
        held_q, got, near_z, far_z, rest, cb = tie((held_q, got, near_z, far_z, rest, cb))
        held_q = join(held_q, got)
        later_q = swap_each(held_q, ("y", "x"))
        far_q = other_core(held_q)
        last_z = swap(rest, STEPS["z"][2])
        later_q, far_q, last_z = tie((later_q, far_q, last_z))
        held_r = cut_rows((rest, near_z, far_z, last_z), 80)
        far_later_q = other_core(later_q)
        got_r = swap_each(held_r, ("x", "y"))
        qkv = interleave(held_q, later_q, far_q, far_later_q)
    else:
        me = jnp.zeros((2,), jnp.int32)

        def whole(w):
            return lax.all_gather(
                lax.all_gather(w, "fsdp", axis=0, tiled=True), "seq", axis=1, tiled=True
            )

        gains_all = lax.all_gather(gains, "fsdp", axis=1, tiled=True).T
        wide = jnp.concatenate(
            [
                jnp.concatenate([block, gains_all, jnp.zeros((768, 62), BF)], axis=1)
                for block in jnp.split(whole(w_qkv), GRID_S, axis=1)
            ],
            axis=1,
        )
        slots = split_slots(wide, 640)
        qkv = (slots[0][:, :48], slots[1][:, :48], slots[2][:, 48:], slots[3][:, 48:])
        qkv = tuple(half for part in qkv for half in (part[:8], part[8:]))
        slots_in = split_slots(whole(w_in), 576)
        slots_out = split_slots(whole(w_out), 192)
        slots_down = split_slots(whole(w_down), 192)
        slots = [pack(*blocks) for blocks in zip(slots_in, slots_out, slots_down)]
        rest = (slots[0][:, :80], slots[1][:, :80], slots[2][:, 80:], slots[3][:, 80:])
        rest = tuple(half for part in rest for half in (part[:8], part[8:]))
        cb = swap(theirs, STEPS["x"][0])
    seg_mine = jnp.concatenate([sega, cb[count, :count].astype(F32)])[None]

    act = shape((512, 768), BF)
    q, kv, norm, weight, gain_rows = call(
        project_kernel,
        [act, shape((512, 1536 + PAIR), BF), act, shape((768, 2304), BF), shape((8, 768), F32)],
        [
            pltpu.VMEM((768, 128), BF), pltpu.VMEM((4, 768, 640), BF),
            pltpu.SemaphoreType.DMA,
        ],
        me, xa, xb, seg_mine, cos, sin_a, sin_b, *qkv,
        flops=10_000_000_000, moved=20_000_000, name="project",
    )
    far_r, later_r = (), ()
    if here:
        q, kv, held_r, got_r = tie((q, kv, held_r, got_r))
        held_r = join(held_r, got_r)
        later_r = swap_each(held_r, ("y", "x"))
        far_r = other_core(held_r)
    kv_far = swap(kv, STEPS["core"][0])

    pair_spec = pl.BlockSpec((512, PAIR), lambda p: (0, p))
    value_spec = pl.BlockSpec((512, PAIR), lambda p: (0, p + HEADS // 2))
    mark_spec = pl.BlockSpec((512, PAIR), lambda p: (0, HEADS))

    def fixed(dims):
        return pl.BlockSpec(dims, lambda p: (0, 0))

    params = pltpu.CompilerParams(
        vmem_limit_bytes=VMEM_LIMIT, dimension_semantics=("arbitrary",)
    )
    att, lse = pl.pallas_call(
        attend_kernel,
        grid=(HEADS // 2,),
        out_shape=[act, shape((512, 768), F32)],
        in_specs=[pair_spec] * 3 + [value_spec] * 2 + [mark_spec] * 2,
        out_specs=[pair_spec] * 2,
        scratch_shapes=[pltpu.VMEM((512, 1024), F32)],
        compiler_params=params,
        cost_estimate=pl.CostEstimate(
            flops=17_000_000_000, bytes_accessed=8_000_000, transcendentals=6_000_000
        ),
        name="attend",
    )(q, kv, kv_far, kv, kv_far, kv, kv_far)

    if here:
        att, lse, far_r, later_r = tie((att, lse, far_r, later_r))
        rest = interleave(held_r, later_r, far_r, other_core(later_r))
    slot = shape((16, 80, 640), BF)
    mix_pair, mix_b, dmid, datt, g2, fb0, fb1, fc0, fc1 = call(
        feed_kernel,
        [
            shape((2, 256, 768), BF), shape((256, 768), BF), shape((512, 768), F32), act,
            shape((8, 768), F32), slot, slot, slot, slot,
        ],
        [
            pltpu.VMEM((4, 768, 640), BF), pltpu.VMEM((8, 4, 64, 640), BF),
            pltpu.VMEM((768, 768), BF), pltpu.VMEM((1152, 768), BF),
            pltpu.VMEM((512, 768), BF), pltpu.VMEM((2, 512, 576), BF),
            pltpu.VMEM((4, 512, 576), BF), pltpu.VMEM((512, 768), BF),
            pltpu.VMEM((4, 768, 640), BF), pltpu.VMEM((8, 4, 64, 640), BF),
            pltpu.VMEM((2, 768, 512), BF),
            pltpu.SemaphoreType.DMA((3,)), pltpu.VMEM((256, 768), BF),
            pltpu.VMEM((512, 768), BF),
        ],
        me, place, xa, xb, ca, cb, att, gain_rows, *rest,
        flops=35_000_000_000, moved=30_000_000, name="feed",
    )

    def attend_back(first, pairs, *args):
        pair_at = pl.BlockSpec((512, PAIR), lambda p: (0, p + first))
        value_at = pl.BlockSpec((512, PAIR), lambda p: (0, p + first + HEADS // 2))
        both_spec = pl.BlockSpec((512, 2 * PAIR), lambda p: (0, p))
        return pl.pallas_call(
            attend_back_kernel,
            grid=(pairs,),
            out_shape=[
                shape((512, pairs * PAIR), BF),
                shape((512, 2 * pairs * PAIR), F32),
                shape((512, 2 * pairs * PAIR), BF),
            ],
            in_specs=[pair_at] * 3 + [value_at] * 2 + [pair_at] * 3
            + [mark_spec] * 2
            + [fixed((512, PAIR))] * 3,
            out_specs=[pair_spec, both_spec, both_spec],
            scratch_shapes=[pltpu.VMEM((1024, 512), F32)],
            compiler_params=params,
            cost_estimate=pl.CostEstimate(
                flops=6_000_000_000 * pairs, bytes_accessed=4_000_000, transcendentals=2_000_000
            ),
            name="attend_back",
        )(*args)

    attend_args = (
        kv, kv_far, kv, kv_far, att, datt, lse, kv, kv_far,
        cos, sin_a, sin_b,
    )
    back_a = attend_back(0, 2, q, *attend_args)
    own_r, far_r, one_r, two_r = (fb0, fc0), (), (), ()
    mix_far = swap(mix_b, STEPS["x"][0])
    if here:
        far_r = other_core((fb1, fc1))
        back_a, far_r, mix_far = tie((back_a, far_r, mix_far))
        sent = tuple(sums((own_r, far_r), 8, 8, 4))
        sent, q = tie((sent, q))
        one_r = swap_each(sent, ("y", "x"))
    mixed = untrade(place, mix_pair, mix_far)
    far_a = swap(back_a[2], STEPS["core"][0])
    back_b = attend_back(2, 4, q, *attend_args)
    back_b, one_r, mixed = tie((back_b, one_r, mixed))
    far_b = swap(back_b[2], STEPS["core"][0])
    if here:
        sent = tuple(sums((own_r, far_r, one_r), 4, 4, 2))
        sent, far_b = tie((sent, far_b))
        two_r = swap_each(sent, ("x", "y"))

    slot = shape((16, 48, 640), BF)
    dp, lb0, lb1, lc0, lc1 = call(
        weight_grad_kernel,
        [shape((512, 2304), BF), slot, slot, slot, slot],
        [
            pltpu.VMEM((4, 768, 640), BF), pltpu.VMEM((768, 512), BF),
            pltpu.SemaphoreType.DMA,
        ],
        me, norm, weight, gain_rows, g2,
        *(
            part
            for back, far in ((back_a, far_a), (back_b, far_b))
            for part in (back[0], back[1], far)
        ),
        cos, sin_a, sin_b,
        flops=14_000_000_000, moved=20_000_000, name="weight_grad",
    )
    dp, lb0, lb1, lc0, lc1, two_r = tie((dp, lb0, lb1, lc0, lc1, two_r))
    if here:
        own_q = (lb0, lc0)
        far_q = other_core((lb1, lc1))
        blocks_r = tuple(sums((own_r, far_r, one_r, two_r), 0, 4, 1, joined=True))
        far_q, blocks_r = tie((far_q, blocks_r))
        sent, blocks_r, dp = tie((small_sums((own_q, far_q), 8, 8), blocks_r, dp))
        one_q = swap_each(sent, ("y", "x"))
    gt_pair, gt_b = call(
        token_grad_kernel,
        [shape((2, 256, 768), BF), shape((256, 768), BF)],
        [pltpu.VMEM((256, 768), BF), pltpu.SemaphoreType.DMA],
        place, xa, xb, weight, gain_rows, dp, dmid,
        flops=8_000_000_000, moved=10_000_000, name="token_grad",
    )
    if here:
        half = blocks_r[2].shape[0] // 2
        last_z = swap(blocks_r[3], STEPS["z"][2])
        far_z = swap(blocks_r[2][:half], STEPS["z"][1])
        gt_pair, gt_b, one_q, last_z, far_z, blocks_r = tie(
            (gt_pair, gt_b, one_q, last_z, far_z, blocks_r)
        )
        near_z = swap(blocks_r[1], STEPS["z"][0])
        far_z = (far_z, swap(blocks_r[2][half:], STEPS["z"][1]))
        sent, gt_b = tie((small_sums((own_q, far_q, one_q), 4, 4), gt_b))
        two_q = swap_each(sent, ("x", "y"))
    gt_far = swap(gt_b, STEPS["x"][0])
    grad_tokens = untrade(place, gt_pair, gt_far)

    if here:
        two_q, gt_pair, near_z, far_z = tie((two_q, gt_pair, near_z, far_z))
        got_r = (near_z, jnp.concatenate(far_z, axis=0), last_z)
        blocks = small_blocks((own_q, far_q, one_q, two_q))
        rest_sum = last_sum(blocks_r[0], got_r)
        got_q, grad_tokens = tie((swap_z(blocks), grad_tokens))
        grad_qkv = last_sum(blocks[0], got_q)
        grad_in, grad_out, grad_down = unpack(rest_sum)
        grad_gains = grad_qkv[:, 576:578].T
        grad_qkv = grad_qkv[:, :576]
    else:
        full_b = join_slots(fb0, fb1, ORDER_B)
        full_c = join_slots(fc0, fc1, ORDER_C)
        full_q = jnp.concatenate(
            [join_slots(lb0, lb1, ORDER_B), join_slots(lc0, lc1, ORDER_C)], axis=2
        )
        grad_in, grad_out, grad_down = unpack(jnp.concatenate([full_b, full_c], axis=2))

        def share(full):
            flat = full.transpose(0, 2, 1, 3).reshape(-1, GRID_S * full.shape[-1])
            part = lax.psum_scatter(
                flat.astype(F32), "fsdp", scatter_dimension=0, tiled=True
            )
            return lax.psum_scatter(part, "seq", scatter_dimension=1, tiled=True)

        grad_in, grad_out, grad_down = share(grad_in), share(grad_out), share(grad_down)
        grad_qkv = share(full_q[..., :576])
        gain_sum = full_q[:, 0, :, 576:578].reshape(768, 2).astype(F32).T
        grad_gains = lax.psum(
            lax.psum_scatter(gain_sum, "fsdp", scatter_dimension=1, tiled=True), "seq"
        )
    return (mixed, grad_tokens, grad_qkv, grad_out, grad_in, grad_down, grad_gains)


def place_kernel(place, pair, back, out, sem):
    copy = pltpu.make_async_copy(back, out.at[1 - (place[1] >> 1)], sem)
    copy.start()
    copy.wait()


def untrade(place, pair, back):
    anywhere = pl.BlockSpec(memory_space=pl.ANY)
    return pl.pallas_call(
        place_kernel,
        out_shape=shape(pair.shape, pair.dtype),
        in_specs=[
            pl.BlockSpec(memory_space=pltpu.SMEM), anywhere,
            pl.BlockSpec(memory_space=pltpu.VMEM),
        ],
        out_specs=anywhere,
        scratch_shapes=[pltpu.SemaphoreType.DMA],
        input_output_aliases={1: 0},
        name="place",
    )(place, pair, back)


def solution(mesh):
    return jax.shard_map(
        per_device,
        mesh=mesh,
        in_specs=(
            P("fsdp", "seq", None),
            P("fsdp", "seq"),
            P("fsdp", "seq"),
            P("fsdp", "seq"),
            P("fsdp", "seq"),
            P("fsdp", "seq"),
            P(None, "fsdp"),
            P("fsdp", "seq", None),
        ),
        out_specs=(
            P("fsdp", "seq", None),
            P("fsdp", "seq", None),
            P("fsdp", "seq"),
            P("fsdp", "seq"),
            P("fsdp", "seq"),
            P("fsdp", "seq"),
            P(None, "fsdp"),
        ),
        check_vma=False,
    )
```

```python
import functools
import math

import jax
import jax.numpy as jnp
from jax import lax
from jax.experimental import pallas as pl
from jax.experimental.pallas import tpu as pltpu
from jax.sharding import PartitionSpec as P

HEADS = 12
HEAD = 64
PAIR = 2 * HEAD
EPS = 1e-05
FILL = -1000000000.0
BF = jnp.bfloat16
F32 = jnp.float32
VMEM_LIMIT = 60 * 1024 * 1024

STEPS = {
    "x": [("seq", 2)],
    "y": [("fsdp", 1)],
    "z": [("fsdp", 2), ("fsdp", 4), ("fsdp", 6)],
    "core": [("seq", 1)],
}
ORDER_B = ("z", "x", "y")
ORDER_C = ("z", "y", "x")
GRID_F = 8
GRID_S = 4


def swap(value, step):
    axis, flip = step
    size = lax.axis_size(axis)
    return lax.ppermute(value, axis, [(i, i ^ flip) for i in range(size)])


tie = lax.optimization_barrier


def send_z(block):
    return (block,) + tuple(swap(block, step) for step in STEPS["z"])


def cut_rows(blocks, cut):
    return jnp.stack([b[:cut] for b in blocks]), jnp.stack([b[cut:] for b in blocks])


def join(held, got):
    return tuple(jnp.concatenate(pair, axis=0) for pair in zip(held, got))


def interleave(*lists):
    return tuple(piece for part in zip(*lists) for piece in part)


def other_core(parts):
    return tuple(swap(part, STEPS["core"][0]) for part in parts)


def sum_kernel(arrays, joined, *refs):
    ins, outs = refs[: 2 * arrays], refs[2 * arrays :]
    top = 0
    for part in range(2):
        total = ins[arrays * part][...]
        for ref in ins[arrays * part + 1 : arrays * part + arrays]:
            total = (total.astype(F32) + ref[...].astype(F32)).astype(BF)
        rows = total.shape[1]
        if joined:
            for i, out in enumerate(outs):
                out[top : top + rows, :] = total[i]
        else:
            outs[part][...] = total
        top += rows


def sums(lists, start, count, steps, joined=False):
    parts = list(zip(*lists))
    size = count // steps
    ins, specs, outs = [], [], []
    for part in parts:
        rows, width = part[0].shape[1:]
        for array in part:
            ins.append(array)
            specs.append(
                pl.BlockSpec((size, rows, width), lambda i: (start // size + i, 0, 0))
            )
        outs.append(shape((count, rows, width), BF))
    out_specs = [pl.BlockSpec((size,) + o.shape[1:], lambda i: (i, 0, 0)) for o in outs]
    if joined:
        rows = sum(o.shape[1] for o in outs)
        outs = [shape((rows, width), BF)] * count
        out_specs = [pl.BlockSpec((rows, width), lambda i: (0, 0))] * count
    return pl.pallas_call(
        functools.partial(sum_kernel, len(lists), joined),
        grid=(steps,),
        out_shape=outs,
        in_specs=specs,
        out_specs=out_specs,
        compiler_params=pltpu.CompilerParams(dimension_semantics=("arbitrary",)),
        cost_estimate=pl.CostEstimate(
            flops=1_000_000, bytes_accessed=3_000_000, transcendentals=0
        ),
        name="sums",
    )(*ins)


def level(value):
    return lax.reduce_precision(value, 8, 7)


def level_sum(arrays, at):
    total = arrays[0][at].astype(F32)
    for array in arrays[1:]:
        total = level(total + array[at].astype(F32))
    return total.astype(BF)


def small_sums(lists, start, count):
    return tuple(level_sum(part, slice(start, start + count)) for part in zip(*lists))


def small_blocks(lists):
    parts = [level_sum(part, slice(0, 4)) for part in zip(*lists)]
    return [jnp.concatenate([part[i] for part in parts], axis=0) for i in range(4)]


def swap_each(parts, phases):
    return tuple(swap(part, STEPS[phase][0]) for part, phase in zip(parts, phases))


def swap_z(blocks):
    return tuple(swap(blocks[i + 1], step) for i, step in enumerate(STEPS["z"]))


def last_sum(mine, got):
    got = [g.astype(F32) for g in got]
    return (mine.astype(F32) + got[0]) + (got[1] + got[2])


def codes_of(order):
    codes = [(0, 0)]
    for phase in order:
        grown = list(codes)
        for axis, flip in STEPS[phase]:
            for f, s in codes:
                grown.append((f ^ flip, s) if axis == "fsdp" else (f, s ^ flip))
        codes = grown
    return codes


def dot(a, b):
    return jnp.dot(a, b, preferred_element_type=F32)


def dot_nt(a, b, precision=None):
    return lax.dot_general(
        a, b, (((1,), (1,)), ((), ())), preferred_element_type=F32, precision=precision
    )


def dot_tn(a, b, precision=None):
    return lax.dot_general(
        a, b, (((0,), (0,)), ((), ())), preferred_element_type=F32, precision=precision
    )


def norm_stats(x):
    center = x - jnp.mean(x, axis=-1, keepdims=True)
    spread = jnp.mean(center * center, axis=-1, keepdims=True)
    rate = lax.rsqrt(spread + EPS)
    return center * rate, rate


def norm_back(e, hat, rate):
    return rate * (
        e
        - jnp.mean(e, axis=-1, keepdims=True)
        - hat * jnp.mean(e * hat, axis=-1, keepdims=True)
    )


def turn(u, cosine, sine_a, sine_b):
    return u * cosine + pltpu.roll(u, PAIR - 32, 1) * sine_a + pltpu.roll(u, 32, 1) * sine_b


def turn_back(u, cosine, sine_a, sine_b):
    return u * cosine - pltpu.roll(u, PAIR - 32, 1) * sine_a - pltpu.roll(u, 32, 1) * sine_b


def owners(me, order, pieces):
    codes = codes_of(order)
    for i, piece in enumerate(pieces):
        far, later = divmod(i, 2)
        for k in range(8):
            f, s = codes[8 * later + k]
            yield piece, k, me[0] ^ f, me[1] ^ (s ^ far)


def results(me, order, near, far):
    for core, out in enumerate((near, far)):
        for k, (f, s) in enumerate(codes_of(order)):
            yield out, k, me[0] ^ f, me[1] ^ (s ^ core)


def rows_at(start, count):
    return pl.ds(pl.multiple_of(start, 16), count)


def await_all(ref, sem):
    pltpu.make_async_copy(ref, ref, sem).wait()


def project_kernel(me, xa, xb, seg, cos, sin_a, sin_b, *refs):
    pieces = refs[:8]
    q_o, kv_o, n_o, w_o, g_o, gcol, buf, sem = refs[8:]
    kv_o[:, 1536:] = jnp.broadcast_to(seg[...], (PAIR, 512)).T.astype(BF)
    for order, start, part in ((ORDER_B, 0, pieces[:4]), (ORDER_C, 48, pieces[4:])):
        for piece, k, f, s in owners(me, order, part):
            to = buf.at[s, rows_at(f * 96 + start, 48)]
            pltpu.make_async_copy(piece.at[k], to, sem).start()
    await_all(buf, sem)
    gcol[...] = buf[0, :, 512:640]
    for f in range(GRID_F):
        rows = slice(96 * f, 96 * f + 96)
        w_o[rows, :] = jnp.concatenate([buf[s, rows, :576] for s in range(GRID_S)], axis=1)
    row_i = lax.broadcasted_iota(jnp.int32, (8, 128), 0)
    lane_i = lax.broadcasted_iota(jnp.int32, (8, 128), 1)
    hot = jnp.where(lane_i == row_i + 64, 1.0, 0.0).astype(BF)
    gains = dot_nt(hot, gcol[...])
    g_o[...] = gains
    for half, xr in enumerate((xa, xb)):
        hat, _ = norm_stats(xr[...].astype(F32))
        n_o[256 * half : 256 * half + 256, :] = (hat * gains[0:1, :]).astype(BF)
    for j in range(9):
        y = dot(n_o[...], w_o[:, 256 * j : 256 * j + 256])
        if j < 6:
            y = jnp.concatenate(
                [
                    turn(y[:, 128 * i : 128 * i + 128], cos[...], sin_a[...], sin_b[...])
                    for i in range(2)
                ],
                axis=1,
            )
        if j < 3:
            q_o[:, 256 * j : 256 * j + 256] = (y.astype(BF) * 0.125).astype(BF)
        else:
            kv_o[:, 256 * (j - 3) : 256 * (j - 3) + 256] = y.astype(BF)


def head_masks():
    lane = lax.broadcasted_iota(jnp.int32, (1, PAIR), 1)
    first = jnp.where(lane < HEAD, 1.0, 0.0)
    return lane < HEAD, (first.astype(BF), (1.0 - first).astype(BF))


def attend_kernel(q, ka, kb, va, vb, seg_a, seg_b, out, lse, bias):
    @pl.when(pl.program_id(0) == 0)
    def _():
        own, far = seg_a[...].astype(F32), seg_b[...].astype(F32)
        for side, keys in enumerate((own, far)):
            same = own[:, :1] == keys.T[:1, :]
            bias[:, 512 * side : 512 * side + 512] = jnp.where(same, 0.0, FILL)

    lane, masks = head_masks()
    column = lax.broadcasted_iota(jnp.int32, (512, PAIR), 1)
    ones = jnp.where(column == 0, 1.0, 0.0).astype(BF)
    near, far = (jnp.concatenate([v[...], ones], axis=1) for v in (va, vb))
    for t in range(4):
        rows = slice(128 * t, 128 * t + 128)
        outs, logs = [], []
        for mask in masks:
            qm = q[rows, :] * mask
            sa = dot_nt(qm, ka[...]) + bias[rows, :512]
            sb = dot_nt(qm, kb[...]) + bias[rows, 512:]
            peak = jnp.max(jnp.maximum(sa, sb), axis=-1, keepdims=True)
            ea = jnp.exp(sa - peak).astype(BF)
            eb = jnp.exp(sb - peak).astype(BF)
            o = dot(ea, near) + dot(eb, far)
            total = o[:, PAIR : PAIR + 1]
            outs.append(o[:, :PAIR] * (1.0 / total))
            logs.append(peak + jnp.log(total))
        out[rows, :] = jnp.where(lane, outs[0], outs[1]).astype(BF)
        lse[rows, :] = jnp.where(lane, logs[0], logs[1])


def attend_back_kernel(
    q, ka, kb, va, vb, att, datt, lse, seg_a, seg_b, cos, sin_a, sin_b,
    dq_o, near_o, far_o, bias,
):
    @pl.when(pl.program_id(0) == 0)
    def _():
        own, far = seg_a[...].astype(F32), seg_b[...].astype(F32)
        for side, keys in enumerate((own, far)):
            same = keys[:, :1] == own.T[:1, :]
            bias[512 * side : 512 * side + 512, :] = jnp.where(same, 0.0, FILL)

    lane, masks = head_masks()
    row_i = lax.broadcasted_iota(jnp.int32, (8, PAIR), 0)
    lane_i = lax.broadcasted_iota(jnp.int32, (8, PAIR), 1)
    hot = jnp.where(lane_i == row_i * HEAD, 1.0, 0.0)
    spread = jnp.where((lane_i // HEAD) == row_i, 1.0, 0.0)
    high = lax.Precision.HIGHEST
    log_rows = dot_nt(hot, lse[...], high)
    delta_rows = dot_nt(spread, datt[...].astype(F32) * att[...].astype(F32), high)
    dq_parts = [[None, None], [None, None]]
    dk_parts = [None, None]
    dv_parts = [None, None]
    for side, (k, v) in enumerate(((ka, va), (kb, vb))):
        keys = slice(512 * side, 512 * side + 512)
        for t in range(2):
            rows = slice(256 * t, 256 * t + 256)
            for h, mask in enumerate(masks):
                qm = q[rows, :] * mask
                dm = datt[rows, :] * mask
                s = dot_nt(k[...], qm) + bias[keys, rows]
                p = jnp.exp(s - log_rows[h : h + 1, rows])
                dp = dot_nt(v[...], dm)
                ds = (p * (dp - delta_rows[h : h + 1, rows])).astype(BF)
                dv = dot(p.astype(BF), dm)
                dk = dot(ds, qm)
                dq = dot_tn(ds, k[...])
                dv_parts[side] = dv if dv_parts[side] is None else dv_parts[side] + dv
                dk_parts[side] = dk if dk_parts[side] is None else dk_parts[side] + dk
                old = dq_parts[t][h]
                dq_parts[t][h] = dq if old is None else old + dq
    near_o[:, :PAIR] = dk_parts[0].astype(BF)
    near_o[:, PAIR:] = dv_parts[0].astype(BF)
    far_o[:, :PAIR] = dk_parts[1].astype(BF)
    far_o[:, PAIR:] = dv_parts[1].astype(BF)
    for t in range(2):
        rows = slice(256 * t, 256 * t + 256)
        dq = jnp.where(lane, dq_parts[t][0], dq_parts[t][1]) * 0.125
        dq_o[rows, :] = turn_back(dq, cos[rows, :], sin_a[rows, :], sin_b[rows, :]).astype(BF)


def feed_kernel(me, place, xa, xb, ca, cb, att, gains, *refs):
    pieces = refs[:8]
    mix_pair, mix_b, dmid_to, datt_to, g2_o, near_b, far_b, near_c, far_c = refs[8:17]
    dmid_o, datt_o = refs[-2:]
    refs = refs[:-2]
    wide, wide_dn, wout, wdn, n2, hid, di, db, grads, grads_dn, flip, sem, mix_a, cot = refs[17:]
    for piece, k, f, s in owners(me, ORDER_B, pieces[:4]):
        to = wide.at[s, rows_at(f * 96, 80)]
        pltpu.make_async_copy(piece.at[k], to, sem.at[0]).start()
    for piece, k, f, s in owners(me, ORDER_C, pieces[4:]):
        to = wide.at[s, rows_at(f * 96 + 80, 16)]
        pltpu.make_async_copy(piece.at[k, pl.ds(0, 16)], to, sem.at[0]).start()
        to = wide_dn.at[f, s]
        pltpu.make_async_copy(piece.at[k, pl.ds(16, 64)], to, sem.at[1]).start()
    await_all(wide, sem.at[0])
    await_all(wide_dn, sem.at[1])
    for f in range(GRID_F):
        at, low = 96 * f, 144 * f
        first, second, third = (
            jnp.concatenate(
                [wide_dn[f, s, :, 192 * j : 192 * j + 192] for s in range(GRID_S)], axis=1
            )
            for j in range(3)
        )
        wout[at : at + 64, :] = first
        wout[at + 64 : at + 96, :] = second[:32]
        wdn[low : low + 32, :] = second[32:]
        wdn[low + 32 : low + 96, :] = third
        wdn[low + 96 : low + 144, :] = jnp.concatenate(
            [
                strip
                for s in range(GRID_S)
                for strip in (
                    wide[s, at : at + 48, 576:],
                    wide[s, at + 48 : at + 96, 576:],
                    wide_dn[f, s, :48, 576:],
                )
            ],
            axis=1,
        )
    gain = gains[1:2, :]
    gain_grad = jnp.zeros((1, 768), F32)
    tokens = jnp.concatenate([xa[...], xb[...]], axis=0)
    cot[:256, :] = ca[...]
    cot[256:, :] = cb[:256, :]
    mid = tokens.astype(F32) + dot(att[...], wout[...])
    hat, rate = norm_stats(mid)
    n2[...] = (hat * gain).astype(BF)
    branch = None
    for h in range(2):
        down = wdn[576 * h : 576 * h + 576, :]
        a = dot(n2[...], wide[h, :, :576])
        gate = dot(n2[...], wide[2 + h, :, :576])
        cdf = 0.5 * (1.0 + lax.erf(a * math.sqrt(0.5)))
        gelu = a * cdf
        hidden = (gelu * gate).astype(BF)
        hid[h] = hidden
        slope = cdf + a * (jnp.exp(-0.5 * a * a) * (1.0 / math.sqrt(2.0 * math.pi)))
        dh = dot_nt(cot[...], down)
        di[h] = (dh * gate * slope).astype(BF)
        di[2 + h] = (dh * gelu).astype(BF)
        part = dot(hidden, down)
        branch = part if branch is None else branch + part
    mixed = (mid + branch).astype(BF)
    mix_a[...] = mixed[:256]
    mix_b[...] = mixed[256:]
    dn = None
    for s in range(4):
        part = dot_nt(di[s], wide[s, :, :576])
        dn = part if dn is None else dn + part
    gain_grad = gain_grad + jnp.sum(dn * hat, axis=0, keepdims=True)
    dmid = cot[...].astype(F32) + norm_back(dn * gain, hat, rate)
    dmid_o[...] = dmid
    db[...] = dmid.astype(BF)
    datt_o[...] = dot_nt(db[...], wout[...]).astype(BF)
    g2_o[...] = jnp.broadcast_to(gain_grad, (8, 768))

    later = (
        pltpu.make_async_copy(dmid_o, dmid_to, sem.at[3]),
        pltpu.make_async_copy(datt_o, datt_to, sem.at[4]),
    )
    for copy in later:
        copy.start()
    own = pltpu.make_async_copy(mix_a, mix_pair.at[place[1] >> 1], sem.at[2])
    own.start()
    flip[0] = n2[...].T
    flip[1] = att[...].T
    grad_out = dot(flip[1], db[...]).astype(BF)
    for h in range(2):
        grad_down = dot_tn(hid[h], cot[...]).astype(BF)
        for part in range(4):
            f = 4 * h + part
            at = 96 * f
            for s in range(4):
                out = grad_out[at : at + 96, 192 * s : 192 * s + 192]
                low = grad_down[144 * part : 144 * part + 144, 192 * s : 192 * s + 192]
                grads_dn[f, s] = jnp.concatenate(
                    [
                        out[:64],
                        jnp.concatenate([out[64:], low[:32]], axis=0),
                        low[32:96],
                        jnp.concatenate([low[96:, 128:], jnp.zeros((16, 64), BF)], axis=0),
                    ],
                    axis=1,
                )
                grads[s, at : at + 48, 576:] = low[96:, :64]
                grads[s, at + 48 : at + 96, 576:] = low[96:, 64:128]
    for out, k, f, s in results(me, ORDER_C, near_c, far_c):
        to = out.at[k, pl.ds(16, 64)]
        pltpu.make_async_copy(grads_dn.at[f, s], to, sem.at[1]).start()
    for s in range(4):
        grads[s, :, :576] = dot(flip[0], di[s]).astype(BF)
    for out, k, f, s in results(me, ORDER_B, near_b, far_b):
        held = grads.at[s, rows_at(f * 96, 80)]
        pltpu.make_async_copy(held, out.at[k], sem.at[0]).start()
    for out, k, f, s in results(me, ORDER_C, near_c, far_c):
        held = grads.at[s, rows_at(f * 96 + 80, 16)]
        pltpu.make_async_copy(held, out.at[k, pl.ds(0, 16)], sem.at[0]).start()
    await_all(grads, sem.at[0])
    await_all(grads_dn, sem.at[1])
    own.wait()
    for copy in later:
        copy.wait()


def weight_grad_kernel(
    me, norm_in, weight_in, gains, g2, *refs
):
    heads = refs[:6]
    cos, sin_a, sin_b, dp_o, near_b, far_b, near_c, far_c = refs[6:14]
    grads, flip, dp, norm, weight, sem, sems = refs[14:]
    norm_copy = pltpu.make_async_copy(norm_in, norm, sems.at[0])
    weight_copy = pltpu.make_async_copy(weight_in, weight, sems.at[1])
    dp_copy = pltpu.make_async_copy(dp, dp_o, sems.at[2])
    norm_copy.start()
    weight_copy.start()
    for p, (at, pairs) in enumerate(((0, 2), (2 * PAIR, 4))):
        dq, near, far = heads[3 * p : 3 * p + 3]
        dp[:, at : at + pairs * PAIR] = dq[...]
        for i in range(pairs):
            cols = slice(2 * PAIR * i, 2 * PAIR * i + 2 * PAIR)
            total = near[:, cols].astype(F32) + far[:, cols].astype(F32)
            start = 768 + at + PAIR * i
            dp[:, start : start + PAIR] = turn_back(
                total[:, :PAIR], cos[...], sin_a[...], sin_b[...]
            ).astype(BF)
            dp[:, 768 + start : 768 + start + PAIR] = total[:, PAIR:].astype(BF)
    row_i = lax.broadcasted_iota(jnp.int32, (8, 128), 0)
    lane_i = lax.broadcasted_iota(jnp.int32, (8, 128), 1)
    hot = jnp.where((lane_i == row_i + 64) & (row_i < 2), 1.0, 0.0)
    total = jnp.zeros((768, 1), F32)
    dp_copy.start()
    norm_copy.wait()
    flip[...] = norm[...].T
    weight_copy.wait()
    for s in range(4):
        cols = slice(576 * s, 576 * s + 576)
        grad = dot(flip[...], dp[:, cols])
        total = total + jnp.sum(grad * weight[:, cols].astype(F32), axis=1, keepdims=True)
        grads[s] = jnp.concatenate([grad, jnp.zeros((768, 64), F32)], axis=1).astype(BF)
    row_w = lax.broadcasted_iota(jnp.int32, (8, 768), 0)
    rows = jnp.where(row_w == 0, 1.0 / gains[0:1, :], g2[...])
    columns = dot_tn(rows, hot, lax.Precision.HIGHEST)
    lane = lax.broadcasted_iota(jnp.int32, (1, 128), 1)
    columns = jnp.where(lane == 64, columns * total, columns).astype(BF)
    for s in range(4):
        grads[s, :, 512:] = grads[s, :, 512:] + columns
    for order, start, near, far in ((ORDER_B, 0, near_b, far_b), (ORDER_C, 48, near_c, far_c)):
        for out, k, f, s in results(me, order, near, far):
            held = grads.at[s, rows_at(f * 96 + start, 48)]
            pltpu.make_async_copy(held, out.at[k], sem).start()
    await_all(grads, sem)
    dp_copy.wait()


def token_grad_kernel(place, xa, xb, weight, gains, dp, dmid, gt_pair, gt_b, gt_a, sem):
    gain = gains[0:1, :]
    for t, (xr, gt) in enumerate(((xa, gt_a), (xb, gt_b))):
        rows = slice(256 * t, 256 * t + 256)
        dn = dot_nt(dp[rows, :], weight[...])
        hat, rate = norm_stats(xr[...].astype(F32))
        gt[...] = (dmid[rows, :] + norm_back(dn * gain, hat, rate)).astype(BF)
    own = pltpu.make_async_copy(gt_a, gt_pair.at[place[1] >> 1], sem)
    own.start()
    own.wait()


def call(kernel, outs, scratch, *args, flops=0, moved=0, name=None, away=(), away_outs=()):
    def spec(a):
        space = pltpu.SMEM if a.dtype == jnp.int32 else pltpu.VMEM
        return pl.BlockSpec(memory_space=pl.ANY if len(a.shape) == 3 else space)

    anywhere = pl.BlockSpec(memory_space=pl.ANY)
    specs = [anywhere if i in away else spec(a) for i, a in enumerate(args)]
    return pl.pallas_call(
        kernel,
        out_shape=outs,
        in_specs=specs,
        out_specs=[anywhere if i in away_outs else spec(a) for i, a in enumerate(outs)],
        scratch_shapes=scratch,
        compiler_params=pltpu.CompilerParams(vmem_limit_bytes=VMEM_LIMIT),
        cost_estimate=pl.CostEstimate(flops=flops, bytes_accessed=moved, transcendentals=0),
        name=name,
    )(*args)


def shape(dims, dtype):
    return jax.ShapeDtypeStruct(dims, dtype)


def pack(w_in, w_out, w_down):
    both = jnp.concatenate([w_out, w_down], axis=-2)
    rest = both[..., 192:, :]
    strip = jnp.concatenate([rest[..., :64], rest[..., 64:128]], axis=-2)
    tail = jnp.concatenate([rest[..., 128:], jnp.zeros_like(rest[..., :16, 128:])], axis=-2)
    chunks = [both[..., 64 * j : 64 * j + 64, :] for j in range(3)]
    return jnp.concatenate(
        [
            jnp.concatenate([w_in, strip], axis=-1),
            jnp.concatenate(chunks + [tail], axis=-1),
        ],
        axis=-2,
    )


def unpack(block):
    top, low = block[..., :96, :], block[..., 96:, :]
    chunks = [low[..., 192 * j : 192 * j + 192] for j in range(3)]
    strip = jnp.concatenate(
        [top[..., :48, 576:], top[..., 48:, 576:], low[..., :48, 576:]], axis=-1
    )
    both = jnp.concatenate(chunks + [strip], axis=-2)
    return top[..., :576], both[..., :96, :], both[..., 96:, :]


def split_slots(full, width):
    rows = full.shape[0] // GRID_F
    blocks = full.reshape(GRID_F, rows, GRID_S, width).transpose(0, 2, 1, 3)
    found = []
    for order in (ORDER_B, ORDER_C):
        for core in range(2):
            found.append(jnp.stack([blocks[f, s ^ core] for f, s in codes_of(order)]))
    return found


def join_slots(own, other, order):
    table = {}
    for k, (f, s) in enumerate(codes_of(order)):
        table[f, s] = own[k]
        table[f, s ^ 1] = other[k]
    return jnp.stack([jnp.stack([table[f, s] for s in range(GRID_S)]) for f in range(GRID_F)])


def per_device(tokens, segments, w_qkv, w_out, w_in, w_down, gains, cotangent):
    here = lax.axis_size("fsdp") == GRID_F and lax.axis_size("seq") == GRID_S
    s_index = lax.axis_index("seq")
    x_index = s_index // 2
    partner = s_index ^ 2

    count = tokens.shape[1]
    place = jnp.stack([lax.axis_index("fsdp"), s_index]).astype(jnp.int32)

    def pick(pair, i):
        return lax.dynamic_index_in_dim(pair, i, 0, keepdims=False)

    xa, ca = pick(tokens, x_index), pick(cotangent, x_index)
    sega = pick(segments, x_index).astype(F32)
    marks = pick(segments, 1 - x_index).astype(BF)[None]
    marks = jnp.pad(marks, ((0, 15), (0, tokens.shape[2] - count)))
    theirs = jnp.concatenate([pick(cotangent, 1 - x_index), marks], axis=0)
    xb = swap(pick(tokens, 1 - x_index), STEPS["x"][0])

    rows = tokens.shape[1]
    places = jnp.concatenate(
        [s_index * rows + jnp.arange(rows), partner * rows + jnp.arange(rows)]
    ).astype(F32)
    freqs = jnp.exp(-jnp.arange(32, dtype=F32) * (2.0 * math.log(160000.0) / HEAD))
    angles = places[:, None] * freqs[None, :]
    cosine, sine = jnp.cos(angles), jnp.sin(angles)
    zero = jnp.zeros_like(sine)
    cos = jnp.concatenate([cosine] * 4, axis=1)
    sin_a = jnp.concatenate([-sine, zero] * 2, axis=1)
    sin_b = jnp.concatenate([zero, sine] * 2, axis=1)
    if here:
        me = place
        wide = jnp.concatenate(
            [w_qkv, gains.T, jnp.zeros((w_qkv.shape[0], 62), BF)], axis=1
        )
        rest = pack(w_in, w_out, w_down)
        held_q = send_z(wide)
        held_q, xb, rest, theirs, xa, ca, sega, place, cos, sin_a, sin_b = tie(
            (held_q, xb, rest, theirs, xa, ca, sega, place, cos, sin_a, sin_b)
        )
        me = place
        cb = swap(theirs, STEPS["x"][0])
        near_z, far_z = (swap(rest, step) for step in STEPS["z"][:2])
        held_q = cut_rows(held_q, 48)
        got = swap_each(held_q, ("x", "y"))
        held_q, got, near_z, far_z, rest, cb = tie((held_q, got, near_z, far_z, rest, cb))
        held_q = join(held_q, got)
        later_q = swap_each(held_q, ("y", "x"))
        far_q = other_core(held_q)
        last_z = swap(rest, STEPS["z"][2])
        later_q, far_q, last_z = tie((later_q, far_q, last_z))
        held_r = cut_rows((rest, near_z, far_z, last_z), 80)
        far_later_q = other_core(later_q)
        got_r = swap_each(held_r, ("x", "y"))
        qkv = interleave(held_q, later_q, far_q, far_later_q)
    else:
        me = jnp.zeros((2,), jnp.int32)

        def whole(w):
            return lax.all_gather(
                lax.all_gather(w, "fsdp", axis=0, tiled=True), "seq", axis=1, tiled=True
            )

        gains_all = lax.all_gather(gains, "fsdp", axis=1, tiled=True).T
        wide = jnp.concatenate(
            [
                jnp.concatenate([block, gains_all, jnp.zeros((768, 62), BF)], axis=1)
                for block in jnp.split(whole(w_qkv), GRID_S, axis=1)
            ],
            axis=1,
        )
        slots = split_slots(wide, 640)
        qkv = (slots[0][:, :48], slots[1][:, :48], slots[2][:, 48:], slots[3][:, 48:])
        qkv = tuple(half for part in qkv for half in (part[:8], part[8:]))
        slots_in = split_slots(whole(w_in), 576)
        slots_out = split_slots(whole(w_out), 192)
        slots_down = split_slots(whole(w_down), 192)
        slots = [pack(*blocks) for blocks in zip(slots_in, slots_out, slots_down)]
        rest = (slots[0][:, :80], slots[1][:, :80], slots[2][:, 80:], slots[3][:, 80:])
        rest = tuple(half for part in rest for half in (part[:8], part[8:]))
        cb = swap(theirs, STEPS["x"][0])
    seg_mine = jnp.concatenate([sega, cb[count, :count].astype(F32)])[None]

    act = shape((512, 768), BF)
    q, kv, norm, weight, gain_rows = call(
        project_kernel,
        [act, shape((512, 1536 + PAIR), BF), act, shape((768, 2304), BF), shape((8, 768), F32)],
        [
            pltpu.VMEM((768, 128), BF), pltpu.VMEM((4, 768, 640), BF),
            pltpu.SemaphoreType.DMA,
        ],
        me, xa, xb, seg_mine, cos, sin_a, sin_b, *qkv,
        flops=10_000_000_000, moved=20_000_000, name="project",
    )
    far_r, later_r = (), ()
    if here:
        q, kv, held_r, got_r = tie((q, kv, held_r, got_r))
        held_r = join(held_r, got_r)
        later_r = swap_each(held_r, ("y", "x"))
        far_r = other_core(held_r)
    kv_far = swap(kv, STEPS["core"][0])

    pair_spec = pl.BlockSpec((512, PAIR), lambda p: (0, p))
    value_spec = pl.BlockSpec((512, PAIR), lambda p: (0, p + HEADS // 2))
    mark_spec = pl.BlockSpec((512, PAIR), lambda p: (0, HEADS))

    def fixed(dims):
        return pl.BlockSpec(dims, lambda p: (0, 0))

    params = pltpu.CompilerParams(
        vmem_limit_bytes=VMEM_LIMIT, dimension_semantics=("arbitrary",)
    )
    att, lse = pl.pallas_call(
        attend_kernel,
        grid=(HEADS // 2,),
        out_shape=[act, shape((512, 768), F32)],
        in_specs=[pair_spec] * 3 + [value_spec] * 2 + [mark_spec] * 2,
        out_specs=[pair_spec] * 2,
        scratch_shapes=[pltpu.VMEM((512, 1024), F32)],
        compiler_params=params,
        cost_estimate=pl.CostEstimate(
            flops=17_000_000_000, bytes_accessed=8_000_000, transcendentals=6_000_000
        ),
        name="attend",
    )(q, kv, kv_far, kv, kv_far, kv, kv_far)

    if here:
        att, lse, far_r, later_r = tie((att, lse, far_r, later_r))
        rest = interleave(held_r, later_r, far_r, other_core(later_r))
    slot = shape((16, 80, 640), BF)
    mix_pair, mix_b, dmid, datt, g2, fb0, fb1, fc0, fc1 = call(
        feed_kernel,
        [
            shape((2, 256, 768), BF), shape((256, 768), BF), shape((512, 768), F32), act,
            shape((8, 768), F32), slot, slot, slot, slot,
        ],
        [
            pltpu.VMEM((4, 768, 640), BF), pltpu.VMEM((8, 4, 64, 640), BF),
            pltpu.VMEM((768, 768), BF), pltpu.VMEM((1152, 768), BF),
            pltpu.VMEM((512, 768), BF), pltpu.VMEM((2, 512, 576), BF),
            pltpu.VMEM((4, 512, 576), BF), pltpu.VMEM((512, 768), BF),
            pltpu.VMEM((4, 768, 640), BF), pltpu.VMEM((8, 4, 64, 640), BF),
            pltpu.VMEM((2, 768, 512), BF),
            pltpu.SemaphoreType.DMA((5,)), pltpu.VMEM((256, 768), BF),
            pltpu.VMEM((512, 768), BF), pltpu.VMEM((512, 768), F32),
            pltpu.VMEM((512, 768), BF),
        ],
        me, place, xa, xb, ca, cb, att, gain_rows, *rest,
        flops=35_000_000_000, moved=30_000_000, name="feed", away_outs=(2, 3),
    )

    def attend_back(first, pairs, *args):
        pair_at = pl.BlockSpec((512, PAIR), lambda p: (0, p + first))
        value_at = pl.BlockSpec((512, PAIR), lambda p: (0, p + first + HEADS // 2))
        both_spec = pl.BlockSpec((512, 2 * PAIR), lambda p: (0, p))
        return pl.pallas_call(
            attend_back_kernel,
            grid=(pairs,),
            out_shape=[
                shape((512, pairs * PAIR), BF),
                shape((512, 2 * pairs * PAIR), BF),
                shape((512, 2 * pairs * PAIR), BF),
            ],
            in_specs=[pair_at] * 3 + [value_at] * 2 + [pair_at] * 3
            + [mark_spec] * 2
            + [fixed((512, PAIR))] * 3,
            out_specs=[pair_spec, both_spec, both_spec],
            scratch_shapes=[pltpu.VMEM((1024, 512), F32)],
            compiler_params=params,
            cost_estimate=pl.CostEstimate(
                flops=6_000_000_000 * pairs, bytes_accessed=4_000_000, transcendentals=2_000_000
            ),
            name="attend_back",
        )(*args)

    attend_args = (
        kv, kv_far, kv, kv_far, att, datt, lse, kv, kv_far,
        cos, sin_a, sin_b,
    )
    back_a = attend_back(0, 2, q, *attend_args)
    own_r, far_r, one_r, two_r = (fb0, fc0), (), (), ()
    mix_far = swap(mix_b, STEPS["x"][0])
    if here:
        far_r = other_core((fb1, fc1))
        back_a, far_r, mix_far = tie((back_a, far_r, mix_far))
        sent = tuple(sums((own_r, far_r), 8, 8, 2))
        sent, q = tie((sent, q))
        one_r = swap_each(sent, ("y", "x"))
    far_a = swap(back_a[2], STEPS["core"][0])
    back_b = attend_back(2, 4, q, *attend_args)
    back_b, one_r = tie((back_b, one_r))
    far_b = swap(back_b[2], STEPS["core"][0])
    if here:
        sent = tuple(sums((own_r, far_r, one_r), 4, 4, 2))
        sent, far_b = tie((sent, far_b))
        two_r = swap_each(sent, ("x", "y"))

    slot = shape((16, 48, 640), BF)
    dp, lb0, lb1, lc0, lc1 = call(
        weight_grad_kernel,
        [shape((512, 2304), BF), slot, slot, slot, slot],
        [
            pltpu.VMEM((4, 768, 640), BF), pltpu.VMEM((768, 512), BF),
            pltpu.VMEM((512, 2304), BF), pltpu.VMEM((512, 768), BF),
            pltpu.VMEM((768, 2304), BF), pltpu.SemaphoreType.DMA,
            pltpu.SemaphoreType.DMA((3,)),
        ],
        me, norm, weight, gain_rows, g2,
        *(
            part
            for back, far in ((back_a, far_a), (back_b, far_b))
            for part in (back[0], back[1], far)
        ),
        cos, sin_a, sin_b,
        flops=14_000_000_000, moved=20_000_000, name="weight_grad",
        away=(1, 2), away_outs=(0,),
    )
    dp, lb0, lb1, lc0, lc1, two_r = tie((dp, lb0, lb1, lc0, lc1, two_r))
    if here:
        own_q = (lb0, lc0)
        far_q = other_core((lb1, lc1))
        blocks_r = tuple(sums((own_r, far_r, one_r, two_r), 0, 4, 1, joined=True))
        far_q, blocks_r = tie((far_q, blocks_r))
        sent, blocks_r, dp = tie((small_sums((own_q, far_q), 8, 8), blocks_r, dp))
        one_q = swap_each(sent, ("y", "x"))
    gt_pair, gt_b = call(
        token_grad_kernel,
        [shape((2, 256, 768), BF), shape((256, 768), BF)],
        [pltpu.VMEM((256, 768), BF), pltpu.SemaphoreType.DMA],
        place, xa, xb, weight, gain_rows, dp, dmid,
        flops=8_000_000_000, moved=10_000_000, name="token_grad",
    )
    if here:
        half = blocks_r[2].shape[0] // 2
        last_z = swap(blocks_r[3], STEPS["z"][2])
        far_z = swap(blocks_r[2][:half], STEPS["z"][1])
        near_z = swap(blocks_r[1], STEPS["z"][0])
        gt_pair, gt_b, one_q, near_z, last_z, far_z, blocks_r, mix_pair, mix_far = tie(
            (gt_pair, gt_b, one_q, near_z, last_z, far_z, blocks_r, mix_pair, mix_far)
        )
        far_z = (far_z, swap(blocks_r[2][half:], STEPS["z"][1]))
        sent, gt_b = tie((small_sums((own_q, far_q, one_q), 4, 4), gt_b))
        two_q = swap_each(sent, ("x", "y"))
    mixed = untrade(place, mix_pair, mix_far)
    if here:
        two_q, far_z, mixed, gt_b = tie((two_q, far_z, mixed, gt_b))
    gt_far = swap(gt_b, STEPS["x"][0])
    grad_tokens = untrade(place, gt_pair, gt_far)

    if here:
        got_r = (near_z, jnp.concatenate(far_z, axis=0), last_z)
        blocks = small_blocks((own_q, far_q, one_q, two_q))
        rest_sum = last_sum(blocks_r[0], got_r)
        got_q, grad_tokens = tie((swap_z(blocks), grad_tokens))
        grad_qkv = last_sum(blocks[0], got_q)
        grad_in, grad_out, grad_down = unpack(rest_sum)
        grad_gains = grad_qkv[:, 576:578].T
        grad_qkv = grad_qkv[:, :576]
    else:
        full_b = join_slots(fb0, fb1, ORDER_B)
        full_c = join_slots(fc0, fc1, ORDER_C)
        full_q = jnp.concatenate(
            [join_slots(lb0, lb1, ORDER_B), join_slots(lc0, lc1, ORDER_C)], axis=2
        )
        grad_in, grad_out, grad_down = unpack(jnp.concatenate([full_b, full_c], axis=2))

        def share(full):
            flat = full.transpose(0, 2, 1, 3).reshape(-1, GRID_S * full.shape[-1])
            part = lax.psum_scatter(
                flat.astype(F32), "fsdp", scatter_dimension=0, tiled=True
            )
            return lax.psum_scatter(part, "seq", scatter_dimension=1, tiled=True)

        grad_in, grad_out, grad_down = share(grad_in), share(grad_out), share(grad_down)
        grad_qkv = share(full_q[..., :576])
        gain_sum = full_q[:, 0, :, 576:578].reshape(768, 2).astype(F32).T
        grad_gains = lax.psum(
            lax.psum_scatter(gain_sum, "fsdp", scatter_dimension=1, tiled=True), "seq"
        )
    return (mixed, grad_tokens, grad_qkv, grad_out, grad_in, grad_down, grad_gains)


def place_kernel(place, pair, back, out, sem):
    copy = pltpu.make_async_copy(back, out.at[1 - (place[1] >> 1)], sem)
    copy.start()
    copy.wait()


def untrade(place, pair, back):
    anywhere = pl.BlockSpec(memory_space=pl.ANY)
    return pl.pallas_call(
        place_kernel,
        out_shape=shape(pair.shape, pair.dtype),
        in_specs=[
            pl.BlockSpec(memory_space=pltpu.SMEM), anywhere,
            pl.BlockSpec(memory_space=pltpu.VMEM),
        ],
        out_specs=anywhere,
        scratch_shapes=[pltpu.SemaphoreType.DMA],
        input_output_aliases={1: 0},
        name="place",
    )(place, pair, back)


def solution(mesh):
    return jax.shard_map(
        per_device,
        mesh=mesh,
        in_specs=(
            P("fsdp", "seq", None),
            P("fsdp", "seq"),
            P("fsdp", "seq"),
            P("fsdp", "seq"),
            P("fsdp", "seq"),
            P("fsdp", "seq"),
            P(None, "fsdp"),
            P("fsdp", "seq", None),
        ),
        out_specs=(
            P("fsdp", "seq", None),
            P("fsdp", "seq", None),
            P("fsdp", "seq"),
            P("fsdp", "seq"),
            P("fsdp", "seq"),
            P("fsdp", "seq"),
            P(None, "fsdp"),
        ),
        check_vma=False,
    )
```

```python
import functools
import math

import jax
import jax.numpy as jnp
from jax import lax
from jax.experimental import pallas as pl
from jax.experimental.pallas import tpu as pltpu
from jax.sharding import PartitionSpec as P

HEADS = 12
HEAD = 64
PAIR = 2 * HEAD
EPS = 1e-05
FILL = -1000000000.0
BF = jnp.bfloat16
F32 = jnp.float32
VMEM_LIMIT = 60 * 1024 * 1024

STEPS = {
    "x": [("seq", 2)],
    "y": [("fsdp", 1)],
    "z": [("fsdp", 2), ("fsdp", 4), ("fsdp", 6)],
    "core": [("seq", 1)],
}
ORDER_B = ("z", "x", "y")
ORDER_C = ("z", "y", "x")
GRID_F = 8
GRID_S = 4


def swap(value, step):
    axis, flip = step
    size = lax.axis_size(axis)
    return lax.ppermute(value, axis, [(i, i ^ flip) for i in range(size)])


tie = lax.optimization_barrier


def send_z(block):
    return (block,) + tuple(swap(block, step) for step in STEPS["z"])


def cut_rows(blocks, cut):
    return jnp.stack([b[:cut] for b in blocks]), jnp.stack([b[cut:] for b in blocks])


def join(held, got):
    return tuple(jnp.concatenate(pair, axis=0) for pair in zip(held, got))


def interleave(*lists):
    return tuple(piece for part in zip(*lists) for piece in part)


def other_core(parts):
    return tuple(swap(part, STEPS["core"][0]) for part in parts)


def sum_kernel(arrays, joined, *refs):
    ins, outs = refs[: 2 * arrays], refs[2 * arrays :]
    top = 0
    for part in range(2):
        total = ins[arrays * part][...]
        for ref in ins[arrays * part + 1 : arrays * part + arrays]:
            total = (total.astype(F32) + ref[...].astype(F32)).astype(BF)
        rows = total.shape[1]
        if joined:
            for i, out in enumerate(outs):
                out[top : top + rows, :] = total[i]
        else:
            outs[part][...] = total
        top += rows


def sums(lists, start, count, steps, joined=False):
    parts = list(zip(*lists))
    size = count // steps
    ins, specs, outs = [], [], []
    for part in parts:
        rows, width = part[0].shape[1:]
        for array in part:
            ins.append(array)
            specs.append(
                pl.BlockSpec((size, rows, width), lambda i: (start // size + i, 0, 0))
            )
        outs.append(shape((count, rows, width), BF))
    out_specs = [pl.BlockSpec((size,) + o.shape[1:], lambda i: (i, 0, 0)) for o in outs]
    if joined:
        rows = sum(o.shape[1] for o in outs)
        outs = [shape((rows, width), BF)] * count
        out_specs = [pl.BlockSpec((rows, width), lambda i: (0, 0))] * count
    return pl.pallas_call(
        functools.partial(sum_kernel, len(lists), joined),
        grid=(steps,),
        out_shape=outs,
        in_specs=specs,
        out_specs=out_specs,
        compiler_params=pltpu.CompilerParams(dimension_semantics=("arbitrary",)),
        cost_estimate=pl.CostEstimate(
            flops=1_000_000, bytes_accessed=3_000_000, transcendentals=0
        ),
        name="sums",
    )(*ins)


def level(value):
    return lax.reduce_precision(value, 8, 7)


def level_sum(arrays, at):
    total = arrays[0][at].astype(F32)
    for array in arrays[1:]:
        total = level(total + array[at].astype(F32))
    return total.astype(BF)


def small_sums(lists, start, count):
    return tuple(level_sum(part, slice(start, start + count)) for part in zip(*lists))


def small_blocks(lists):
    parts = [level_sum(part, slice(0, 4)) for part in zip(*lists)]
    return [jnp.concatenate([part[i] for part in parts], axis=0) for i in range(4)]


def swap_each(parts, phases):
    return tuple(swap(part, STEPS[phase][0]) for part, phase in zip(parts, phases))


def swap_z(blocks):
    return tuple(swap(blocks[i + 1], step) for i, step in enumerate(STEPS["z"]))


def last_sum(mine, got):
    got = [g.astype(F32) for g in got]
    return (mine.astype(F32) + got[0]) + (got[1] + got[2])


def codes_of(order):
    codes = [(0, 0)]
    for phase in order:
        grown = list(codes)
        for axis, flip in STEPS[phase]:
            for f, s in codes:
                grown.append((f ^ flip, s) if axis == "fsdp" else (f, s ^ flip))
        codes = grown
    return codes


def dot(a, b):
    return jnp.dot(a, b, preferred_element_type=F32)


def dot_nt(a, b, precision=None):
    return lax.dot_general(
        a, b, (((1,), (1,)), ((), ())), preferred_element_type=F32, precision=precision
    )


def dot_tn(a, b, precision=None):
    return lax.dot_general(
        a, b, (((0,), (0,)), ((), ())), preferred_element_type=F32, precision=precision
    )


def norm_stats(x):
    center = x - jnp.mean(x, axis=-1, keepdims=True)
    spread = jnp.mean(center * center, axis=-1, keepdims=True)
    rate = lax.rsqrt(spread + EPS)
    return center * rate, rate


def norm_back(e, hat, rate):
    return rate * (
        e
        - jnp.mean(e, axis=-1, keepdims=True)
        - hat * jnp.mean(e * hat, axis=-1, keepdims=True)
    )


def turn(u, cosine, sine_a, sine_b):
    return u * cosine + pltpu.roll(u, PAIR - 32, 1) * sine_a + pltpu.roll(u, 32, 1) * sine_b


def turn_back(u, cosine, sine_a, sine_b):
    return u * cosine - pltpu.roll(u, PAIR - 32, 1) * sine_a - pltpu.roll(u, 32, 1) * sine_b


def owners(me, order, pieces):
    codes = codes_of(order)
    for i, piece in enumerate(pieces):
        far, later = divmod(i, 2)
        for k in range(8):
            f, s = codes[8 * later + k]
            yield piece, k, me[0] ^ f, me[1] ^ (s ^ far)


def results(me, order, near, far):
    for core, out in enumerate((near, far)):
        for k, (f, s) in enumerate(codes_of(order)):
            yield out, k, me[0] ^ f, me[1] ^ (s ^ core)


def rows_at(start, count):
    return pl.ds(pl.multiple_of(start, 16), count)


def await_all(ref, sem):
    pltpu.make_async_copy(ref, ref, sem).wait()


def project_kernel(me, xa, xb, seg, cos, sin_a, sin_b, *refs):
    pieces = refs[:8]
    q_o, kv_o, n_o, w_o, g_o, gcol, buf, sem = refs[8:]
    kv_o[:, 1536:] = jnp.broadcast_to(seg[...], (PAIR, 512)).T.astype(BF)
    for order, start, part in ((ORDER_B, 0, pieces[:4]), (ORDER_C, 48, pieces[4:])):
        for piece, k, f, s in owners(me, order, part):
            to = buf.at[s, rows_at(f * 96 + start, 48)]
            pltpu.make_async_copy(piece.at[k], to, sem).start()
    await_all(buf, sem)
    gcol[...] = buf[0, :, 512:640]
    for f in range(GRID_F):
        rows = slice(96 * f, 96 * f + 96)
        w_o[rows, :] = jnp.concatenate([buf[s, rows, :576] for s in range(GRID_S)], axis=1)
    row_i = lax.broadcasted_iota(jnp.int32, (8, 128), 0)
    lane_i = lax.broadcasted_iota(jnp.int32, (8, 128), 1)
    hot = jnp.where(lane_i == row_i + 64, 1.0, 0.0).astype(BF)
    gains = dot_nt(hot, gcol[...])
    g_o[...] = gains
    for half, xr in enumerate((xa, xb)):
        hat, _ = norm_stats(xr[...].astype(F32))
        n_o[256 * half : 256 * half + 256, :] = (hat * gains[0:1, :]).astype(BF)
    for j in range(9):
        y = dot(n_o[...], w_o[:, 256 * j : 256 * j + 256])
        if j < 6:
            y = jnp.concatenate(
                [
                    turn(y[:, 128 * i : 128 * i + 128], cos[...], sin_a[...], sin_b[...])
                    for i in range(2)
                ],
                axis=1,
            )
        if j < 3:
            q_o[:, 256 * j : 256 * j + 256] = (y.astype(BF) * 0.125).astype(BF)
        else:
            kv_o[:, 256 * (j - 3) : 256 * (j - 3) + 256] = y.astype(BF)


def head_masks():
    lane = lax.broadcasted_iota(jnp.int32, (1, PAIR), 1)
    first = jnp.where(lane < HEAD, 1.0, 0.0)
    return lane < HEAD, (first.astype(BF), (1.0 - first).astype(BF))


def attend_kernel(q, ka, kb, va, vb, seg_a, seg_b, out, lse, bias):
    @pl.when(pl.program_id(0) == 0)
    def _():
        own, far = seg_a[...].astype(F32), seg_b[...].astype(F32)
        for side, keys in enumerate((own, far)):
            same = own[:, :1] == keys.T[:1, :]
            bias[:, 512 * side : 512 * side + 512] = jnp.where(same, 0.0, FILL)

    lane, masks = head_masks()
    column = lax.broadcasted_iota(jnp.int32, (512, PAIR), 1)
    ones = jnp.where(column == 0, 1.0, 0.0).astype(BF)
    near, far = (jnp.concatenate([v[...], ones], axis=1) for v in (va, vb))
    for t in range(4):
        rows = slice(128 * t, 128 * t + 128)
        outs, logs = [], []
        for mask in masks:
            qm = q[rows, :] * mask
            sa = dot_nt(qm, ka[...]) + bias[rows, :512]
            sb = dot_nt(qm, kb[...]) + bias[rows, 512:]
            peak = jnp.max(jnp.maximum(sa, sb), axis=-1, keepdims=True)
            ea = jnp.exp(sa - peak).astype(BF)
            eb = jnp.exp(sb - peak).astype(BF)
            o = dot(ea, near) + dot(eb, far)
            total = o[:, PAIR : PAIR + 1]
            outs.append(o[:, :PAIR] * (1.0 / total))
            logs.append(peak + jnp.log(total))
        out[rows, :] = jnp.where(lane, outs[0], outs[1]).astype(BF)
        lse[rows, :] = jnp.where(lane, logs[0], logs[1])


def attend_back_kernel(
    q, ka, kb, va, vb, att, datt, lse, seg_a, seg_b, cos, sin_a, sin_b,
    dq_o, near_o, far_o, bias,
):
    @pl.when(pl.program_id(0) == 0)
    def _():
        own, far = seg_a[...].astype(F32), seg_b[...].astype(F32)
        for side, keys in enumerate((own, far)):
            same = keys[:, :1] == own.T[:1, :]
            bias[512 * side : 512 * side + 512, :] = jnp.where(same, 0.0, FILL)

    lane, masks = head_masks()
    row_i = lax.broadcasted_iota(jnp.int32, (8, PAIR), 0)
    lane_i = lax.broadcasted_iota(jnp.int32, (8, PAIR), 1)
    hot = jnp.where(lane_i == row_i * HEAD, 1.0, 0.0)
    spread = jnp.where((lane_i // HEAD) == row_i, 1.0, 0.0)
    high = lax.Precision.HIGHEST
    log_rows = dot_nt(hot, lse[...], high)
    delta_rows = dot_nt(spread, datt[...].astype(F32) * att[...].astype(F32), high)
    dq_parts = [[None, None], [None, None]]
    dk_parts = [None, None]
    dv_parts = [None, None]
    for side, (k, v) in enumerate(((ka, va), (kb, vb))):
        keys = slice(512 * side, 512 * side + 512)
        for t in range(2):
            rows = slice(256 * t, 256 * t + 256)
            for h, mask in enumerate(masks):
                qm = q[rows, :] * mask
                dm = datt[rows, :] * mask
                s = dot_nt(k[...], qm) + bias[keys, rows]
                p = jnp.exp(s - log_rows[h : h + 1, rows])
                dp = dot_nt(v[...], dm)
                ds = (p * (dp - delta_rows[h : h + 1, rows])).astype(BF)
                dv = dot(p.astype(BF), dm)
                dk = dot(ds, qm)
                dq = dot_tn(ds, k[...])
                dv_parts[side] = dv if dv_parts[side] is None else dv_parts[side] + dv
                dk_parts[side] = dk if dk_parts[side] is None else dk_parts[side] + dk
                old = dq_parts[t][h]
                dq_parts[t][h] = dq if old is None else old + dq
    near_o[:, :PAIR] = dk_parts[0]
    near_o[:, PAIR:] = dv_parts[0]
    far_o[:, :PAIR] = dk_parts[1].astype(BF)
    far_o[:, PAIR:] = dv_parts[1].astype(BF)
    for t in range(2):
        rows = slice(256 * t, 256 * t + 256)
        dq = jnp.where(lane, dq_parts[t][0], dq_parts[t][1]) * 0.125
        dq_o[rows, :] = turn_back(dq, cos[rows, :], sin_a[rows, :], sin_b[rows, :]).astype(BF)


def feed_kernel(me, place, xa, xb, ca, cb, att, gains, *refs):
    pieces = refs[:8]
    mix_pair, mix_b, dmid_to, datt_to, g2_o, near_b, far_b, near_c, far_c = refs[8:17]
    dmid_o, datt_o = refs[-2:]
    refs = refs[:-2]
    wide, wide_dn, wout, wdn, n2, hid, di, db, grads, grads_dn, flip, sem, mix_a, cot = refs[17:]
    for piece, k, f, s in owners(me, ORDER_B, pieces[:4]):
        to = wide.at[s, rows_at(f * 96, 80)]
        pltpu.make_async_copy(piece.at[k], to, sem.at[0]).start()
    for piece, k, f, s in owners(me, ORDER_C, pieces[4:]):
        to = wide.at[s, rows_at(f * 96 + 80, 16)]
        pltpu.make_async_copy(piece.at[k, pl.ds(0, 16)], to, sem.at[0]).start()
        to = wide_dn.at[f, s]
        pltpu.make_async_copy(piece.at[k, pl.ds(16, 64)], to, sem.at[1]).start()
    await_all(wide, sem.at[0])
    await_all(wide_dn, sem.at[1])
    for f in range(GRID_F):
        at, low = 96 * f, 144 * f
        first, second, third = (
            jnp.concatenate(
                [wide_dn[f, s, :, 192 * j : 192 * j + 192] for s in range(GRID_S)], axis=1
            )
            for j in range(3)
        )
        wout[at : at + 64, :] = first
        wout[at + 64 : at + 96, :] = second[:32]
        wdn[low : low + 32, :] = second[32:]
        wdn[low + 32 : low + 96, :] = third
        wdn[low + 96 : low + 144, :] = jnp.concatenate(
            [
                strip
                for s in range(GRID_S)
                for strip in (
                    wide[s, at : at + 48, 576:],
                    wide[s, at + 48 : at + 96, 576:],
                    wide_dn[f, s, :48, 576:],
                )
            ],
            axis=1,
        )
    gain = gains[1:2, :]
    gain_grad = jnp.zeros((1, 768), F32)
    tokens = jnp.concatenate([xa[...], xb[...]], axis=0)
    cot[:256, :] = ca[...]
    cot[256:, :] = cb[:256, :]
    mid = tokens.astype(F32) + dot(att[...], wout[...])
    hat, rate = norm_stats(mid)
    n2[...] = (hat * gain).astype(BF)
    branch = None
    for h in range(2):
        down = wdn[576 * h : 576 * h + 576, :]
        a = dot(n2[...], wide[h, :, :576])
        gate = dot(n2[...], wide[2 + h, :, :576])
        cdf = 0.5 * (1.0 + lax.erf(a * math.sqrt(0.5)))
        gelu = a * cdf
        hidden = (gelu * gate).astype(BF)
        hid[h] = hidden
        slope = cdf + a * (jnp.exp(-0.5 * a * a) * (1.0 / math.sqrt(2.0 * math.pi)))
        dh = dot_nt(cot[...], down)
        di[h] = (dh * gate * slope).astype(BF)
        di[2 + h] = (dh * gelu).astype(BF)
        part = dot(hidden, down)
        branch = part if branch is None else branch + part
    mixed = (mid + branch).astype(BF)
    mix_a[...] = mixed[:256]
    mix_b[...] = mixed[256:]
    dn = None
    for s in range(4):
        part = dot_nt(di[s], wide[s, :, :576])
        dn = part if dn is None else dn + part
    gain_grad = gain_grad + jnp.sum(dn * hat, axis=0, keepdims=True)
    dmid = cot[...].astype(F32) + norm_back(dn * gain, hat, rate)
    dmid_o[...] = dmid
    db[...] = dmid.astype(BF)
    datt_o[...] = dot_nt(db[...], wout[...]).astype(BF)
    g2_o[...] = jnp.broadcast_to(gain_grad, (8, 768))

    later = (
        pltpu.make_async_copy(dmid_o, dmid_to, sem.at[3]),
        pltpu.make_async_copy(datt_o, datt_to, sem.at[4]),
    )
    for copy in later:
        copy.start()
    own = pltpu.make_async_copy(mix_a, mix_pair.at[place[1] >> 1], sem.at[2])
    own.start()
    flip[0] = n2[...].T
    flip[1] = att[...].T
    grad_out = dot(flip[1], db[...]).astype(BF)
    for h in range(2):
        grad_down = dot_tn(hid[h], cot[...]).astype(BF)
        for part in range(4):
            f = 4 * h + part
            at = 96 * f
            for s in range(4):
                out = grad_out[at : at + 96, 192 * s : 192 * s + 192]
                low = grad_down[144 * part : 144 * part + 144, 192 * s : 192 * s + 192]
                grads_dn[f, s] = jnp.concatenate(
                    [
                        out[:64],
                        jnp.concatenate([out[64:], low[:32]], axis=0),
                        low[32:96],
                        jnp.concatenate([low[96:, 128:], jnp.zeros((16, 64), BF)], axis=0),
                    ],
                    axis=1,
                )
                grads[s, at : at + 48, 576:] = low[96:, :64]
                grads[s, at + 48 : at + 96, 576:] = low[96:, 64:128]
    for out, k, f, s in results(me, ORDER_C, near_c, far_c):
        to = out.at[k, pl.ds(16, 64)]
        pltpu.make_async_copy(grads_dn.at[f, s], to, sem.at[1]).start()
    for s in range(4):
        grads[s, :, :576] = dot(flip[0], di[s]).astype(BF)
    for out, k, f, s in results(me, ORDER_B, near_b, far_b):
        held = grads.at[s, rows_at(f * 96, 80)]
        pltpu.make_async_copy(held, out.at[k], sem.at[0]).start()
    for out, k, f, s in results(me, ORDER_C, near_c, far_c):
        held = grads.at[s, rows_at(f * 96 + 80, 16)]
        pltpu.make_async_copy(held, out.at[k, pl.ds(0, 16)], sem.at[0]).start()
    await_all(grads, sem.at[0])
    await_all(grads_dn, sem.at[1])
    own.wait()
    for copy in later:
        copy.wait()


def weight_grad_kernel(
    me, norm, weight, gains, g2, *refs
):
    heads = refs[:6]
    cos, sin_a, sin_b, dp, near_b, far_b, near_c, far_c, grads, flip, sem = refs[6:]
    for p, (at, pairs) in enumerate(((0, 2), (2 * PAIR, 4))):
        dq, near, far = heads[3 * p : 3 * p + 3]
        dp[:, at : at + pairs * PAIR] = dq[...]
        for i in range(pairs):
            cols = slice(2 * PAIR * i, 2 * PAIR * i + 2 * PAIR)
            total = near[:, cols] + far[:, cols].astype(F32)
            start = 768 + at + PAIR * i
            dp[:, start : start + PAIR] = turn_back(
                total[:, :PAIR], cos[...], sin_a[...], sin_b[...]
            ).astype(BF)
            dp[:, 768 + start : 768 + start + PAIR] = total[:, PAIR:].astype(BF)
    row_i = lax.broadcasted_iota(jnp.int32, (8, 128), 0)
    lane_i = lax.broadcasted_iota(jnp.int32, (8, 128), 1)
    hot = jnp.where((lane_i == row_i + 64) & (row_i < 2), 1.0, 0.0)
    total = jnp.zeros((768, 1), F32)
    flip[...] = norm[...].T
    for s in range(4):
        cols = slice(576 * s, 576 * s + 576)
        grad = dot(flip[...], dp[:, cols])
        total = total + jnp.sum(grad * weight[:, cols].astype(F32), axis=1, keepdims=True)
        grads[s] = jnp.concatenate([grad, jnp.zeros((768, 64), F32)], axis=1).astype(BF)
    row_w = lax.broadcasted_iota(jnp.int32, (8, 768), 0)
    rows = jnp.where(row_w == 0, 1.0 / gains[0:1, :], g2[...])
    columns = dot_tn(rows, hot, lax.Precision.HIGHEST)
    lane = lax.broadcasted_iota(jnp.int32, (1, 128), 1)
    columns = jnp.where(lane == 64, columns * total, columns).astype(BF)
    for s in range(4):
        grads[s, :, 512:] = grads[s, :, 512:] + columns
    for order, start, near, far in ((ORDER_B, 0, near_b, far_b), (ORDER_C, 48, near_c, far_c)):
        for out, k, f, s in results(me, order, near, far):
            held = grads.at[s, rows_at(f * 96 + start, 48)]
            pltpu.make_async_copy(held, out.at[k], sem).start()
    await_all(grads, sem)


def token_grad_kernel(place, xa, xb, weight, gains, dp, dmid, gt_pair, gt_b, gt_a, sem):
    gain = gains[0:1, :]
    for t, (xr, gt) in enumerate(((xa, gt_a), (xb, gt_b))):
        rows = slice(256 * t, 256 * t + 256)
        dn = dot_nt(dp[rows, :], weight[...])
        hat, rate = norm_stats(xr[...].astype(F32))
        gt[...] = (dmid[rows, :] + norm_back(dn * gain, hat, rate)).astype(BF)
    own = pltpu.make_async_copy(gt_a, gt_pair.at[place[1] >> 1], sem)
    own.start()
    own.wait()


def call(kernel, outs, scratch, *args, flops=0, moved=0, name=None, away_outs=()):
    def spec(a):
        space = pltpu.SMEM if a.dtype == jnp.int32 else pltpu.VMEM
        return pl.BlockSpec(memory_space=pl.ANY if len(a.shape) == 3 else space)

    specs = [spec(a) for a in args]
    return pl.pallas_call(
        kernel,
        out_shape=outs,
        in_specs=specs,
        out_specs=[
            pl.BlockSpec(memory_space=pl.ANY) if i in away_outs else spec(a)
            for i, a in enumerate(outs)
        ],
        scratch_shapes=scratch,
        compiler_params=pltpu.CompilerParams(vmem_limit_bytes=VMEM_LIMIT),
        cost_estimate=pl.CostEstimate(flops=flops, bytes_accessed=moved, transcendentals=0),
        name=name,
    )(*args)


def shape(dims, dtype):
    return jax.ShapeDtypeStruct(dims, dtype)


def pack(w_in, w_out, w_down):
    both = jnp.concatenate([w_out, w_down], axis=-2)
    rest = both[..., 192:, :]
    strip = jnp.concatenate([rest[..., :64], rest[..., 64:128]], axis=-2)
    tail = jnp.concatenate([rest[..., 128:], jnp.zeros_like(rest[..., :16, 128:])], axis=-2)
    chunks = [both[..., 64 * j : 64 * j + 64, :] for j in range(3)]
    return jnp.concatenate(
        [
            jnp.concatenate([w_in, strip], axis=-1),
            jnp.concatenate(chunks + [tail], axis=-1),
        ],
        axis=-2,
    )


def unpack(block):
    top, low = block[..., :96, :], block[..., 96:, :]
    chunks = [low[..., 192 * j : 192 * j + 192] for j in range(3)]
    strip = jnp.concatenate(
        [top[..., :48, 576:], top[..., 48:, 576:], low[..., :48, 576:]], axis=-1
    )
    both = jnp.concatenate(chunks + [strip], axis=-2)
    return top[..., :576], both[..., :96, :], both[..., 96:, :]


def split_slots(full, width):
    rows = full.shape[0] // GRID_F
    blocks = full.reshape(GRID_F, rows, GRID_S, width).transpose(0, 2, 1, 3)
    found = []
    for order in (ORDER_B, ORDER_C):
        for core in range(2):
            found.append(jnp.stack([blocks[f, s ^ core] for f, s in codes_of(order)]))
    return found


def join_slots(own, other, order):
    table = {}
    for k, (f, s) in enumerate(codes_of(order)):
        table[f, s] = own[k]
        table[f, s ^ 1] = other[k]
    return jnp.stack([jnp.stack([table[f, s] for s in range(GRID_S)]) for f in range(GRID_F)])


def per_device(tokens, segments, w_qkv, w_out, w_in, w_down, gains, cotangent):
    here = lax.axis_size("fsdp") == GRID_F and lax.axis_size("seq") == GRID_S
    s_index = lax.axis_index("seq")
    x_index = s_index // 2
    partner = s_index ^ 2

    count = tokens.shape[1]
    place = jnp.stack([lax.axis_index("fsdp"), s_index]).astype(jnp.int32)

    def pick(pair, i):
        return lax.dynamic_index_in_dim(pair, i, 0, keepdims=False)

    xa, ca = pick(tokens, x_index), pick(cotangent, x_index)
    sega = pick(segments, x_index).astype(F32)
    marks = pick(segments, 1 - x_index).astype(BF)[None]
    marks = jnp.pad(marks, ((0, 15), (0, tokens.shape[2] - count)))
    theirs = jnp.concatenate([pick(cotangent, 1 - x_index), marks], axis=0)
    xb = swap(pick(tokens, 1 - x_index), STEPS["x"][0])

    rows = tokens.shape[1]
    places = jnp.concatenate(
        [s_index * rows + jnp.arange(rows), partner * rows + jnp.arange(rows)]
    ).astype(F32)
    freqs = jnp.exp(-jnp.arange(32, dtype=F32) * (2.0 * math.log(160000.0) / HEAD))
    angles = places[:, None] * freqs[None, :]
    cosine, sine = jnp.cos(angles), jnp.sin(angles)
    zero = jnp.zeros_like(sine)
    cos = jnp.concatenate([cosine] * 4, axis=1)
    sin_a = jnp.concatenate([-sine, zero] * 2, axis=1)
    sin_b = jnp.concatenate([zero, sine] * 2, axis=1)
    if here:
        me = place
        wide = jnp.concatenate(
            [w_qkv, gains.T, jnp.zeros((w_qkv.shape[0], 62), BF)], axis=1
        )
        rest = pack(w_in, w_out, w_down)
        held_q = send_z(wide)
        held_q, xb, rest, theirs, xa, ca, sega, place, cos, sin_a, sin_b = tie(
            (held_q, xb, rest, theirs, xa, ca, sega, place, cos, sin_a, sin_b)
        )
        me = place
        cb = swap(theirs, STEPS["x"][0])
        near_z, far_z = (swap(rest, step) for step in STEPS["z"][:2])
        held_q = cut_rows(held_q, 48)
        got = swap_each(held_q, ("x", "y"))
        held_q, got, near_z, far_z, rest, cb = tie((held_q, got, near_z, far_z, rest, cb))
        held_q = join(held_q, got)
        later_q = swap_each(held_q, ("y", "x"))
        far_q = other_core(held_q)
        last_z = swap(rest, STEPS["z"][2])
        later_q, far_q, last_z = tie((later_q, far_q, last_z))
        held_r = cut_rows((rest, near_z, far_z, last_z), 80)
        far_later_q = other_core(later_q)
        got_r = swap_each(held_r, ("x", "y"))
        qkv = interleave(held_q, later_q, far_q, far_later_q)
    else:
        me = jnp.zeros((2,), jnp.int32)

        def whole(w):
            return lax.all_gather(
                lax.all_gather(w, "fsdp", axis=0, tiled=True), "seq", axis=1, tiled=True
            )

        gains_all = lax.all_gather(gains, "fsdp", axis=1, tiled=True).T
        wide = jnp.concatenate(
            [
                jnp.concatenate([block, gains_all, jnp.zeros((768, 62), BF)], axis=1)
                for block in jnp.split(whole(w_qkv), GRID_S, axis=1)
            ],
            axis=1,
        )
        slots = split_slots(wide, 640)
        qkv = (slots[0][:, :48], slots[1][:, :48], slots[2][:, 48:], slots[3][:, 48:])
        qkv = tuple(half for part in qkv for half in (part[:8], part[8:]))
        slots_in = split_slots(whole(w_in), 576)
        slots_out = split_slots(whole(w_out), 192)
        slots_down = split_slots(whole(w_down), 192)
        slots = [pack(*blocks) for blocks in zip(slots_in, slots_out, slots_down)]
        rest = (slots[0][:, :80], slots[1][:, :80], slots[2][:, 80:], slots[3][:, 80:])
        rest = tuple(half for part in rest for half in (part[:8], part[8:]))
        cb = swap(theirs, STEPS["x"][0])
    seg_mine = jnp.concatenate([sega, cb[count, :count].astype(F32)])[None]

    act = shape((512, 768), BF)
    q, kv, norm, weight, gain_rows = call(
        project_kernel,
        [act, shape((512, 1536 + PAIR), BF), act, shape((768, 2304), BF), shape((8, 768), F32)],
        [
            pltpu.VMEM((768, 128), BF), pltpu.VMEM((4, 768, 640), BF),
            pltpu.SemaphoreType.DMA,
        ],
        me, xa, xb, seg_mine, cos, sin_a, sin_b, *qkv,
        flops=10_000_000_000, moved=20_000_000, name="project",
    )
    far_r, later_r = (), ()
    if here:
        q, kv, held_r, got_r = tie((q, kv, held_r, got_r))
        held_r = join(held_r, got_r)
        later_r = swap_each(held_r, ("y", "x"))
        far_r = other_core(held_r)
    kv_far = swap(kv, STEPS["core"][0])

    pair_spec = pl.BlockSpec((512, PAIR), lambda p: (0, p))
    value_spec = pl.BlockSpec((512, PAIR), lambda p: (0, p + HEADS // 2))
    mark_spec = pl.BlockSpec((512, PAIR), lambda p: (0, HEADS))

    def fixed(dims):
        return pl.BlockSpec(dims, lambda p: (0, 0))

    params = pltpu.CompilerParams(
        vmem_limit_bytes=VMEM_LIMIT, dimension_semantics=("arbitrary",)
    )
    att, lse = pl.pallas_call(
        attend_kernel,
        grid=(HEADS // 2,),
        out_shape=[act, shape((512, 768), F32)],
        in_specs=[pair_spec] * 3 + [value_spec] * 2 + [mark_spec] * 2,
        out_specs=[pair_spec] * 2,
        scratch_shapes=[pltpu.VMEM((512, 1024), F32)],
        compiler_params=params,
        cost_estimate=pl.CostEstimate(
            flops=17_000_000_000, bytes_accessed=8_000_000, transcendentals=6_000_000
        ),
        name="attend",
    )(q, kv, kv_far, kv, kv_far, kv, kv_far)

    if here:
        att, lse, far_r, later_r = tie((att, lse, far_r, later_r))
        rest = interleave(held_r, later_r, far_r, other_core(later_r))
    slot = shape((16, 80, 640), BF)
    mix_pair, mix_b, dmid, datt, g2, fb0, fb1, fc0, fc1 = call(
        feed_kernel,
        [
            shape((2, 256, 768), BF), shape((256, 768), BF), shape((512, 768), F32), act,
            shape((8, 768), F32), slot, slot, slot, slot,
        ],
        [
            pltpu.VMEM((4, 768, 640), BF), pltpu.VMEM((8, 4, 64, 640), BF),
            pltpu.VMEM((768, 768), BF), pltpu.VMEM((1152, 768), BF),
            pltpu.VMEM((512, 768), BF), pltpu.VMEM((2, 512, 576), BF),
            pltpu.VMEM((4, 512, 576), BF), pltpu.VMEM((512, 768), BF),
            pltpu.VMEM((4, 768, 640), BF), pltpu.VMEM((8, 4, 64, 640), BF),
            pltpu.VMEM((2, 768, 512), BF),
            pltpu.SemaphoreType.DMA((5,)), pltpu.VMEM((256, 768), BF),
            pltpu.VMEM((512, 768), BF), pltpu.VMEM((512, 768), F32),
            pltpu.VMEM((512, 768), BF),
        ],
        me, place, xa, xb, ca, cb, att, gain_rows, *rest,
        flops=35_000_000_000, moved=30_000_000, name="feed", away_outs=(2, 3),
    )

    def attend_back(first, pairs, *args):
        pair_at = pl.BlockSpec((512, PAIR), lambda p: (0, p + first))
        value_at = pl.BlockSpec((512, PAIR), lambda p: (0, p + first + HEADS // 2))
        both_spec = pl.BlockSpec((512, 2 * PAIR), lambda p: (0, p))
        return pl.pallas_call(
            attend_back_kernel,
            grid=(pairs,),
            out_shape=[
                shape((512, pairs * PAIR), BF),
                shape((512, 2 * pairs * PAIR), F32),
                shape((512, 2 * pairs * PAIR), BF),
            ],
            in_specs=[pair_at] * 3 + [value_at] * 2 + [pair_at] * 3
            + [mark_spec] * 2
            + [fixed((512, PAIR))] * 3,
            out_specs=[pair_spec, both_spec, both_spec],
            scratch_shapes=[pltpu.VMEM((1024, 512), F32)],
            compiler_params=params,
            cost_estimate=pl.CostEstimate(
                flops=6_000_000_000 * pairs, bytes_accessed=4_000_000, transcendentals=2_000_000
            ),
            name="attend_back",
        )(*args)

    attend_args = (
        kv, kv_far, kv, kv_far, att, datt, lse, kv, kv_far,
        cos, sin_a, sin_b,
    )
    back_a = attend_back(0, 2, q, *attend_args)
    own_r, far_r, one_r, two_r = (fb0, fc0), (), (), ()
    mix_far = swap(mix_b, STEPS["x"][0])
    if here:
        far_r = other_core((fb1, fc1))
        back_a, far_r, mix_far = tie((back_a, far_r, mix_far))
        sent = tuple(sums((own_r, far_r), 8, 8, 2))
        sent, q = tie((sent, q))
        one_r = swap_each(sent, ("y", "x"))
    mixed = untrade(place, mix_pair, mix_far)
    far_a = swap(back_a[2], STEPS["core"][0])
    back_b = attend_back(2, 4, q, *attend_args)
    back_b, one_r, mixed = tie((back_b, one_r, mixed))
    far_b = swap(back_b[2], STEPS["core"][0])
    if here:
        sent = tuple(sums((own_r, far_r, one_r), 4, 4, 2))
        sent, far_b = tie((sent, far_b))
        two_r = swap_each(sent, ("x", "y"))

    slot = shape((16, 48, 640), BF)
    dp, lb0, lb1, lc0, lc1 = call(
        weight_grad_kernel,
        [shape((512, 2304), BF), slot, slot, slot, slot],
        [
            pltpu.VMEM((4, 768, 640), BF), pltpu.VMEM((768, 512), BF),
            pltpu.SemaphoreType.DMA,
        ],
        me, norm, weight, gain_rows, g2,
        *(
            part
            for back, far in ((back_a, far_a), (back_b, far_b))
            for part in (back[0], back[1], far)
        ),
        cos, sin_a, sin_b,
        flops=14_000_000_000, moved=20_000_000, name="weight_grad",
    )
    dp, lb0, lb1, lc0, lc1, two_r = tie((dp, lb0, lb1, lc0, lc1, two_r))
    if here:
        own_q = (lb0, lc0)
        far_q = other_core((lb1, lc1))
        blocks_r = tuple(sums((own_r, far_r, one_r, two_r), 0, 4, 1, joined=True))
        far_q, blocks_r = tie((far_q, blocks_r))
        sent, blocks_r, dp = tie((small_sums((own_q, far_q), 8, 8), blocks_r, dp))
        one_q = swap_each(sent, ("y", "x"))
    gt_pair, gt_b = call(
        token_grad_kernel,
        [shape((2, 256, 768), BF), shape((256, 768), BF)],
        [pltpu.VMEM((256, 768), BF), pltpu.SemaphoreType.DMA],
        place, xa, xb, weight, gain_rows, dp, dmid,
        flops=8_000_000_000, moved=10_000_000, name="token_grad",
    )
    if here:
        half = blocks_r[2].shape[0] // 2
        last_z = swap(blocks_r[3], STEPS["z"][2])
        far_z = swap(blocks_r[2][:half], STEPS["z"][1])
        gt_pair, gt_b, one_q, last_z, far_z, blocks_r = tie(
            (gt_pair, gt_b, one_q, last_z, far_z, blocks_r)
        )
        near_z = swap(blocks_r[1], STEPS["z"][0])
        far_z = (far_z, swap(blocks_r[2][half:], STEPS["z"][1]))
        sent, gt_b = tie((small_sums((own_q, far_q, one_q), 4, 4), gt_b))
        two_q = swap_each(sent, ("x", "y"))
    gt_far = swap(gt_b, STEPS["x"][0])
    grad_tokens = untrade(place, gt_pair, gt_far)

    if here:
        two_q, gt_pair, near_z, far_z = tie((two_q, gt_pair, near_z, far_z))
        got_r = (near_z, jnp.concatenate(far_z, axis=0), last_z)
        blocks = small_blocks((own_q, far_q, one_q, two_q))
        rest_sum = last_sum(blocks_r[0], got_r)
        got_q, grad_tokens = tie((swap_z(blocks), grad_tokens))
        grad_qkv = last_sum(blocks[0], got_q)
        grad_in, grad_out, grad_down = unpack(rest_sum)
        grad_gains = grad_qkv[:, 576:578].T
        grad_qkv = grad_qkv[:, :576]
    else:
        full_b = join_slots(fb0, fb1, ORDER_B)
        full_c = join_slots(fc0, fc1, ORDER_C)
        full_q = jnp.concatenate(
            [join_slots(lb0, lb1, ORDER_B), join_slots(lc0, lc1, ORDER_C)], axis=2
        )
        grad_in, grad_out, grad_down = unpack(jnp.concatenate([full_b, full_c], axis=2))

        def share(full):
            flat = full.transpose(0, 2, 1, 3).reshape(-1, GRID_S * full.shape[-1])
            part = lax.psum_scatter(
                flat.astype(F32), "fsdp", scatter_dimension=0, tiled=True
            )
            return lax.psum_scatter(part, "seq", scatter_dimension=1, tiled=True)

        grad_in, grad_out, grad_down = share(grad_in), share(grad_out), share(grad_down)
        grad_qkv = share(full_q[..., :576])
        gain_sum = full_q[:, 0, :, 576:578].reshape(768, 2).astype(F32).T
        grad_gains = lax.psum(
            lax.psum_scatter(gain_sum, "fsdp", scatter_dimension=1, tiled=True), "seq"
        )
    return (mixed, grad_tokens, grad_qkv, grad_out, grad_in, grad_down, grad_gains)


def place_kernel(place, pair, back, out, sem):
    copy = pltpu.make_async_copy(back, out.at[1 - (place[1] >> 1)], sem)
    copy.start()
    copy.wait()


def untrade(place, pair, back):
    anywhere = pl.BlockSpec(memory_space=pl.ANY)
    return pl.pallas_call(
        place_kernel,
        out_shape=shape(pair.shape, pair.dtype),
        in_specs=[
            pl.BlockSpec(memory_space=pltpu.SMEM), anywhere,
            pl.BlockSpec(memory_space=pltpu.VMEM),
        ],
        out_specs=anywhere,
        scratch_shapes=[pltpu.SemaphoreType.DMA],
        input_output_aliases={1: 0},
        name="place",
    )(place, pair, back)


def solution(mesh):
    return jax.shard_map(
        per_device,
        mesh=mesh,
        in_specs=(
            P("fsdp", "seq", None),
            P("fsdp", "seq"),
            P("fsdp", "seq"),
            P("fsdp", "seq"),
            P("fsdp", "seq"),
            P("fsdp", "seq"),
            P(None, "fsdp"),
            P("fsdp", "seq", None),
        ),
        out_specs=(
            P("fsdp", "seq", None),
            P("fsdp", "seq", None),
            P("fsdp", "seq"),
            P("fsdp", "seq"),
            P("fsdp", "seq"),
            P("fsdp", "seq"),
            P(None, "fsdp"),
        ),
        check_vma=False,
    )
```

```python
import functools
import math

import jax
import jax.numpy as jnp
from jax import lax
from jax.experimental import pallas as pl
from jax.experimental.pallas import tpu as pltpu
from jax.sharding import PartitionSpec as P

HEADS = 12
HEAD = 64
PAIR = 2 * HEAD
EPS = 1e-05
FILL = -1000000000.0
BF = jnp.bfloat16
F32 = jnp.float32
VMEM_LIMIT = 60 * 1024 * 1024

STEPS = {
    "x": [("seq", 2)],
    "y": [("fsdp", 1)],
    "z": [("fsdp", 2), ("fsdp", 4), ("fsdp", 6)],
    "core": [("seq", 1)],
}
ORDER_B = ("z", "x", "y")
ORDER_C = ("z", "y", "x")
GRID_F = 8
GRID_S = 4


def swap(value, step):
    axis, flip = step
    size = lax.axis_size(axis)
    return lax.ppermute(value, axis, [(i, i ^ flip) for i in range(size)])


tie = lax.optimization_barrier


def send_z(block):
    return (block,) + tuple(swap(block, step) for step in STEPS["z"])


def cut_rows(blocks, cut):
    return jnp.stack([b[:cut] for b in blocks]), jnp.stack([b[cut:] for b in blocks])


def join(held, got):
    return tuple(jnp.concatenate(pair, axis=0) for pair in zip(held, got))


def interleave(*lists):
    return tuple(piece for part in zip(*lists) for piece in part)


def other_core(parts):
    return tuple(swap(part, STEPS["core"][0]) for part in parts)


def sum_kernel(arrays, joined, *refs):
    ins, outs = refs[: 2 * arrays], refs[2 * arrays :]
    top = 0
    for part in range(2):
        total = ins[arrays * part][...]
        for ref in ins[arrays * part + 1 : arrays * part + arrays]:
            total = (total.astype(F32) + ref[...].astype(F32)).astype(BF)
        rows = total.shape[1]
        if joined:
            for i, out in enumerate(outs):
                out[top : top + rows, :] = total[i]
        else:
            outs[part][...] = total
        top += rows


def sums(lists, start, count, steps, joined=False):
    parts = list(zip(*lists))
    size = count // steps
    ins, specs, outs = [], [], []
    for part in parts:
        rows, width = part[0].shape[1:]
        for array in part:
            ins.append(array)
            specs.append(
                pl.BlockSpec((size, rows, width), lambda i: (start // size + i, 0, 0))
            )
        outs.append(shape((count, rows, width), BF))
    out_specs = [pl.BlockSpec((size,) + o.shape[1:], lambda i: (i, 0, 0)) for o in outs]
    if joined:
        rows = sum(o.shape[1] for o in outs)
        outs = [shape((rows, width), BF)] * count
        out_specs = [pl.BlockSpec((rows, width), lambda i: (0, 0))] * count
    return pl.pallas_call(
        functools.partial(sum_kernel, len(lists), joined),
        grid=(steps,),
        out_shape=outs,
        in_specs=specs,
        out_specs=out_specs,
        compiler_params=pltpu.CompilerParams(dimension_semantics=("arbitrary",)),
        cost_estimate=pl.CostEstimate(
            flops=1_000_000, bytes_accessed=3_000_000, transcendentals=0
        ),
        name="sums",
    )(*ins)


def level(value):
    return lax.reduce_precision(value, 8, 7)


def level_sum(arrays, at):
    total = arrays[0][at].astype(F32)
    for array in arrays[1:]:
        total = level(total + array[at].astype(F32))
    return total.astype(BF)


def small_sums(lists, start, count):
    return tuple(level_sum(part, slice(start, start + count)) for part in zip(*lists))


def small_blocks(lists):
    parts = [level_sum(part, slice(0, 4)) for part in zip(*lists)]
    return [jnp.concatenate([part[i] for part in parts], axis=0) for i in range(4)]


def swap_each(parts, phases):
    return tuple(swap(part, STEPS[phase][0]) for part, phase in zip(parts, phases))


def swap_z(blocks):
    return tuple(swap(blocks[i + 1], step) for i, step in enumerate(STEPS["z"]))


def last_sum(mine, got):
    got = [g.astype(F32) for g in got]
    return (mine.astype(F32) + got[0]) + (got[1] + got[2])


def codes_of(order):
    codes = [(0, 0)]
    for phase in order:
        grown = list(codes)
        for axis, flip in STEPS[phase]:
            for f, s in codes:
                grown.append((f ^ flip, s) if axis == "fsdp" else (f, s ^ flip))
        codes = grown
    return codes


def dot(a, b):
    return jnp.dot(a, b, preferred_element_type=F32)


def dot_nt(a, b, precision=None):
    return lax.dot_general(
        a, b, (((1,), (1,)), ((), ())), preferred_element_type=F32, precision=precision
    )


def dot_tn(a, b, precision=None):
    return lax.dot_general(
        a, b, (((0,), (0,)), ((), ())), preferred_element_type=F32, precision=precision
    )


def norm_stats(x):
    center = x - jnp.mean(x, axis=-1, keepdims=True)
    spread = jnp.mean(center * center, axis=-1, keepdims=True)
    rate = lax.rsqrt(spread + EPS)
    return center * rate, rate


def norm_back(e, hat, rate):
    return rate * (
        e
        - jnp.mean(e, axis=-1, keepdims=True)
        - hat * jnp.mean(e * hat, axis=-1, keepdims=True)
    )


def turn(u, cosine, sine_a, sine_b):
    return u * cosine + pltpu.roll(u, PAIR - 32, 1) * sine_a + pltpu.roll(u, 32, 1) * sine_b


def turn_back(u, cosine, sine_a, sine_b):
    return u * cosine - pltpu.roll(u, PAIR - 32, 1) * sine_a - pltpu.roll(u, 32, 1) * sine_b


def owners(me, order, pieces):
    codes = codes_of(order)
    for i, piece in enumerate(pieces):
        far, later = divmod(i, 2)
        for k in range(8):
            f, s = codes[8 * later + k]
            yield piece, k, me[0] ^ f, me[1] ^ (s ^ far)


def results(me, order, near, far):
    for core, out in enumerate((near, far)):
        for k, (f, s) in enumerate(codes_of(order)):
            yield out, k, me[0] ^ f, me[1] ^ (s ^ core)


def rows_at(start, count):
    return pl.ds(pl.multiple_of(start, 16), count)


def await_all(ref, sem):
    pltpu.make_async_copy(ref, ref, sem).wait()


def project_kernel(me, xa, xb, seg, cos, sin_a, sin_b, *refs):
    pieces = refs[:8]
    q_o, kv_o, n_o, w_o, g_o, gcol, buf, sem = refs[8:]
    kv_o[:, 1536:] = jnp.broadcast_to(seg[...], (PAIR, 512)).T.astype(BF)
    for order, start, part in ((ORDER_B, 0, pieces[:4]), (ORDER_C, 48, pieces[4:])):
        for piece, k, f, s in owners(me, order, part):
            to = buf.at[s, rows_at(f * 96 + start, 48)]
            pltpu.make_async_copy(piece.at[k], to, sem).start()
    await_all(buf, sem)
    gcol[...] = buf[0, :, 512:640]
    for f in range(GRID_F):
        rows = slice(96 * f, 96 * f + 96)
        w_o[rows, :] = jnp.concatenate([buf[s, rows, :576] for s in range(GRID_S)], axis=1)
    row_i = lax.broadcasted_iota(jnp.int32, (8, 128), 0)
    lane_i = lax.broadcasted_iota(jnp.int32, (8, 128), 1)
    hot = jnp.where(lane_i == row_i + 64, 1.0, 0.0).astype(BF)
    gains = dot_nt(hot, gcol[...])
    g_o[...] = gains
    for half, xr in enumerate((xa, xb)):
        hat, _ = norm_stats(xr[...].astype(F32))
        n_o[256 * half : 256 * half + 256, :] = (hat * gains[0:1, :]).astype(BF)
    for j in range(9):
        y = dot(n_o[...], w_o[:, 256 * j : 256 * j + 256])
        if j < 6:
            y = jnp.concatenate(
                [
                    turn(y[:, 128 * i : 128 * i + 128], cos[...], sin_a[...], sin_b[...])
                    for i in range(2)
                ],
                axis=1,
            )
        if j < 3:
            q_o[:, 256 * j : 256 * j + 256] = (y.astype(BF) * 0.125).astype(BF)
        else:
            kv_o[:, 256 * (j - 3) : 256 * (j - 3) + 256] = y.astype(BF)


def head_masks():
    lane = lax.broadcasted_iota(jnp.int32, (1, PAIR), 1)
    first = jnp.where(lane < HEAD, 1.0, 0.0)
    return lane < HEAD, (first.astype(BF), (1.0 - first).astype(BF))


def attend_kernel(q, ka, kb, va, vb, seg_a, seg_b, out, lse, bias):
    @pl.when(pl.program_id(0) == 0)
    def _():
        own, far = seg_a[...].astype(F32), seg_b[...].astype(F32)
        for side, keys in enumerate((own, far)):
            same = own[:, :1] == keys.T[:1, :]
            bias[:, 512 * side : 512 * side + 512] = jnp.where(same, 0.0, FILL)

    lane, masks = head_masks()
    column = lax.broadcasted_iota(jnp.int32, (512, PAIR), 1)
    ones = jnp.where(column == 0, 1.0, 0.0).astype(BF)
    near, far = (jnp.concatenate([v[...], ones], axis=1) for v in (va, vb))
    for t in range(4):
        rows = slice(128 * t, 128 * t + 128)
        outs, logs = [], []
        for mask in masks:
            qm = q[rows, :] * mask
            sa = dot_nt(qm, ka[...]) + bias[rows, :512]
            sb = dot_nt(qm, kb[...]) + bias[rows, 512:]
            peak = jnp.max(jnp.maximum(sa, sb), axis=-1, keepdims=True)
            ea = jnp.exp(sa - peak).astype(BF)
            eb = jnp.exp(sb - peak).astype(BF)
            o = dot(ea, near) + dot(eb, far)
            total = o[:, PAIR : PAIR + 1]
            outs.append(o[:, :PAIR] * (1.0 / total))
            logs.append(peak + jnp.log(total))
        out[rows, :] = jnp.where(lane, outs[0], outs[1]).astype(BF)
        lse[rows, :] = jnp.where(lane, logs[0], logs[1])


def attend_back_kernel(
    q, ka, kb, va, vb, att, datt, lse, seg_a, seg_b, cos, sin_a, sin_b,
    dq_o, near_o, far_o, bias,
):
    @pl.when(pl.program_id(0) == 0)
    def _():
        own, far = seg_a[...].astype(F32), seg_b[...].astype(F32)
        for side, keys in enumerate((own, far)):
            same = keys[:, :1] == own.T[:1, :]
            bias[512 * side : 512 * side + 512, :] = jnp.where(same, 0.0, FILL)

    lane, masks = head_masks()
    row_i = lax.broadcasted_iota(jnp.int32, (8, PAIR), 0)
    lane_i = lax.broadcasted_iota(jnp.int32, (8, PAIR), 1)
    hot = jnp.where(lane_i == row_i * HEAD, 1.0, 0.0)
    spread = jnp.where((lane_i // HEAD) == row_i, 1.0, 0.0)
    high = lax.Precision.HIGHEST
    log_rows = dot_nt(hot, lse[...], high)
    delta_rows = dot_nt(spread, datt[...].astype(F32) * att[...].astype(F32), high)
    dq_parts = [[None, None], [None, None]]
    dk_parts = [None, None]
    dv_parts = [None, None]
    for side, (k, v) in enumerate(((ka, va), (kb, vb))):
        keys = slice(512 * side, 512 * side + 512)
        for t in range(2):
            rows = slice(256 * t, 256 * t + 256)
            for h, mask in enumerate(masks):
                qm = q[rows, :] * mask
                dm = datt[rows, :] * mask
                s = dot_nt(k[...], qm) + bias[keys, rows]
                p = jnp.exp(s - log_rows[h : h + 1, rows])
                dp = dot_nt(v[...], dm)
                ds = (p * (dp - delta_rows[h : h + 1, rows])).astype(BF)
                dv = dot(p.astype(BF), dm)
                dk = dot(ds, qm)
                dq = dot_tn(ds, k[...])
                dv_parts[side] = dv if dv_parts[side] is None else dv_parts[side] + dv
                dk_parts[side] = dk if dk_parts[side] is None else dk_parts[side] + dk
                old = dq_parts[t][h]
                dq_parts[t][h] = dq if old is None else old + dq
    near_o[:, :PAIR] = dk_parts[0]
    near_o[:, PAIR:] = dv_parts[0]
    far_o[:, :PAIR] = dk_parts[1].astype(BF)
    far_o[:, PAIR:] = dv_parts[1].astype(BF)
    for t in range(2):
        rows = slice(256 * t, 256 * t + 256)
        dq = jnp.where(lane, dq_parts[t][0], dq_parts[t][1]) * 0.125
        dq_o[rows, :] = turn_back(dq, cos[rows, :], sin_a[rows, :], sin_b[rows, :]).astype(BF)


def feed_kernel(me, place, xa, xb, ca, cb, att, gains, *refs):
    pieces = refs[:8]
    mix_pair, mix_b, dmid_to, datt_to, g2_o, near_b, far_b, near_c, far_c = refs[8:17]
    dmid_o, datt_o = refs[-2:]
    refs = refs[:-2]
    wide, wide_dn, wout, wdn, n2, hid, di, db, grads, grads_dn, flip, sem, mix_a, cot = refs[17:]
    for piece, k, f, s in owners(me, ORDER_B, pieces[:4]):
        to = wide.at[s, rows_at(f * 96, 80)]
        pltpu.make_async_copy(piece.at[k], to, sem.at[0]).start()
    for piece, k, f, s in owners(me, ORDER_C, pieces[4:]):
        to = wide.at[s, rows_at(f * 96 + 80, 16)]
        pltpu.make_async_copy(piece.at[k, pl.ds(0, 16)], to, sem.at[0]).start()
        to = wide_dn.at[f, s]
        pltpu.make_async_copy(piece.at[k, pl.ds(16, 64)], to, sem.at[1]).start()
    await_all(wide, sem.at[0])
    await_all(wide_dn, sem.at[1])
    for f in range(GRID_F):
        at, low = 96 * f, 144 * f
        first, second, third = (
            jnp.concatenate(
                [wide_dn[f, s, :, 192 * j : 192 * j + 192] for s in range(GRID_S)], axis=1
            )
            for j in range(3)
        )
        wout[at : at + 64, :] = first
        wout[at + 64 : at + 96, :] = second[:32]
        wdn[low : low + 32, :] = second[32:]
        wdn[low + 32 : low + 96, :] = third
        wdn[low + 96 : low + 144, :] = jnp.concatenate(
            [
                strip
                for s in range(GRID_S)
                for strip in (
                    wide[s, at : at + 48, 576:],
                    wide[s, at + 48 : at + 96, 576:],
                    wide_dn[f, s, :48, 576:],
                )
            ],
            axis=1,
        )
    gain = gains[1:2, :]
    gain_grad = jnp.zeros((1, 768), F32)
    tokens = jnp.concatenate([xa[...], xb[...]], axis=0)
    cot[:256, :] = ca[...]
    cot[256:, :] = cb[:256, :]
    mid = tokens.astype(F32) + dot(att[...], wout[...])
    hat, rate = norm_stats(mid)
    n2[...] = (hat * gain).astype(BF)
    branch = None
    for h in range(2):
        down = wdn[576 * h : 576 * h + 576, :]
        a = dot(n2[...], wide[h, :, :576])
        gate = dot(n2[...], wide[2 + h, :, :576])
        cdf = 0.5 * (1.0 + lax.erf(a * math.sqrt(0.5)))
        gelu = a * cdf
        hidden = (gelu * gate).astype(BF)
        hid[h] = hidden
        slope = cdf + a * (jnp.exp(-0.5 * a * a) * (1.0 / math.sqrt(2.0 * math.pi)))
        dh = dot_nt(cot[...], down)
        di[h] = (dh * gate * slope).astype(BF)
        di[2 + h] = (dh * gelu).astype(BF)
        part = dot(hidden, down)
        branch = part if branch is None else branch + part
    mixed = (mid + branch).astype(BF)
    mix_a[...] = mixed[:256]
    mix_b[...] = mixed[256:]
    dn = None
    for s in range(4):
        part = dot_nt(di[s], wide[s, :, :576])
        dn = part if dn is None else dn + part
    gain_grad = gain_grad + jnp.sum(dn * hat, axis=0, keepdims=True)
    dmid = cot[...].astype(F32) + norm_back(dn * gain, hat, rate)
    dmid_o[...] = dmid
    db[...] = dmid.astype(BF)
    datt_o[...] = dot_nt(db[...], wout[...]).astype(BF)
    g2_o[...] = jnp.broadcast_to(gain_grad, (8, 768))

    later = (
        pltpu.make_async_copy(dmid_o, dmid_to, sem.at[3]),
        pltpu.make_async_copy(datt_o, datt_to, sem.at[4]),
    )
    for copy in later:
        copy.start()
    own = pltpu.make_async_copy(mix_a, mix_pair.at[place[1] >> 1], sem.at[2])
    own.start()
    flip[0] = n2[...].T
    flip[1] = att[...].T
    grad_out = dot(flip[1], db[...]).astype(BF)
    for h in range(2):
        grad_down = dot_tn(hid[h], cot[...]).astype(BF)
        for part in range(4):
            f = 4 * h + part
            at = 96 * f
            for s in range(4):
                out = grad_out[at : at + 96, 192 * s : 192 * s + 192]
                low = grad_down[144 * part : 144 * part + 144, 192 * s : 192 * s + 192]
                grads_dn[f, s] = jnp.concatenate(
                    [
                        out[:64],
                        jnp.concatenate([out[64:], low[:32]], axis=0),
                        low[32:96],
                        jnp.concatenate([low[96:, 128:], jnp.zeros((16, 64), BF)], axis=0),
                    ],
                    axis=1,
                )
                grads[s, at : at + 48, 576:] = low[96:, :64]
                grads[s, at + 48 : at + 96, 576:] = low[96:, 64:128]
    for out, k, f, s in results(me, ORDER_C, near_c, far_c):
        to = out.at[k, pl.ds(16, 64)]
        pltpu.make_async_copy(grads_dn.at[f, s], to, sem.at[1]).start()
    for s in range(4):
        grads[s, :, :576] = dot(flip[0], di[s]).astype(BF)
    for out, k, f, s in results(me, ORDER_B, near_b, far_b):
        held = grads.at[s, rows_at(f * 96, 80)]
        pltpu.make_async_copy(held, out.at[k], sem.at[0]).start()
    for out, k, f, s in results(me, ORDER_C, near_c, far_c):
        held = grads.at[s, rows_at(f * 96 + 80, 16)]
        pltpu.make_async_copy(held, out.at[k, pl.ds(0, 16)], sem.at[0]).start()
    await_all(grads, sem.at[0])
    await_all(grads_dn, sem.at[1])
    own.wait()
    for copy in later:
        copy.wait()


def weight_grad_kernel(
    me, norm, weight, gains, g2, *refs
):
    heads = refs[:6]
    cos, sin_a, sin_b, dp, near_b, far_b, near_c, far_c, grads, flip, sem = refs[6:]
    for p, (at, pairs) in enumerate(((0, 2), (2 * PAIR, 4))):
        dq, near, far = heads[3 * p : 3 * p + 3]
        dp[:, at : at + pairs * PAIR] = dq[...]
        for i in range(pairs):
            cols = slice(2 * PAIR * i, 2 * PAIR * i + 2 * PAIR)
            total = near[:, cols] + far[:, cols].astype(F32)
            start = 768 + at + PAIR * i
            dp[:, start : start + PAIR] = turn_back(
                total[:, :PAIR], cos[...], sin_a[...], sin_b[...]
            ).astype(BF)
            dp[:, 768 + start : 768 + start + PAIR] = total[:, PAIR:].astype(BF)
    row_i = lax.broadcasted_iota(jnp.int32, (8, 128), 0)
    lane_i = lax.broadcasted_iota(jnp.int32, (8, 128), 1)
    hot = jnp.where((lane_i == row_i + 64) & (row_i < 2), 1.0, 0.0)
    total = jnp.zeros((768, 1), F32)
    flip[...] = norm[...].T
    for s in range(4):
        cols = slice(576 * s, 576 * s + 576)
        grad = dot(flip[...], dp[:, cols])
        total = total + jnp.sum(grad * weight[:, cols].astype(F32), axis=1, keepdims=True)
        grads[s] = jnp.concatenate([grad, jnp.zeros((768, 64), F32)], axis=1).astype(BF)
    row_w = lax.broadcasted_iota(jnp.int32, (8, 768), 0)
    rows = jnp.where(row_w == 0, 1.0 / gains[0:1, :], g2[...])
    columns = dot_tn(rows, hot, lax.Precision.HIGHEST)
    lane = lax.broadcasted_iota(jnp.int32, (1, 128), 1)
    columns = jnp.where(lane == 64, columns * total, columns).astype(BF)
    for s in range(4):
        grads[s, :, 512:] = grads[s, :, 512:] + columns
    for order, start, near, far in ((ORDER_B, 0, near_b, far_b), (ORDER_C, 48, near_c, far_c)):
        for out, k, f, s in results(me, order, near, far):
            held = grads.at[s, rows_at(f * 96 + start, 48)]
            pltpu.make_async_copy(held, out.at[k], sem).start()
    await_all(grads, sem)


def token_grad_kernel(place, xa, xb, weight, gains, dp, dmid, gt_pair, gt_b, gt_a, sem):
    gain = gains[0:1, :]
    for t, (xr, gt) in enumerate(((xa, gt_a), (xb, gt_b))):
        rows = slice(256 * t, 256 * t + 256)
        dn = dot_nt(dp[rows, :], weight[...])
        hat, rate = norm_stats(xr[...].astype(F32))
        gt[...] = (dmid[rows, :] + norm_back(dn * gain, hat, rate)).astype(BF)
    own = pltpu.make_async_copy(gt_a, gt_pair.at[place[1] >> 1], sem)
    own.start()
    own.wait()


def call(kernel, outs, scratch, *args, flops=0, moved=0, name=None, away_outs=()):
    def spec(a):
        space = pltpu.SMEM if a.dtype == jnp.int32 else pltpu.VMEM
        return pl.BlockSpec(memory_space=pl.ANY if len(a.shape) == 3 else space)

    specs = [spec(a) for a in args]
    return pl.pallas_call(
        kernel,
        out_shape=outs,
        in_specs=specs,
        out_specs=[
            pl.BlockSpec(memory_space=pl.ANY) if i in away_outs else spec(a)
            for i, a in enumerate(outs)
        ],
        scratch_shapes=scratch,
        compiler_params=pltpu.CompilerParams(vmem_limit_bytes=VMEM_LIMIT),
        cost_estimate=pl.CostEstimate(flops=flops, bytes_accessed=moved, transcendentals=0),
        name=name,
    )(*args)


def shape(dims, dtype):
    return jax.ShapeDtypeStruct(dims, dtype)


def pack(w_in, w_out, w_down):
    both = jnp.concatenate([w_out, w_down], axis=-2)
    rest = both[..., 192:, :]
    strip = jnp.concatenate([rest[..., :64], rest[..., 64:128]], axis=-2)
    tail = jnp.concatenate([rest[..., 128:], jnp.zeros_like(rest[..., :16, 128:])], axis=-2)
    chunks = [both[..., 64 * j : 64 * j + 64, :] for j in range(3)]
    return jnp.concatenate(
        [
            jnp.concatenate([w_in, strip], axis=-1),
            jnp.concatenate(chunks + [tail], axis=-1),
        ],
        axis=-2,
    )


def unpack(block):
    top, low = block[..., :96, :], block[..., 96:, :]
    chunks = [low[..., 192 * j : 192 * j + 192] for j in range(3)]
    strip = jnp.concatenate(
        [top[..., :48, 576:], top[..., 48:, 576:], low[..., :48, 576:]], axis=-1
    )
    both = jnp.concatenate(chunks + [strip], axis=-2)
    return top[..., :576], both[..., :96, :], both[..., 96:, :]


def split_slots(full, width):
    rows = full.shape[0] // GRID_F
    blocks = full.reshape(GRID_F, rows, GRID_S, width).transpose(0, 2, 1, 3)
    found = []
    for order in (ORDER_B, ORDER_C):
        for core in range(2):
            found.append(jnp.stack([blocks[f, s ^ core] for f, s in codes_of(order)]))
    return found


def join_slots(own, other, order):
    table = {}
    for k, (f, s) in enumerate(codes_of(order)):
        table[f, s] = own[k]
        table[f, s ^ 1] = other[k]
    return jnp.stack([jnp.stack([table[f, s] for s in range(GRID_S)]) for f in range(GRID_F)])


def per_device(tokens, segments, w_qkv, w_out, w_in, w_down, gains, cotangent):
    here = lax.axis_size("fsdp") == GRID_F and lax.axis_size("seq") == GRID_S
    s_index = lax.axis_index("seq")
    x_index = s_index // 2
    partner = s_index ^ 2

    count = tokens.shape[1]
    place = jnp.stack([lax.axis_index("fsdp"), s_index]).astype(jnp.int32)

    def pick(pair, i):
        return lax.dynamic_index_in_dim(pair, i, 0, keepdims=False)

    xa, ca = pick(tokens, x_index), pick(cotangent, x_index)
    sega = pick(segments, x_index).astype(F32)
    marks = pick(segments, 1 - x_index).astype(BF)[None]
    marks = jnp.pad(marks, ((0, 15), (0, tokens.shape[2] - count)))
    theirs = jnp.concatenate([pick(cotangent, 1 - x_index), marks], axis=0)
    xb = swap(pick(tokens, 1 - x_index), STEPS["x"][0])

    rows = tokens.shape[1]
    places = jnp.concatenate(
        [s_index * rows + jnp.arange(rows), partner * rows + jnp.arange(rows)]
    ).astype(F32)
    freqs = jnp.exp(-jnp.arange(32, dtype=F32) * (2.0 * math.log(160000.0) / HEAD))
    angles = places[:, None] * freqs[None, :]
    cosine, sine = jnp.cos(angles), jnp.sin(angles)
    zero = jnp.zeros_like(sine)
    cos = jnp.concatenate([cosine] * 4, axis=1)
    sin_a = jnp.concatenate([-sine, zero] * 2, axis=1)
    sin_b = jnp.concatenate([zero, sine] * 2, axis=1)
    if here:
        me = place
        wide = jnp.concatenate(
            [w_qkv, gains.T, jnp.zeros((w_qkv.shape[0], 62), BF)], axis=1
        )
        rest = pack(w_in, w_out, w_down)
        held_q = send_z(wide)
        held_q, xb, rest, theirs, xa, ca, sega, place, cos, sin_a, sin_b = tie(
            (held_q, xb, rest, theirs, xa, ca, sega, place, cos, sin_a, sin_b)
        )
        me = place
        cb = swap(theirs, STEPS["x"][0])
        near_z, far_z = (swap(rest, step) for step in STEPS["z"][:2])
        held_q = cut_rows(held_q, 48)
        got = swap_each(held_q, ("x", "y"))
        held_q, got, near_z, far_z, rest, cb = tie((held_q, got, near_z, far_z, rest, cb))
        held_q = join(held_q, got)
        later_q = swap_each(held_q, ("y", "x"))
        far_q = other_core(held_q)
        last_z = swap(rest, STEPS["z"][2])
        later_q, far_q, last_z = tie((later_q, far_q, last_z))
        held_r = cut_rows((rest, near_z, far_z, last_z), 80)
        far_later_q = other_core(later_q)
        got_r = swap_each(held_r, ("x", "y"))
        qkv = interleave(held_q, later_q, far_q, far_later_q)
    else:
        me = jnp.zeros((2,), jnp.int32)

        def whole(w):
            return lax.all_gather(
                lax.all_gather(w, "fsdp", axis=0, tiled=True), "seq", axis=1, tiled=True
            )

        gains_all = lax.all_gather(gains, "fsdp", axis=1, tiled=True).T
        wide = jnp.concatenate(
            [
                jnp.concatenate([block, gains_all, jnp.zeros((768, 62), BF)], axis=1)
                for block in jnp.split(whole(w_qkv), GRID_S, axis=1)
            ],
            axis=1,
        )
        slots = split_slots(wide, 640)
        qkv = (slots[0][:, :48], slots[1][:, :48], slots[2][:, 48:], slots[3][:, 48:])
        qkv = tuple(half for part in qkv for half in (part[:8], part[8:]))
        slots_in = split_slots(whole(w_in), 576)
        slots_out = split_slots(whole(w_out), 192)
        slots_down = split_slots(whole(w_down), 192)
        slots = [pack(*blocks) for blocks in zip(slots_in, slots_out, slots_down)]
        rest = (slots[0][:, :80], slots[1][:, :80], slots[2][:, 80:], slots[3][:, 80:])
        rest = tuple(half for part in rest for half in (part[:8], part[8:]))
        cb = swap(theirs, STEPS["x"][0])
    seg_mine = jnp.concatenate([sega, cb[count, :count].astype(F32)])[None]

    act = shape((512, 768), BF)
    q, kv, norm, weight, gain_rows = call(
        project_kernel,
        [act, shape((512, 1536 + PAIR), BF), act, shape((768, 2304), BF), shape((8, 768), F32)],
        [
            pltpu.VMEM((768, 128), BF), pltpu.VMEM((4, 768, 640), BF),
            pltpu.SemaphoreType.DMA,
        ],
        me, xa, xb, seg_mine, cos, sin_a, sin_b, *qkv,
        flops=10_000_000_000, moved=20_000_000, name="project",
    )
    far_r, later_r = (), ()
    if here:
        q, kv, held_r, got_r = tie((q, kv, held_r, got_r))
        held_r = join(held_r, got_r)
        later_r = swap_each(held_r, ("y", "x"))
        far_r = other_core(held_r)
    kv_far = swap(kv, STEPS["core"][0])

    pair_spec = pl.BlockSpec((512, PAIR), lambda p: (0, p))
    value_spec = pl.BlockSpec((512, PAIR), lambda p: (0, p + HEADS // 2))
    mark_spec = pl.BlockSpec((512, PAIR), lambda p: (0, HEADS))

    def fixed(dims):
        return pl.BlockSpec(dims, lambda p: (0, 0))

    params = pltpu.CompilerParams(
        vmem_limit_bytes=VMEM_LIMIT, dimension_semantics=("arbitrary",)
    )
    att, lse = pl.pallas_call(
        attend_kernel,
        grid=(HEADS // 2,),
        out_shape=[act, shape((512, 768), F32)],
        in_specs=[pair_spec] * 3 + [value_spec] * 2 + [mark_spec] * 2,
        out_specs=[pair_spec] * 2,
        scratch_shapes=[pltpu.VMEM((512, 1024), F32)],
        compiler_params=params,
        cost_estimate=pl.CostEstimate(
            flops=17_000_000_000, bytes_accessed=8_000_000, transcendentals=6_000_000
        ),
        name="attend",
    )(q, kv, kv_far, kv, kv_far, kv, kv_far)

    if here:
        att, lse, far_r, later_r = tie((att, lse, far_r, later_r))
        rest = interleave(held_r, later_r, far_r, other_core(later_r))
    slot = shape((16, 80, 640), BF)
    mix_pair, mix_b, dmid, datt, g2, fb0, fb1, fc0, fc1 = call(
        feed_kernel,
        [
            shape((2, 256, 768), BF), shape((256, 768), BF), shape((512, 768), F32), act,
            shape((8, 768), F32), slot, slot, slot, slot,
        ],
        [
            pltpu.VMEM((4, 768, 640), BF), pltpu.VMEM((8, 4, 64, 640), BF),
            pltpu.VMEM((768, 768), BF), pltpu.VMEM((1152, 768), BF),
            pltpu.VMEM((512, 768), BF), pltpu.VMEM((2, 512, 576), BF),
            pltpu.VMEM((4, 512, 576), BF), pltpu.VMEM((512, 768), BF),
            pltpu.VMEM((4, 768, 640), BF), pltpu.VMEM((8, 4, 64, 640), BF),
            pltpu.VMEM((2, 768, 512), BF),
            pltpu.SemaphoreType.DMA((5,)), pltpu.VMEM((256, 768), BF),
            pltpu.VMEM((512, 768), BF), pltpu.VMEM((512, 768), F32),
            pltpu.VMEM((512, 768), BF),
        ],
        me, place, xa, xb, ca, cb, att, gain_rows, *rest,
        flops=35_000_000_000, moved=30_000_000, name="feed", away_outs=(2, 3),
    )

    def attend_back(first, pairs, *args):
        pair_at = pl.BlockSpec((512, PAIR), lambda p: (0, p + first))
        value_at = pl.BlockSpec((512, PAIR), lambda p: (0, p + first + HEADS // 2))
        both_spec = pl.BlockSpec((512, 2 * PAIR), lambda p: (0, p))
        return pl.pallas_call(
            attend_back_kernel,
            grid=(pairs,),
            out_shape=[
                shape((512, pairs * PAIR), BF),
                shape((512, 2 * pairs * PAIR), F32),
                shape((512, 2 * pairs * PAIR), BF),
            ],
            in_specs=[pair_at] * 3 + [value_at] * 2 + [pair_at] * 3
            + [mark_spec] * 2
            + [fixed((512, PAIR))] * 3,
            out_specs=[pair_spec, both_spec, both_spec],
            scratch_shapes=[pltpu.VMEM((1024, 512), F32)],
            compiler_params=params,
            cost_estimate=pl.CostEstimate(
                flops=6_000_000_000 * pairs, bytes_accessed=4_000_000, transcendentals=2_000_000
            ),
            name="attend_back",
        )(*args)

    attend_args = (
        kv, kv_far, kv, kv_far, att, datt, lse, kv, kv_far,
        cos, sin_a, sin_b,
    )
    back_a = attend_back(0, 2, q, *attend_args)
    own_r, far_r, one_r, two_r = (fb0, fc0), (), (), ()
    mix_far = swap(mix_b, STEPS["x"][0])
    if here:
        far_r = other_core((fb1, fc1))
        back_a, far_r, mix_far = tie((back_a, far_r, mix_far))
        sent = tuple(sums((own_r, far_r), 8, 8, 2))
        sent, q = tie((sent, q))
        one_r = swap_each(sent, ("y", "x"))
    mixed = untrade(place, mix_pair, mix_far)
    far_a = swap(back_a[2], STEPS["core"][0])
    back_b = attend_back(2, 4, q, *attend_args)
    back_b, one_r, mixed = tie((back_b, one_r, mixed))
    far_b = swap(back_b[2], STEPS["core"][0])
    if here:
        sent = tuple(sums((own_r, far_r, one_r), 4, 4, 1))
        sent, far_b = tie((sent, far_b))
        two_r = swap_each(sent, ("x", "y"))

    slot = shape((16, 48, 640), BF)
    dp, lb0, lb1, lc0, lc1 = call(
        weight_grad_kernel,
        [shape((512, 2304), BF), slot, slot, slot, slot],
        [
            pltpu.VMEM((4, 768, 640), BF), pltpu.VMEM((768, 512), BF),
            pltpu.SemaphoreType.DMA,
        ],
        me, norm, weight, gain_rows, g2,
        *(
            part
            for back, far in ((back_a, far_a), (back_b, far_b))
            for part in (back[0], back[1], far)
        ),
        cos, sin_a, sin_b,
        flops=14_000_000_000, moved=20_000_000, name="weight_grad",
    )
    dp, lb0, lb1, lc0, lc1, two_r = tie((dp, lb0, lb1, lc0, lc1, two_r))
    if here:
        own_q = (lb0, lc0)
        far_q = other_core((lb1, lc1))
        blocks_r = tuple(sums((own_r, far_r, one_r, two_r), 0, 4, 1, joined=True))
        far_q, blocks_r = tie((far_q, blocks_r))
        sent, blocks_r, dp = tie((small_sums((own_q, far_q), 8, 8), blocks_r, dp))
        one_q = swap_each(sent, ("y", "x"))
    gt_pair, gt_b = call(
        token_grad_kernel,
        [shape((2, 256, 768), BF), shape((256, 768), BF)],
        [pltpu.VMEM((256, 768), BF), pltpu.SemaphoreType.DMA],
        place, xa, xb, weight, gain_rows, dp, dmid,
        flops=8_000_000_000, moved=10_000_000, name="token_grad",
    )
    if here:
        half = blocks_r[2].shape[0] // 2
        last_z = swap(blocks_r[3], STEPS["z"][2])
        far_z = swap(blocks_r[2][:half], STEPS["z"][1])
        gt_pair, gt_b, one_q, last_z, far_z, blocks_r = tie(
            (gt_pair, gt_b, one_q, last_z, far_z, blocks_r)
        )
        near_z = swap(blocks_r[1], STEPS["z"][0])
        far_z = (far_z, swap(blocks_r[2][half:], STEPS["z"][1]))
        sent, gt_b = tie((small_sums((own_q, far_q, one_q), 4, 4), gt_b))
        two_q = swap_each(sent, ("x", "y"))
    gt_far = swap(gt_b, STEPS["x"][0])
    grad_tokens = untrade(place, gt_pair, gt_far)

    if here:
        two_q, gt_pair, near_z, far_z = tie((two_q, gt_pair, near_z, far_z))
        got_r = (near_z, jnp.concatenate(far_z, axis=0), last_z)
        blocks = small_blocks((own_q, far_q, one_q, two_q))
        rest_sum = last_sum(blocks_r[0], got_r)
        got_q, grad_tokens = tie((swap_z(blocks), grad_tokens))
        grad_qkv = last_sum(blocks[0], got_q)
        grad_in, grad_out, grad_down = unpack(rest_sum)
        grad_gains = grad_qkv[:, 576:578].T
        grad_qkv = grad_qkv[:, :576]
    else:
        full_b = join_slots(fb0, fb1, ORDER_B)
        full_c = join_slots(fc0, fc1, ORDER_C)
        full_q = jnp.concatenate(
            [join_slots(lb0, lb1, ORDER_B), join_slots(lc0, lc1, ORDER_C)], axis=2
        )
        grad_in, grad_out, grad_down = unpack(jnp.concatenate([full_b, full_c], axis=2))

        def share(full):
            flat = full.transpose(0, 2, 1, 3).reshape(-1, GRID_S * full.shape[-1])
            part = lax.psum_scatter(
                flat.astype(F32), "fsdp", scatter_dimension=0, tiled=True
            )
            return lax.psum_scatter(part, "seq", scatter_dimension=1, tiled=True)

        grad_in, grad_out, grad_down = share(grad_in), share(grad_out), share(grad_down)
        grad_qkv = share(full_q[..., :576])
        gain_sum = full_q[:, 0, :, 576:578].reshape(768, 2).astype(F32).T
        grad_gains = lax.psum(
            lax.psum_scatter(gain_sum, "fsdp", scatter_dimension=1, tiled=True), "seq"
        )
    return (mixed, grad_tokens, grad_qkv, grad_out, grad_in, grad_down, grad_gains)


def place_kernel(place, pair, back, out, sem):
    copy = pltpu.make_async_copy(back, out.at[1 - (place[1] >> 1)], sem)
    copy.start()
    copy.wait()


def untrade(place, pair, back):
    anywhere = pl.BlockSpec(memory_space=pl.ANY)
    return pl.pallas_call(
        place_kernel,
        out_shape=shape(pair.shape, pair.dtype),
        in_specs=[
            pl.BlockSpec(memory_space=pltpu.SMEM), anywhere,
            pl.BlockSpec(memory_space=pltpu.VMEM),
        ],
        out_specs=anywhere,
        scratch_shapes=[pltpu.SemaphoreType.DMA],
        input_output_aliases={1: 0},
        name="place",
    )(place, pair, back)


def solution(mesh):
    return jax.shard_map(
        per_device,
        mesh=mesh,
        in_specs=(
            P("fsdp", "seq", None),
            P("fsdp", "seq"),
            P("fsdp", "seq"),
            P("fsdp", "seq"),
            P("fsdp", "seq"),
            P("fsdp", "seq"),
            P(None, "fsdp"),
            P("fsdp", "seq", None),
        ),
        out_specs=(
            P("fsdp", "seq", None),
            P("fsdp", "seq", None),
            P("fsdp", "seq"),
            P("fsdp", "seq"),
            P("fsdp", "seq"),
            P("fsdp", "seq"),
            P(None, "fsdp"),
        ),
        check_vma=False,
    )
```
